32 devices in a mesh: groups: 2 (over y), store: 4 (over x, core), tensor: 4 (over z).
Axes of the slice: x: 2, y: 2, z: 4, core: 2. Of those that a mesh axis runs over, the one named last changes fastest.
Arguments:
- hidden: bfloat16 [2, 1024, 8192], P(None, ('groups', 'store'), 'tensor'), parts along dimension 1, may hold values from -6 to 6
- input_norm_scale: float32 [8192], replicated, may hold values from 0.1 to 1.9
- query_key_value_weight: bfloat16 [8192, 5120], P(None, 'tensor'), may hold values from -0.0625 to 0.0625
- output_weight: bfloat16 [4096, 8192], P(None, 'tensor'), may hold values from -0.09375 to 0.09375
- adapter_down_weight: bfloat16 [256, 8192, 64], P(('groups', 'store'), 'tensor'), parts along dimension 0, may hold values from -0.0625 to 0.0625
- adapter_up_weight: bfloat16 [256, 64, 5120], P(('groups', 'store'), None, 'tensor'), parts along dimension 0, may hold values from -0.75 to 0.75
- row_adapter_index: int32 [1024], P(('groups', 'store')), parts along dimension 0, may hold values from 0 to 127, as said below
- adapter_store_slot: int32 [256], P('groups'), parts along dimension 0, may hold values from 0 to 127, each once
- lengths: int32 [1024], P(('groups', 'store', 'tensor')), parts along dimension 0, may hold values from 1 to 512, 131072 in all
- key_value_cache: bfloat16 [1024, 4, 512, 256], P(('groups', 'store', 'tensor')), parts along dimension 0
Outputs:
- attended: bfloat16 [2, 1024, 8192], P(None, ('groups', 'store'), 'tensor'), parts along dimension 1
The draws below stay inside these ranges and needn't reach their ends.
There are 2 independent parts, one for each index of `groups`. The reference program is written for one: setup_inputs(seed, part) draws one part's arguments, and reference() takes and returns one part's arrays. A program takes and returns all parts, laid end to end along the dimension named above; an argument that names none is the same for every part. Nothing has to cross between parts.
Inputs may be any that keep to these rules, and one draw needn't show every extreme that they name: `row_adapter_index`: ids never decrease along the rows of a part and change only between aligned runs of 8 rows. `adapter_store_slot`: slot k lies with store index k // 32.
All inputs are finite; a program needn't handle non-finite values. No bound on the sum of `lengths` on one device may be relied on, other than what follows from the above.
Results may differ from the reference program's by a relative error of at most 0.0055.
The reference program's roundings to bfloat16 on the way count: a program that leaves them out, or rounds other values in their place, can miss the bound.
Values may be sent and summed in bfloat16 or wider, within the bound.
No kernel may reach another device: no remote copies, remote signals or barrier semaphores. Data moves between devices by JAX's collectives and lax.ppermute only.
A program may use at most 320 MiB of HBM per device.

```python
import math
import jax
import jax.numpy as jnp
import numpy as np
from jax import lax

MODEL_WIDTH = 8192
HEADS = 32
KVH = 4
HD = 128
ADAPTER_RANK = 64
CACHE = 512
ROWS = 512
ADAPTER_COUNT = 128
QW = 4096
MERGED_COLUMNS = 5120
N_TENSOR = 4


def draw_row_adapter_index(key, part):
    key = jax.random.fold_in(key, 5)
    first_key, second_key, order_key = jax.random.split(key, 3)
    groups = ROWS // 8
    first = jax.random.randint(first_key, (groups,), 0, ADAPTER_COUNT)
    second = jax.random.randint(second_key, (groups,), 0, ADAPTER_COUNT)
    order = jax.random.permutation(order_key, ADAPTER_COUNT)
    picked = jnp.sort(order[jnp.minimum(first, second)])
    return jnp.repeat(picked, 8, total_repeat_length=ROWS).astype(jnp.int32)


def draw_key_value_cache(key, part):
    key = jax.random.fold_in(key, 17)
    base_key = jax.random.fold_in(key, 0)
    array_shape = (ROWS, KVH, CACHE, 2 * HD)
    values = jax.random.normal(base_key, array_shape, jnp.float32)
    return values.astype(jnp.bfloat16)


def block_levels(stream_key, dims, pieces, smallest, high):
    def one(dim, blocks):
        draws = jax.random.uniform(jax.random.fold_in(jax.random.fold_in(stream_key, 6), dim), (blocks,), jnp.float32, smallest / len(pieces), high / len(pieces))
        return jnp.repeat(jnp.exp(draws), dims[dim] // blocks).reshape((-1,) + (1,) * (len(dims) - dim - 1))

    factor_of = one(*pieces[0])
    for cut in pieces[1:]:
        factor_of = factor_of * one(*cut)
    return factor_of


def length_profile(count, total, limit, skew):
    portions = [(1 << 20) // math.isqrt(rank ** skew) + 1 for rank in range(2, count + 1)]
    spare, holding = total - limit - (count - 1), [1] * (count - 1)
    while spare > 0:
        candidates = [i for i in range(count - 1) if holding[i] < limit]
        pool, budget = sum([portions[i] for i in candidates]), spare
        for i in candidates:
            extra = min(limit - holding[i], max(1, budget * portions[i] // pool), spare)
            holding[i] = holding[i] + extra
            spare = spare - extra
    return np.array([limit] + holding)


def ragged_sizes(stream_key, amount, total, bound, slope):
    if amount == 2:
        one = jax.random.randint(stream_key, (), max(1, total - bound), min(bound, total - 1) + 1)
        return jnp.stack([one, total - one])
    tallies = jnp.asarray(length_profile(amount, total, bound, slope), jnp.int32)
    twos = (amount - 1) // 2
    source_of, taker = tallies[1:1 + 2 * twos:2], tallies[2:2 + 2 * twos:2]
    room = jnp.minimum(source_of - 1, bound - taker)
    shifted = jax.random.randint(jax.random.fold_in(stream_key, 1), (twos,), 0, 1 << 20) % (room + 1)
    tallies = tallies.at[1:1 + 2 * twos:2].set(source_of - shifted).at[2:2 + 2 * twos:2].set(taker + shifted)
    return tallies[jax.random.permutation(jax.random.fold_in(stream_key, 2), amount)]


def noise(stream_key, extent, spread, limit, shards=(), held_as=jnp.bfloat16):
    drawn = spread * jax.random.normal(stream_key, extent, jnp.float32)
    if shards:
        drawn = drawn * block_levels(stream_key, extent, shards, -0.22, 0.18)
    return jnp.clip(drawn, -limit, limit).astype(held_as)


def setup_inputs(seed: int = 0, part: int = 0) -> dict:
    arg_keys = jax.random.split(jax.random.key(seed), 11)
    part_splits = jax.random.split(jax.random.fold_in(arg_keys[10], part), 11)
    hidden = noise(part_splits[0], (2, ROWS, MODEL_WIDTH), 1.0, 6.0, ((1, 4), (2, 4)))
    input_norm_scale = jnp.clip(1.0 + 0.18 * jax.random.normal(arg_keys[1], (MODEL_WIDTH,), jnp.float32), 0.1, 1.9)
    query_key_value_weight = noise(arg_keys[2], (MODEL_WIDTH, MERGED_COLUMNS), MODEL_WIDTH ** -0.5, 0.0625, ((1, 4),))
    output_weight = noise(arg_keys[3], (QW, MODEL_WIDTH), QW ** -0.5, 0.09375, ((1, 4),))
    adapter_down_weight = noise(part_splits[4], (ADAPTER_COUNT, MODEL_WIDTH, ADAPTER_RANK), MODEL_WIDTH ** -0.5, 0.0625, ((0, 4), (1, 4)))
    adapter_up_weight = noise(part_splits[5], (ADAPTER_COUNT, ADAPTER_RANK, MERGED_COLUMNS), ADAPTER_RANK ** -0.5, 0.75, ((0, 4), (2, 4)))
    row_adapter_index = draw_row_adapter_index(jax.random.fold_in(jax.random.fold_in(arg_keys[10], part), 71), part)
    adapter_store_slot = jax.random.permutation(part_splits[7], ADAPTER_COUNT).astype(jnp.int32)
    lengths = ragged_sizes(part_splits[8], ROWS, ROWS * CACHE // 2, CACHE, 2).astype(jnp.int32)
    key_value_cache = draw_key_value_cache(jax.random.fold_in(jax.random.fold_in(arg_keys[10], part), 71), part)
    return {"hidden": hidden, "input_norm_scale": input_norm_scale, "query_key_value_weight": query_key_value_weight, "output_weight": output_weight, "adapter_down_weight": adapter_down_weight, "adapter_up_weight": adapter_up_weight, "row_adapter_index": row_adapter_index, "adapter_store_slot": adapter_store_slot, "lengths": lengths, "key_value_cache": key_value_cache}


eps_norm = 1e-05
rope_base = 500000.0
masked = -1e+30

def rotate(values, angles):
    half = values.shape[-1] // 2
    cosine = jnp.cos(angles)[..., None, :]
    sine = jnp.sin(angles)[..., None, :]
    first = values[..., :half]
    second = values[..., half:]
    return jnp.concatenate([first * cosine - second * sine, second * cosine + first * sine], axis=-1)

def angles_for(lengths, head_dim):
    position = (lengths[None, :] + jnp.arange(2, dtype=jnp.int32)[:, None]).astype(jnp.float32)
    freq = rope_base ** (-(jnp.arange(head_dim // 2, dtype=jnp.float32) * 2.0 / head_dim))
    return position[..., None] * freq

def attend(query, key_new, value_new, key_value_cache, lengths):
    rows = query.shape[1]
    heads = query.shape[2]
    head_dim = query.shape[3]
    kv_heads = key_value_cache.shape[1]
    group = heads // kv_heads
    grouped = query.reshape(2, rows, kv_heads, group, head_dim).astype(jnp.float32)
    keys = key_value_cache[..., :head_dim].astype(jnp.float32)
    vals = key_value_cache[..., head_dim:].astype(jnp.float32)
    scale = head_dim ** (-0.5)
    older = jnp.einsum('srhgd,rhcd->srhgc', grouped, keys) * scale
    live = jnp.arange(key_value_cache.shape[2], dtype=jnp.int32)[None, :] < lengths[:, None]
    older = jnp.where(live[None, :, None, None, :], older, masked)
    fresh = jnp.einsum('srhgd,trhd->srhgt', grouped, key_new.astype(jnp.float32)) * scale
    valid = jnp.arange(2, dtype=jnp.int32)[None, :] <= jnp.arange(2, dtype=jnp.int32)[:, None]
    fresh = jnp.where(valid[:, None, None, None, :], fresh, masked)
    peak = jnp.maximum(lax.optimization_barrier(jnp.max(older, axis=-1, keepdims=True)), lax.optimization_barrier(jnp.max(fresh, axis=-1, keepdims=True)))
    p_old = jnp.exp(older - peak)
    p_new = jnp.exp(fresh - peak)
    total = lax.optimization_barrier(jnp.sum(p_old, axis=-1, keepdims=True)) + lax.optimization_barrier(jnp.sum(p_new, axis=-1, keepdims=True))
    w_old = p_old.astype(jnp.bfloat16).astype(jnp.float32)
    w_new = p_new.astype(jnp.bfloat16).astype(jnp.float32)
    mixed = jnp.einsum('srhgc,rhcd->srhgd', w_old, vals)
    mixed = mixed + jnp.einsum('srhgt,trhd->srhgd', w_new, value_new.astype(jnp.float32))
    return (mixed / total).astype(jnp.bfloat16).reshape(2, rows, heads * head_dim)

def reference(hidden, input_norm_scale, query_key_value_weight, output_weight, adapter_down_weight, adapter_up_weight, row_adapter_index, adapter_store_slot, lengths, key_value_cache):
    values = hidden.astype(jnp.float32)
    scale = lax.rsqrt(lax.optimization_barrier(jnp.mean(values * values, axis=-1, keepdims=True)) + eps_norm)
    normed = (values * scale * input_norm_scale).astype(jnp.bfloat16)
    flat = normed.reshape(2 * ROWS, MODEL_WIDTH)
    base = jnp.dot(flat, query_key_value_weight, preferred_element_type=jnp.float32)
    slots = adapter_store_slot[row_adapter_index].astype(jnp.int32)
    picks = (slots[:, None] == jnp.arange(ADAPTER_COUNT, dtype=jnp.int32)[None, :]).astype(jnp.float32)
    down_products = jnp.transpose(adapter_down_weight, (1, 0, 2)).reshape(MODEL_WIDTH, ADAPTER_COUNT * ADAPTER_RANK)
    every = jnp.dot(flat, down_products, preferred_element_type=jnp.float32).reshape(2, ROWS, ADAPTER_COUNT, ADAPTER_RANK)
    shrink = lax.optimization_barrier(jnp.sum(every * picks[None, :, :, None], axis=2))
    shrink_b = shrink.astype(jnp.bfloat16)
    row_spread = (picks[None, :, :, None] * shrink_b.astype(jnp.float32)[:, :, None, :]).astype(jnp.bfloat16)
    row_spread = row_spread.reshape(2 * ROWS, ADAPTER_COUNT * ADAPTER_RANK)
    adapter_delta = jnp.dot(row_spread, adapter_up_weight.reshape(ADAPTER_COUNT * ADAPTER_RANK, MERGED_COLUMNS), preferred_element_type=jnp.float32)
    qkv = (base + adapter_delta).astype(jnp.bfloat16).reshape(2, ROWS, N_TENSOR, MERGED_COLUMNS // N_TENSOR)
    q_cols = QW // N_TENSOR
    query = qkv[..., :q_cols].reshape(2, ROWS, HEADS, HD)
    pairs = qkv[..., q_cols:].reshape(2, ROWS, 2, KVH, HD)
    angles = angles_for(lengths, HD)
    query_rot = rotate(query.astype(jnp.float32), angles).astype(jnp.bfloat16)
    key_rot = rotate(pairs[:, :, 0].astype(jnp.float32), angles).astype(jnp.bfloat16)
    context = attend(query_rot, key_rot, pairs[:, :, 1], key_value_cache, lengths)
    output = jnp.dot(context.reshape(2 * ROWS, QW), output_weight, preferred_element_type=jnp.float32)
    return output.astype(jnp.bfloat16).reshape(2, ROWS, MODEL_WIDTH)
```

```python
import functools

import jax
import jax.numpy as jnp
from jax import lax
from jax.experimental import pallas as pl
from jax.experimental.pallas import tpu as pltpu
from jax.sharding import PartitionSpec as P

HEADS = 32
KVH = 4
HD = 128
GROUP = HEADS // KVH
RUN = 8
STEPS = 2
LANES = 128
HALVES = 2

eps_norm = 1e-05
rope_base = 500000.0
masked = -1e30

MIB = 1 << 20
F32 = jnp.float32
BF16 = jnp.bfloat16
VMEM = pl.BlockSpec(memory_space=pltpu.VMEM)
SMEM = pl.BlockSpec(memory_space=pltpu.SMEM)
HBM = pl.BlockSpec(memory_space=pltpu.HBM)


def swap(values, axis, distance):
    count = lax.axis_size(axis)
    return lax.ppermute(values, axis, [(i, i ^ distance) for i in range(count)])


def summed_over(values, axis):
    distance = 1
    while distance < lax.axis_size(axis):
        values = values + swap(values, axis, distance)
        distance *= 2
    return values


def base_kernel(x_ref, scale_ref, gain_ref, w_ref, out_ref, held, sems):
    owners, _, span = x_ref.shape
    tiles, depth, _ = held.shape
    copies = [
        pltpu.make_async_copy(w_ref.at[pl.ds(k * depth, depth), :], held.at[k], sems.at[k])
        for k in range(tiles)
    ]
    for copy in copies:
        copy.start()
    scale = scale_ref[...]
    for k, copy in enumerate(copies):
        owner, first = divmod(k * depth, span)
        gain = gain_ref[:, k * depth : (k + 1) * depth]
        rows = x_ref[owner, :, first : first + depth].astype(F32)
        normed = (rows * scale * gain).astype(BF16)
        copy.wait()
        product = jnp.dot(normed, held[k], preferred_element_type=F32)
        if k > 0:
            out_ref[...] += product
        else:
            out_ref[...] = product


def base_rows(x, scale, gain, weight):
    owners, rows, span = x.shape
    depth, columns = weight.shape
    tile = min(512, span)
    tiles = depth // tile
    return pl.pallas_call(
        base_kernel,
        out_shape=jax.ShapeDtypeStruct((rows, columns), F32),
        in_specs=[VMEM] * 3 + [HBM],
        out_specs=VMEM,
        scratch_shapes=[
            pltpu.VMEM((tiles, tile, columns), BF16),
            pltpu.SemaphoreType.DMA((tiles,)),
        ],
        compiler_params=pltpu.CompilerParams(vmem_limit_bytes=48 * MIB),
        cost_estimate=pl.CostEstimate(
            flops=2 * rows * depth * columns,
            bytes_accessed=2 * depth * (rows + columns) + 4 * rows * columns,
            transcendentals=0,
        ),
        name="base_rows",
    )(x, scale, gain, weight)


def shrink_kernel(place_ref, slots, x0, x1, x2, x3, scale_ref, gain_ref, down_ref, out_ref, held, sems):
    runs = held.shape[0] // 4
    pairs = runs // 2

    def fetch(n, carry):
        @pl.when(slots[n] >= 0)
        def _():
            pltpu.make_async_copy(down_ref.at[slots[n]], held.at[n], sems.at[n]).start()

        return carry

    lax.fori_loop(0, 4 * runs, fetch, 0)
    out_ref[...] = jnp.zeros_like(out_ref)
    rank = down_ref.shape[1]
    for slab, (d, x_ref) in enumerate(((0, x0), (2, x2), (1, x1), (3, x3))):
        owner = place_ref[0] ^ d
        for half in range(2):

            def one(i, carry):
                run = half * pairs + i
                n = owner * runs + run

                @pl.when(slots[n] >= 0)
                def _():
                    pltpu.make_async_copy(
                        down_ref.at[slots[n]], held.at[n], sems.at[n]
                    ).wait()
                    place = pl.ds(pl.multiple_of(run * 16, 16), 16)
                    rows = x_ref[place, :].astype(F32) * scale_ref[owner, place, :] * gain_ref[...]
                    rows = rows.astype(BF16)
                    part = lax.dot_general(
                        rows, held[n], (((1,), (1,)), ((), ())), preferred_element_type=F32
                    )
                    out_ref[
                        slab, pl.ds(pl.multiple_of(i * 16, 16), 16), half * rank : (half + 1) * rank
                    ] = part

                return carry

            lax.fori_loop(0, pairs, one, 0)


def shrink_rows(place, slots, blocks, scales, gain, down):
    rows, depth = blocks[0].shape
    rank = down.shape[1]
    runs = rows // 16
    return pl.pallas_call(
        shrink_kernel,
        out_shape=jax.ShapeDtypeStruct((4, rows // 2, 2 * rank), F32),
        in_specs=[SMEM] * 2 + [VMEM] * 6 + [HBM],
        out_specs=VMEM,
        scratch_shapes=[
            pltpu.VMEM((4 * runs, rank, depth), BF16),
            pltpu.SemaphoreType.DMA((4 * runs,)),
        ],
        compiler_params=pltpu.CompilerParams(vmem_limit_bytes=56 * MIB),
        cost_estimate=pl.CostEstimate(
            flops=2 * rows * depth * rank,
            bytes_accessed=8 * rows * depth + down.size,
            transcendentals=0,
        ),
        name="shrink_rows",
    )(place, slots, *blocks, scales, gain, down)


def grow_kernel(place_ref, slots, s_ref, up_ref, out_ref, held, sems):
    runs = held.shape[0] // 4
    pairs = runs // 2
    rank = up_ref.shape[1]

    def fetch(n, carry):
        @pl.when(slots[n] >= 0)
        def _():
            pltpu.make_async_copy(up_ref.at[slots[n]], held.at[n], sems.at[n]).start()

        return carry

    lax.fori_loop(0, 4 * runs, fetch, 0)
    for slab, d in enumerate((0, 2, 1, 3)):
        owner = place_ref[0] ^ d
        for half in range(2):

            def one(i, carry):
                run = half * pairs + i
                n = owner * runs + run
                place = pl.ds(pl.multiple_of(run * 16, 16), 16)

                @pl.when(slots[n] >= 0)
                def _():
                    pltpu.make_async_copy(up_ref.at[slots[n]], held.at[n], sems.at[n]).wait()
                    rows = s_ref[
                        slab, pl.ds(pl.multiple_of(i * 16, 16), 16), half * rank : (half + 1) * rank
                    ]
                    out_ref[slab, place, :] = jnp.dot(
                        rows, held[n], preferred_element_type=F32
                    )

                @pl.when(slots[n] < 0)
                def _():
                    out_ref[slab, place, :] = jnp.zeros((16, out_ref.shape[2]), F32)

                return carry

            lax.fori_loop(0, pairs, one, 0)


def grow_rows(place, slots, shrunk, up):
    _, pair_rows, _ = shrunk.shape
    rows = 2 * pair_rows
    rank, columns = up.shape[1:]
    runs = rows // 16
    return pl.pallas_call(
        grow_kernel,
        out_shape=jax.ShapeDtypeStruct((4, rows, columns), F32),
        in_specs=[SMEM, SMEM, VMEM, HBM],
        out_specs=VMEM,
        scratch_shapes=[
            pltpu.VMEM((4 * runs, rank, columns), BF16),
            pltpu.SemaphoreType.DMA((4 * runs,)),
        ],
        compiler_params=pltpu.CompilerParams(vmem_limit_bytes=60 * MIB),
        cost_estimate=pl.CostEstimate(
            flops=2 * rows * rank * columns,
            bytes_accessed=8 * rows * columns + up.size,
            transcendentals=0,
        ),
        name="grow_rows",
    )(place, slots, shrunk, up)


def attend_kernel(
    unit,
    first_row,
    lengths,
    order,
    qkv_ref,
    cos_ref,
    sin_ref,
    cache_ref,
    out_ref,
    queries,
    keys,
    values,
    context,
    held,
    sems,
):
    rows, _, cached, _ = held.shape
    local = STEPS * rows
    q_columns = GROUP * HD
    part = cached // 2
    scale = HD ** (-0.5)
    team = min(4, rows)

    def copy(r, b):
        span = pl.ds(b * part, part)
        return pltpu.make_async_copy(
            cache_ref.at[first_row + r, :, span, :], held.at[r, :, span, :], sems.at[r, b]
        )

    def longest(group):
        return lengths[order[group * team + team - 1]]

    def fetch(i, carry):
        r = order[i]
        copy(r, 0).start()

        @pl.when(longest(i // team) > part)
        def _():
            copy(r, 1).start()

        return carry

    lax.fori_loop(0, rows, fetch, 0)

    cosine = cos_ref[...]
    sine = sin_ref[...]

    def rotated(x):
        x = x.astype(F32)
        turned = x * cosine + pltpu.roll(x, HD // 2, 1) * sine
        return turned.astype(BF16).astype(F32)

    for k in range(KVH):
        for g in range(GROUP):
            queries[k, g * local : (g + 1) * local, :] = rotated(
                qkv_ref[k, :, g * HD : (g + 1) * HD]
            )
        place = q_columns + (k % 2) * HD
        keys[k] = rotated(qkv_ref[k // 2, :, place : place + HD])
        values[k] = qkv_ref[2 + k // 2, :, place : place + HD].astype(F32)

    early = lax.broadcasted_iota(jnp.int32, (4 * GROUP, 1), 0) % (2 * GROUP) < GROUP

    def scores(r, at, pair, span, live):
        heads = (2 * pair, 2 * pair + 1)
        query = [
            jnp.concatenate(
                [queries[k, pl.ds(at[s], GROUP, stride=local), :] for s in range(STEPS)], axis=0
            )
            for k in heads
        ]
        blank = jnp.zeros((2 * GROUP, HD), F32)
        spread = jnp.concatenate(
            [
                jnp.concatenate([query[0], blank], axis=1),
                jnp.concatenate([blank, query[1]], axis=1),
            ],
            axis=0,
        ).astype(BF16)
        old_keys = jnp.concatenate([held[r, k, :span, :HD] for k in heads], axis=1)
        old = lax.dot_general(
            spread, old_keys, (((1,), (1,)), ((), ())), preferred_element_type=F32
        )
        old = jnp.where(live, old * scale, masked)
        fresh = []
        for t in range(STEPS):
            both = jnp.concatenate(
                [
                    jnp.sum(query[i] * keys[k, pl.ds(at[t], 1), :], axis=1, keepdims=True)
                    for i, k in enumerate(heads)
                ],
                axis=0,
            )
            fresh.append(both * scale)
        fresh[1] = jnp.where(early, masked, fresh[1])
        return old, fresh

    def soften(old, fresh):
        peak = jnp.maximum(jnp.max(old, axis=1, keepdims=True), jnp.maximum(fresh[0], fresh[1]))
        p_old = jnp.exp(old - peak)
        p_new = [jnp.exp(f - peak) for f in fresh]
        total = jnp.sum(p_old, axis=1, keepdims=True) + (p_new[0] + p_new[1])
        return p_old.astype(BF16), [p.astype(BF16).astype(F32) for p in p_new], total

    def mix(r, at, pair, span, w_old, w_new, total):
        heads = (2 * pair, 2 * pair + 1)
        old_values = jnp.concatenate([held[r, k, :span, HD:] for k in heads], axis=1)
        mixed = jnp.dot(w_old, old_values, preferred_element_type=F32)
        for i, k in enumerate(heads):
            own = slice(i * 2 * GROUP, (i + 1) * 2 * GROUP)
            result = mixed[own, i * HD : (i + 1) * HD]
            for t in range(STEPS):
                result = result + w_new[t][own] * values[k, pl.ds(at[t], 1), :]
            result = result / total[own]
            for s in range(STEPS):
                context[k, pl.ds(at[s], GROUP, stride=local), :] = result[
                    s * GROUP : (s + 1) * GROUP
                ]

    def attend_team(members, span):
        jobs = []
        for r in members:
            at = [(r // unit) * (STEPS * unit) + s * unit + r % unit for s in range(STEPS)]
            live = lax.broadcasted_iota(jnp.int32, (4 * GROUP, span), 1) < lengths[r]
            for pair in range(KVH // 2):
                jobs.append((r, at, pair, scores(r, at, pair, span, live)))
        softened = [soften(*job[3]) for job in jobs]
        for (r, at, pair, _), weights in zip(jobs, softened):
            mix(r, at, pair, span, *weights)

    def each(group, carry):
        members = [order[group * team + i] for i in range(team)]
        wide = longest(group) > part
        for r in members:
            copy(r, 0).wait()

        @pl.when(wide)
        def _():
            for r in members:
                copy(r, 1).wait()
            attend_team(members, cached)

        @pl.when(jnp.logical_not(wide))
        def _():
            attend_team(members, part)

        return carry

    lax.fori_loop(0, rows // team, each, 0)
    for k in range(KVH):
        for g in range(GROUP):
            place = (k * GROUP + g) * HD
            out_ref[:, place : place + HD] = context[k, g * local : (g + 1) * local, :].astype(BF16)


def attend(lengths, order, qkv, cosine, sine, cache, first_row, unit):
    rows = lengths.shape[0]
    local = STEPS * rows
    _, kv_heads, cached, width = cache.shape
    return pl.pallas_call(
        functools.partial(attend_kernel, unit, first_row),
        out_shape=jax.ShapeDtypeStruct((local, HEADS * HD), BF16),
        in_specs=[SMEM, SMEM, VMEM, VMEM, VMEM, HBM],
        out_specs=VMEM,
        scratch_shapes=[
            pltpu.VMEM((KVH, GROUP * local, HD), F32),
            pltpu.VMEM((KVH, local, HD), F32),
            pltpu.VMEM((KVH, local, HD), F32),
            pltpu.VMEM((KVH, GROUP * local, HD), F32),
            pltpu.VMEM((rows, kv_heads, cached, width), BF16),
            pltpu.SemaphoreType.DMA((rows, 2)),
        ],
        compiler_params=pltpu.CompilerParams(vmem_limit_bytes=48 * MIB),
        cost_estimate=pl.CostEstimate(
            flops=4 * local * HEADS * HD * cached,
            bytes_accessed=2 * rows * kv_heads * cached * width,
            transcendentals=local * HEADS * cached,
        ),
        name="attend",
    )(lengths, order, qkv, cosine, sine, cache)


def out_kernel(context_ref, w_ref, out_ref, total, held, sems):
    owners, local, _ = context_ref.shape
    rows = local // STEPS
    unit = min(RUN, rows)
    tiles, depth, columns = held.shape
    copies = [
        pltpu.make_async_copy(w_ref.at[pl.ds(k * depth, depth), :], held.at[k], sems.at[k])
        for k in range(tiles)
    ]
    for copy in copies:
        copy.start()
    width = min(512, columns)
    for k, copy in enumerate(copies):
        lhs = context_ref[:, :, k * depth : (k + 1) * depth].reshape(owners * local, depth)
        copy.wait()
        for j in range(columns // width):
            span = slice(j * width, (j + 1) * width)
            product = jnp.dot(lhs, held[k, :, span], preferred_element_type=F32)
            if k > 0:
                product = total[:, span] + product
            if k < tiles - 1:
                total[:, span] = product
                continue
            block = product.reshape(owners, rows // unit, STEPS, unit, width)
            for s in range(STEPS):
                piece = block[:, :, s].reshape(owners, rows, width)
                out_ref[s, :, :, span] = piece.astype(BF16)


def project(context, weight):
    owners, local, depth = context.shape
    columns = weight.shape[1]
    tile = min(512, depth)
    rows = local // STEPS
    return pl.pallas_call(
        out_kernel,
        out_shape=jax.ShapeDtypeStruct((STEPS, owners, rows, columns), BF16),
        in_specs=[VMEM, HBM],
        out_specs=VMEM,
        scratch_shapes=[
            pltpu.VMEM((owners * local, columns), F32),
            pltpu.VMEM((depth // tile, tile, columns), BF16),
            pltpu.SemaphoreType.DMA((depth // tile,)),
        ],
        compiler_params=pltpu.CompilerParams(vmem_limit_bytes=52 * MIB),
        cost_estimate=pl.CostEstimate(
            flops=2 * owners * local * depth * columns,
            bytes_accessed=2 * depth * columns + 2 * owners * local * (depth + columns),
            transcendentals=0,
        ),
        name="project",
    )(context, weight)


def lookup(identity, table):
    hits = identity[:, None] == jnp.arange(table.shape[0], dtype=jnp.int32)[None, :]
    return jnp.sum(jnp.where(hits, table[None, :], 0), axis=1)


def ascending(lengths):
    count = lengths.shape[0]
    rows = jnp.arange(count, dtype=jnp.int32)
    keyed = lengths * count + rows
    rank = jnp.sum((keyed[None, :] < keyed[:, None]).astype(jnp.int32), axis=1)
    return jnp.sum(jnp.where(rank[:, None] == rows[None, :], rows[:, None], 0), axis=0)


def angle_tables(lengths, unit):
    steps = jnp.arange(STEPS, dtype=jnp.int32)
    position = lengths.reshape(-1, 1, unit) + steps[None, :, None]
    freq = rope_base ** (-(jnp.arange(HD // 2, dtype=F32) * 2.0 / HD))
    angles = position.reshape(-1).astype(F32)[:, None] * freq
    cosine = jnp.cos(angles)
    sine = jnp.sin(angles)
    return jnp.concatenate([cosine, cosine], 1), jnp.concatenate([-sine, sine], 1)


def on_device(
    hidden,
    input_norm_scale,
    query_key_value_weight,
    output_weight,
    adapter_down_weight,
    adapter_up_weight,
    row_adapter_index,
    adapter_store_slot,
    lengths,
    key_value_cache,
):
    tensor_count = lax.axis_size("tensor")
    tensor_pos = lax.axis_index("tensor")
    store_pos = lax.axis_index("store")
    _, rows, span = hidden.shape
    model_width = input_norm_scale.shape[0]
    rows_here = lengths.shape[0]
    unit = min(RUN, rows_here)
    halves = HALVES if rows_here % (HALVES * RUN) == 0 else 1
    part_rows = rows_here // halves
    local = STEPS * part_rows
    held_slots = adapter_down_weight.shape[0]
    rank = adapter_down_weight.shape[2]

    raw = hidden.reshape(STEPS, rows // unit, unit, span).transpose(1, 0, 2, 3)
    raw = raw.reshape(STEPS * rows, span)
    values = raw.astype(F32)
    squares = jnp.sum(values * values, axis=1)
    squares = summed_over(squares, "tensor")
    told = jnp.concatenate([squares, row_adapter_index[::RUN].astype(F32)])
    told = told.reshape(1, -1)
    told = jnp.concatenate([told, swap(told, "store", 2)], axis=0)
    told = jnp.concatenate([told, swap(told, "store", 1)], axis=0)
    told = jnp.stack([told[d] for d in (0, 2, 1, 3)])
    told = lax.dynamic_index_in_dim(
        jnp.stack([jnp.stack([told[p ^ q] for q in range(4)]) for p in range(4)]),
        store_pos,
        0,
        keepdims=False,
    )
    scales = lax.rsqrt(told[:, : STEPS * rows] / model_width + eps_norm)
    runs = told[:, STEPS * rows :].astype(jnp.int32)
    slots = lookup(runs.reshape(-1), adapter_store_slot).reshape(runs.shape)
    slots = jnp.where(slots // held_slots == store_pos, slots % held_slots, -1)
    place = store_pos.reshape(1).astype(jnp.int32)
    gains = input_norm_scale.reshape(1, -1)
    gain = lax.dynamic_slice_in_dim(gains, tensor_pos * span, span, 1)
    scales = scales.reshape(-1, tensor_count, halves, local)
    raw = raw.reshape(tensor_count, halves, local, span)

    down = jnp.swapaxes(adapter_down_weight, 1, 2)
    results = []
    context = None
    for h in range(halves):
        own = raw[:, h].reshape(tensor_count * local, span)
        count = own.shape[0]
        part_scales = scales[:, :, h].reshape(-1, count, 1)
        own_scale = lax.dynamic_index_in_dim(part_scales, store_pos, 0, keepdims=False)

        across = swap(own, "store", 2)
        beside = swap(own, "store", 1)
        diagonal = swap(across, "store", 1)

        everything = lax.all_gather(own, "tensor", axis=0, tiled=False)
        if context is not None:
            everything, context = lax.optimization_barrier((everything, context))
        total = base_rows(everything, own_scale, gains, query_key_value_weight)

        mine = slots.reshape(4, -1, halves, max(1, part_rows // RUN))[:, :, h].reshape(-1)
        partial = shrink_rows(
            place, mine, (own, beside, across, diagonal), part_scales, gain, down
        )
        pair = partial[:2] + swap(partial[2:], "store", 1)
        shrunk = pair[0] + swap(pair[1], "store", 2)
        shrunk = summed_over(shrunk, "tensor")
        shrunk = shrunk.astype(BF16)
        pair = jnp.stack([shrunk, swap(shrunk, "store", 2)])
        shrunk = jnp.concatenate([pair, swap(pair, "store", 1)], axis=0)
        grown = grow_rows(place, mine, shrunk, adapter_up_weight)
        pair = grown[:2] + swap(grown[2:], "store", 1)
        delta = pair[0] + swap(pair[1], "store", 2)

        qkv = (total + delta).astype(BF16)
        qkv = qkv.reshape(tensor_count, local, -1)
        moved = lax.all_to_all(qkv, "tensor", split_axis=0, concat_axis=0, tiled=True)
        if tensor_count != 4:
            q_columns = HEADS * HD // tensor_count
            parts = []
            for piece in (moved[..., :q_columns], moved[..., q_columns:]):
                joined = piece.transpose(1, 0, 2).reshape(local, 4, -1)
                parts.append(joined.transpose(1, 0, 2))
            moved = jnp.concatenate(parts, axis=2)

        here = lengths[h * part_rows : (h + 1) * part_rows]
        cosine, sine = angle_tables(here, unit)
        context = attend(
            here, ascending(here), moved, cosine, sine, key_value_cache, h * part_rows, unit
        )

        everything = lax.all_gather(context, "tensor", axis=0, tiled=False)
        if part_rows % RUN == 0:
            result = project(everything, output_weight)
        else:
            everything = everything.reshape(-1, HEADS * HD)
            result = jnp.dot(everything, output_weight, preferred_element_type=F32).astype(BF16)
            result = result.reshape(tensor_count, part_rows // unit, STEPS, unit, -1)
            result = result.transpose(2, 0, 1, 3, 4).reshape(STEPS, tensor_count, part_rows, -1)
        results.append(result)
    output = results[0] if halves == 1 else jnp.concatenate(results, axis=2)
    return output.reshape(STEPS, rows, -1)


def solution(mesh):
    in_specs = (
        P(None, ("groups", "store"), "tensor"),
        P(),
        P(None, "tensor"),
        P(None, "tensor"),
        P(("groups", "store"), "tensor", None),
        P(("groups", "store"), None, "tensor"),
        P(("groups", "store")),
        P("groups"),
        P(("groups", "store", "tensor")),
        P(("groups", "store", "tensor"), None, None, None),
    )
    out_specs = P(None, ("groups", "store"), "tensor")
    return jax.shard_map(
        on_device, mesh=mesh, in_specs=in_specs, out_specs=out_specs, check_vma=False
    )
```

```python
import functools

import jax
import jax.numpy as jnp
from jax import lax
from jax.experimental import pallas as pl
from jax.experimental.pallas import tpu as pltpu
from jax.sharding import PartitionSpec as P

HEADS = 32
KVH = 4
HD = 128
GROUP = HEADS // KVH
RUN = 8
STEPS = 2
LANES = 128
HALVES = 2

eps_norm = 1e-05
rope_base = 500000.0
masked = -1e30

MIB = 1 << 20
F32 = jnp.float32
BF16 = jnp.bfloat16
VMEM = pl.BlockSpec(memory_space=pltpu.VMEM)
SMEM = pl.BlockSpec(memory_space=pltpu.SMEM)
HBM = pl.BlockSpec(memory_space=pltpu.HBM)


def swap(values, axis, distance):
    count = lax.axis_size(axis)
    return lax.ppermute(values, axis, [(i, i ^ distance) for i in range(count)])


def line_gather(block, axis):
    up = down = block
    hops = []
    for hop in range(1, 4):
        up = lax.ppermute(up, axis, [(i, i + 1) for i in range(hop - 1, 3)])
        down = lax.ppermute(down, axis, [(i, i - 1) for i in range(4 - hop, 0, -1)])
        hops.append((up, down))
    return hops


def hop_owners(position, hop):
    below = position - hop
    above = position + hop
    return jnp.stack([jnp.where(below >= 0, below, -1), jnp.where(above < 4, above, -1)])


def block_kernel(count, has_total, owners, *refs):
    x_refs = refs[:count]
    scale_ref, gain_ref, w_ref = refs[count : count + 3]
    out_ref, held, sems = refs[-3:]
    _, tiles, depth, _ = held.shape

    def copy(j, k):
        first = pl.multiple_of((owners[j] * tiles + k) * depth, depth)
        return pltpu.make_async_copy(
            w_ref.at[pl.ds(first, depth), :], held.at[j, k], sems.at[j, k]
        )

    for j in range(count):

        @pl.when(owners[j] >= 0)
        def _():
            for k in range(tiles):
                copy(j, k).start()

    out_ref[...] = refs[count + 3][...] if has_total else jnp.zeros_like(out_ref)
    for j, x_ref in enumerate(x_refs):

        @pl.when(owners[j] >= 0)
        def _():
            scale = scale_ref[...]
            for k in range(tiles):
                span = slice(k * depth, (k + 1) * depth)
                first = pl.multiple_of((owners[j] * tiles + k) * depth, depth)
                gain = gain_ref[:, pl.ds(first, depth)]
                normed = (x_ref[:, span].astype(F32) * scale * gain).astype(BF16)
                copy(j, k).wait()
                out_ref[...] += jnp.dot(normed, held[j, k], preferred_element_type=F32)


def base_block(blocks, scale, gain, weight, owners, total):
    rows, depth = blocks[0].shape
    columns = weight.shape[1]
    tile = min(512, depth)
    count = len(blocks)
    operands = [owners, *blocks, scale, gain, weight]
    if total is not None:
        operands.append(total)
    return pl.pallas_call(
        functools.partial(block_kernel, count, total is not None),
        out_shape=jax.ShapeDtypeStruct((rows, columns), F32),
        in_specs=[SMEM] + [VMEM] * (count + 2) + [HBM] + [VMEM] * (total is not None),
        out_specs=VMEM,
        scratch_shapes=[
            pltpu.VMEM((count, depth // tile, tile, columns), BF16),
            pltpu.SemaphoreType.DMA((count, depth // tile)),
        ],
        compiler_params=pltpu.CompilerParams(vmem_limit_bytes=48 * MIB),
        cost_estimate=pl.CostEstimate(
            flops=2 * count * rows * depth * columns,
            bytes_accessed=2 * depth * (rows + columns) + 8 * rows * columns,
            transcendentals=0,
        ),
        name="base_block",
    )(*operands)


def base_kernel(x_ref, scale_ref, gain_ref, w_ref, out_ref, held, sems):
    owners, _, span = x_ref.shape
    tiles, depth, _ = held.shape
    copies = [
        pltpu.make_async_copy(w_ref.at[pl.ds(k * depth, depth), :], held.at[k], sems.at[k])
        for k in range(tiles)
    ]
    for copy in copies:
        copy.start()
    scale = scale_ref[...]
    for k, copy in enumerate(copies):
        owner, first = divmod(k * depth, span)
        gain = gain_ref[:, k * depth : (k + 1) * depth]
        rows = x_ref[owner, :, first : first + depth].astype(F32)
        normed = (rows * scale * gain).astype(BF16)
        copy.wait()
        product = jnp.dot(normed, held[k], preferred_element_type=F32)
        if k > 0:
            out_ref[...] += product
        else:
            out_ref[...] = product


def base_rows(x, scale, gain, weight):
    owners, rows, span = x.shape
    depth, columns = weight.shape
    tile = min(512, span)
    tiles = depth // tile
    return pl.pallas_call(
        base_kernel,
        out_shape=jax.ShapeDtypeStruct((rows, columns), F32),
        in_specs=[VMEM] * 3 + [HBM],
        out_specs=VMEM,
        scratch_shapes=[
            pltpu.VMEM((tiles, tile, columns), BF16),
            pltpu.SemaphoreType.DMA((tiles,)),
        ],
        compiler_params=pltpu.CompilerParams(vmem_limit_bytes=48 * MIB),
        cost_estimate=pl.CostEstimate(
            flops=2 * rows * depth * columns,
            bytes_accessed=2 * depth * (rows + columns) + 4 * rows * columns,
            transcendentals=0,
        ),
        name="base_rows",
    )(x, scale, gain, weight)


TEAM = 4
SLABS = (0, 2, 1, 3)


def list_runs(place_ref, slots, runs, jobs, start):
    def look(run, carry, slab, d):
        slot = slots[(place_ref[0] ^ d) * runs + run]

        @pl.when(slot >= 0)
        def _():
            jobs[carry] = slab * runs + run
            start(carry, d, run, slot)

        return carry + (slot >= 0).astype(jnp.int32)

    count = jnp.int32(0)
    for slab, d in enumerate(SLABS):
        count = lax.fori_loop(0, runs, functools.partial(look, slab=slab, d=d), count)
    return count


def work_in_teams(count, wait, work):
    def team(g, carry):
        for u in range(TEAM):

            @pl.when(g * TEAM + u < count)
            def _():
                wait(g * TEAM + u)

        work([jnp.minimum(g * TEAM + u, count - 1) for u in range(TEAM)])
        return carry

    lax.fori_loop(0, (count + TEAM - 1) // TEAM, team, 0)


def shrink_kernel(
    place_ref,
    slots,
    x0,
    x1,
    x2,
    x3,
    scale_ref,
    gain_ref,
    down_ref,
    keep_ref,
    send_ref,
    jobs,
    parts,
    held_x,
    held,
    x_sems,
    sems,
):
    runs = held.shape[0] // 4
    rank = held.shape[1]
    x_refs = (x0, x1, x2, x3)

    def x_copy(i, d, run):
        rows = pl.ds(pl.multiple_of(run * 16, 16), 16)
        return pltpu.make_async_copy(x_refs[d].at[rows, :], held_x.at[i], x_sems.at[i])

    def copy(i, slot):
        return pltpu.make_async_copy(down_ref.at[slot], held.at[i], sems.at[i])

    def start(i, d, run, slot):
        copy(i, slot).start()
        x_copy(i, d, run).start()

    def wait(i):
        copy(i, 0).wait()
        x_copy(i, 0, 0).wait()

    def work(members):
        results = []
        for i in members:
            job = jobs[i]
            slab = job // runs
            d = jnp.where(slab == 1, 2, jnp.where(slab == 2, 1, slab))
            rows = pl.ds(pl.multiple_of((job % runs) * 16, 16), 16)
            scale = scale_ref[place_ref[0] ^ d, rows, :]
            normed = (held_x[i].astype(F32) * scale * gain_ref[...]).astype(BF16)
            part = lax.dot_general(
                normed, held[i], (((1,), (1,)), ((), ())), preferred_element_type=F32
            )
            results.append((job, part))
        for job, part in results:
            parts[job] = part

    count = list_runs(place_ref, slots, runs, jobs, start)
    parts[...] = jnp.zeros_like(parts)
    work_in_teams(count, wait, work)
    for slab in range(4):
        for i in range(runs // 2):
            low = slab * runs + i
            out_ref = (keep_ref, send_ref)[slab // 2]
            out_ref[slab % 2, i * 16 : (i + 1) * 16, :] = jnp.concatenate(
                [parts[low], parts[low + runs // 2]], axis=1
            )


def shrink_rows(place, slots, blocks, scales, gain, down):
    rows, depth = blocks[0].shape
    rank = down.shape[1]
    runs = rows // 16
    return pl.pallas_call(
        shrink_kernel,
        out_shape=[jax.ShapeDtypeStruct((2, rows // 2, 2 * rank), F32)] * 2,
        in_specs=[SMEM] * 2 + [HBM] * 4 + [VMEM] * 2 + [HBM],
        out_specs=[VMEM] * 2,
        scratch_shapes=[
            pltpu.SMEM((4 * runs,), jnp.int32),
            pltpu.VMEM((4 * runs, 16, rank), F32),
            pltpu.VMEM((4 * runs, 16, depth), BF16),
            pltpu.VMEM((4 * runs, rank, depth), BF16),
            pltpu.SemaphoreType.DMA((4 * runs,)),
            pltpu.SemaphoreType.DMA((4 * runs,)),
        ],
        compiler_params=pltpu.CompilerParams(vmem_limit_bytes=54 * MIB),
        cost_estimate=pl.CostEstimate(
            flops=2 * rows * depth * rank,
            bytes_accessed=8 * rows * depth + down.size,
            transcendentals=0,
        ),
        name="shrink_rows",
    )(place, slots, *blocks, scales, gain, down)


def grow_kernel(
    place_ref, slots, s0, s1, up_ref, keep_ref, send_ref, jobs, parts, held, sems
):
    runs = held.shape[0] // 4
    rank = held.shape[1]

    def copy(i, slot):
        return pltpu.make_async_copy(up_ref.at[slot], held.at[i], sems.at[i])

    def start(i, d, run, slot):
        copy(i, slot).start()

    def wait(i):
        copy(i, 0).wait()

    def work(members):
        results = []
        for i in members:
            job = jobs[i]
            grown = jnp.dot(parts[job], held[i], preferred_element_type=F32)
            results.append((job, grown))
        for job, grown in results:
            rows = pl.ds(pl.multiple_of((job % runs) * 16, 16), 16)
            slab = job // runs

            @pl.when(slab < 2)
            def _():
                keep_ref[slab, rows, :] = grown

            @pl.when(slab >= 2)
            def _():
                send_ref[slab - 2, rows, :] = grown

    count = list_runs(place_ref, slots, runs, jobs, start)
    for slab in range(4):
        for i in range(runs // 2):
            low = slab * runs + i
            both = (s0, s1)[slab // 2][slab % 2, i * 16 : (i + 1) * 16, :]
            parts[low] = both[:, :rank]
            parts[low + runs // 2] = both[:, rank:]
    keep_ref[...] = jnp.zeros_like(keep_ref)
    send_ref[...] = jnp.zeros_like(send_ref)
    work_in_teams(count, wait, work)


def grow_rows(place, slots, kept, passed, up):
    _, pair_rows, _ = kept.shape
    rows = 2 * pair_rows
    rank, columns = up.shape[1:]
    runs = rows // 16
    return pl.pallas_call(
        grow_kernel,
        out_shape=[jax.ShapeDtypeStruct((2, rows, columns), F32)] * 2,
        in_specs=[SMEM, SMEM, VMEM, VMEM, HBM],
        out_specs=[VMEM] * 2,
        scratch_shapes=[
            pltpu.SMEM((4 * runs,), jnp.int32),
            pltpu.VMEM((4 * runs, 16, rank), BF16),
            pltpu.VMEM((4 * runs, rank, columns), BF16),
            pltpu.SemaphoreType.DMA((4 * runs,)),
        ],
        compiler_params=pltpu.CompilerParams(vmem_limit_bytes=60 * MIB),
        cost_estimate=pl.CostEstimate(
            flops=2 * rows * rank * columns,
            bytes_accessed=8 * rows * columns + up.size,
            transcendentals=0,
        ),
        name="grow_rows",
    )(place, slots, kept, passed, up)


def attend_kernel(
    unit,
    first_row,
    lengths,
    order,
    qkv_ref,
    cos_ref,
    sin_ref,
    cache_ref,
    out_ref,
    queries,
    keys,
    values,
    context,
    held,
    sems,
):
    rows, _, cached, _ = held.shape
    local = STEPS * rows
    q_columns = GROUP * HD
    part = cached // 2
    scale = HD ** (-0.5)
    team = min(4, rows)

    def copy(r, b):
        span = pl.ds(b * part, part)
        return pltpu.make_async_copy(
            cache_ref.at[first_row + r, :, span, :], held.at[r, :, span, :], sems.at[r, b]
        )

    def longest(group):
        return lengths[order[group * team + team - 1]]

    def fetch(i, carry):
        r = order[i]
        copy(r, 0).start()

        @pl.when(longest(i // team) > part)
        def _():
            copy(r, 1).start()

        return carry

    lax.fori_loop(0, rows, fetch, 0)

    cosine = cos_ref[...]
    sine = sin_ref[...]

    def rotated(x):
        x = x.astype(F32)
        turned = x * cosine + pltpu.roll(x, HD // 2, 1) * sine
        return turned.astype(BF16).astype(F32)

    for k in range(KVH):
        for g in range(GROUP):
            queries[k, g * local : (g + 1) * local, :] = rotated(
                qkv_ref[k, :, g * HD : (g + 1) * HD]
            )
        place = q_columns + (k % 2) * HD
        keys[k] = rotated(qkv_ref[k // 2, :, place : place + HD])
        values[k] = qkv_ref[2 + k // 2, :, place : place + HD].astype(F32)

    early = lax.broadcasted_iota(jnp.int32, (4 * GROUP, 1), 0) % (2 * GROUP) < GROUP

    def scores(r, at, pair, span, live):
        heads = (2 * pair, 2 * pair + 1)
        query = [
            jnp.concatenate(
                [queries[k, pl.ds(at[s], GROUP, stride=local), :] for s in range(STEPS)], axis=0
            )
            for k in heads
        ]
        blank = jnp.zeros((2 * GROUP, HD), F32)
        spread = jnp.concatenate(
            [
                jnp.concatenate([query[0], blank], axis=1),
                jnp.concatenate([blank, query[1]], axis=1),
            ],
            axis=0,
        ).astype(BF16)
        old_keys = jnp.concatenate([held[r, k, :span, :HD] for k in heads], axis=1)
        old = lax.dot_general(
            spread, old_keys, (((1,), (1,)), ((), ())), preferred_element_type=F32
        )
        old = jnp.where(live, old * scale, masked)
        fresh = []
        for t in range(STEPS):
            both = jnp.concatenate(
                [
                    jnp.sum(query[i] * keys[k, pl.ds(at[t], 1), :], axis=1, keepdims=True)
                    for i, k in enumerate(heads)
                ],
                axis=0,
            )
            fresh.append(both * scale)
        fresh[1] = jnp.where(early, masked, fresh[1])
        return old, fresh

    def soften(old, fresh):
        peak = jnp.maximum(jnp.max(old, axis=1, keepdims=True), jnp.maximum(fresh[0], fresh[1]))
        p_old = jnp.exp(old - peak)
        p_new = [jnp.exp(f - peak) for f in fresh]
        total = jnp.sum(p_old, axis=1, keepdims=True) + (p_new[0] + p_new[1])
        return p_old.astype(BF16), [p.astype(BF16).astype(F32) for p in p_new], total

    def mix(r, at, pair, span, w_old, w_new, total):
        heads = (2 * pair, 2 * pair + 1)
        old_values = jnp.concatenate([held[r, k, :span, HD:] for k in heads], axis=1)
        mixed = jnp.dot(w_old, old_values, preferred_element_type=F32)
        for i, k in enumerate(heads):
            own = slice(i * 2 * GROUP, (i + 1) * 2 * GROUP)
            result = mixed[own, i * HD : (i + 1) * HD]
            for t in range(STEPS):
                result = result + w_new[t][own] * values[k, pl.ds(at[t], 1), :]
            result = result / total[own]
            for s in range(STEPS):
                context[k, pl.ds(at[s], GROUP, stride=local), :] = result[
                    s * GROUP : (s + 1) * GROUP
                ]

    def attend_team(members, span):
        jobs = []
        for r in members:
            at = [(r // unit) * (STEPS * unit) + s * unit + r % unit for s in range(STEPS)]
            live = lax.broadcasted_iota(jnp.int32, (4 * GROUP, span), 1) < lengths[r]
            for pair in range(KVH // 2):
                jobs.append((r, at, pair, scores(r, at, pair, span, live)))
        softened = [soften(*job[3]) for job in jobs]
        for (r, at, pair, _), weights in zip(jobs, softened):
            mix(r, at, pair, span, *weights)

    def each(group, carry):
        members = [order[group * team + i] for i in range(team)]
        wide = longest(group) > part
        for r in members:
            copy(r, 0).wait()

        @pl.when(wide)
        def _():
            for r in members:
                copy(r, 1).wait()
            attend_team(members, cached)

        @pl.when(jnp.logical_not(wide))
        def _():
            attend_team(members, part)

        return carry

    lax.fori_loop(0, rows // team, each, 0)
    for k in range(KVH):
        for g in range(GROUP):
            place = (k * GROUP + g) * HD
            out_ref[:, place : place + HD] = context[k, g * local : (g + 1) * local, :].astype(BF16)


def attend(lengths, order, qkv, cosine, sine, cache, first_row, unit):
    rows = lengths.shape[0]
    local = STEPS * rows
    _, kv_heads, cached, width = cache.shape
    return pl.pallas_call(
        functools.partial(attend_kernel, unit, first_row),
        out_shape=jax.ShapeDtypeStruct((local, HEADS * HD), BF16),
        in_specs=[SMEM, SMEM, VMEM, VMEM, VMEM, HBM],
        out_specs=VMEM,
        scratch_shapes=[
            pltpu.VMEM((KVH, GROUP * local, HD), F32),
            pltpu.VMEM((KVH, local, HD), F32),
            pltpu.VMEM((KVH, local, HD), F32),
            pltpu.VMEM((KVH, GROUP * local, HD), F32),
            pltpu.VMEM((rows, kv_heads, cached, width), BF16),
            pltpu.SemaphoreType.DMA((rows, 2)),
        ],
        compiler_params=pltpu.CompilerParams(vmem_limit_bytes=48 * MIB),
        cost_estimate=pl.CostEstimate(
            flops=4 * local * HEADS * HD * cached,
            bytes_accessed=2 * rows * kv_heads * cached * width,
            transcendentals=local * HEADS * cached,
        ),
        name="attend",
    )(lengths, order, qkv, cosine, sine, cache)


def out_kernel(context_ref, w_ref, out_ref, total, held, sems):
    owners, local, _ = context_ref.shape
    rows = local // STEPS
    unit = min(RUN, rows)
    tiles, depth, columns = held.shape
    copies = [
        pltpu.make_async_copy(w_ref.at[pl.ds(k * depth, depth), :], held.at[k], sems.at[k])
        for k in range(tiles)
    ]
    for copy in copies:
        copy.start()
    width = min(512, columns)
    for k, copy in enumerate(copies):
        lhs = context_ref[:, :, k * depth : (k + 1) * depth].reshape(owners * local, depth)
        copy.wait()
        for j in range(columns // width):
            span = slice(j * width, (j + 1) * width)
            product = jnp.dot(lhs, held[k, :, span], preferred_element_type=F32)
            if k > 0:
                product = total[:, span] + product
            if k < tiles - 1:
                total[:, span] = product
                continue
            block = product.reshape(owners, rows // unit, STEPS, unit, width)
            for s in range(STEPS):
                piece = block[:, :, s].reshape(owners, rows, width)
                out_ref[s, :, :, span] = piece.astype(BF16)


def project(context, weight):
    owners, local, depth = context.shape
    columns = weight.shape[1]
    tile = min(512, depth)
    rows = local // STEPS
    return pl.pallas_call(
        out_kernel,
        out_shape=jax.ShapeDtypeStruct((STEPS, owners, rows, columns), BF16),
        in_specs=[VMEM, HBM],
        out_specs=VMEM,
        scratch_shapes=[
            pltpu.VMEM((owners * local, columns), F32),
            pltpu.VMEM((depth // tile, tile, columns), BF16),
            pltpu.SemaphoreType.DMA((depth // tile,)),
        ],
        compiler_params=pltpu.CompilerParams(vmem_limit_bytes=52 * MIB),
        cost_estimate=pl.CostEstimate(
            flops=2 * owners * local * depth * columns,
            bytes_accessed=2 * depth * columns + 2 * owners * local * (depth + columns),
            transcendentals=0,
        ),
        name="project",
    )(context, weight)


def lookup(identity, table):
    hits = identity[:, None] == jnp.arange(table.shape[0], dtype=jnp.int32)[None, :]
    return jnp.sum(jnp.where(hits, table[None, :], 0), axis=1)


def ascending(lengths):
    count = lengths.shape[0]
    rows = jnp.arange(count, dtype=jnp.int32)
    keyed = lengths * count + rows
    rank = jnp.sum((keyed[None, :] < keyed[:, None]).astype(jnp.int32), axis=1)
    return jnp.sum(jnp.where(rank[:, None] == rows[None, :], rows[:, None], 0), axis=0)


def angle_tables(lengths, unit):
    steps = jnp.arange(STEPS, dtype=jnp.int32)
    position = lengths.reshape(-1, 1, unit) + steps[None, :, None]
    freq = rope_base ** (-(jnp.arange(HD // 2, dtype=F32) * 2.0 / HD))
    angles = position.reshape(-1).astype(F32)[:, None] * freq
    cosine = jnp.cos(angles)
    sine = jnp.sin(angles)
    return jnp.concatenate([cosine, cosine], 1), jnp.concatenate([-sine, sine], 1)


def on_device(
    hidden,
    input_norm_scale,
    query_key_value_weight,
    output_weight,
    adapter_down_weight,
    adapter_up_weight,
    row_adapter_index,
    adapter_store_slot,
    lengths,
    key_value_cache,
):
    tensor_count = lax.axis_size("tensor")
    tensor_pos = lax.axis_index("tensor")
    store_pos = lax.axis_index("store")
    _, rows, span = hidden.shape
    model_width = input_norm_scale.shape[0]
    rows_here = lengths.shape[0]
    unit = min(RUN, rows_here)
    halves = HALVES if rows_here % (HALVES * RUN) == 0 else 1
    part_rows = rows_here // halves
    local = STEPS * part_rows
    held_slots = adapter_down_weight.shape[0]
    rank = adapter_down_weight.shape[2]

    raw = hidden.reshape(STEPS, tensor_count, halves, part_rows // unit, unit, span)
    raw = raw.transpose(2, 1, 3, 0, 4, 5).reshape(STEPS * rows, span)
    values = raw.astype(F32)
    squares = jnp.sum(values * values, axis=1)
    own_runs = row_adapter_index[::RUN]
    if halves > 1:
        own_runs = own_runs.reshape(tensor_count, halves, -1).swapaxes(0, 1).reshape(-1)
    told = jnp.concatenate([squares, own_runs.astype(F32)])
    told = lax.all_gather(told, ("store", "tensor"), axis=0, tiled=False)
    told = told.reshape(-1, tensor_count, told.shape[-1])
    runs = told[:, 0, STEPS * rows :].astype(jnp.int32)
    told = jnp.sum(told[:, :, : STEPS * rows], axis=1)
    scales = lax.rsqrt(told / model_width + eps_norm)
    slots = lookup(runs.reshape(-1), adapter_store_slot).reshape(runs.shape)
    slots = jnp.where(slots // held_slots == store_pos, slots % held_slots, -1)
    place = store_pos.reshape(1).astype(jnp.int32)
    gains = input_norm_scale.reshape(1, -1)
    gain = lax.dynamic_slice_in_dim(gains, tensor_pos * span, span, 1)
    scales = scales[:, :, None]
    own_scale = lax.dynamic_index_in_dim(scales, store_pos, 0, keepdims=False)

    line = tensor_count == 4
    owners = [tensor_pos.reshape(1).astype(jnp.int32)]
    owners += [hop_owners(tensor_pos, hop) for hop in (1, 2, 3)]
    hops = line_gather(raw, "tensor") if line else None

    across = swap(raw, "store", 2)
    beside = swap(raw, "store", 1)
    diagonal = swap(across, "store", 1)
    mine = slots.reshape(-1)
    down = jnp.swapaxes(adapter_down_weight, 1, 2)
    if line:
        diagonal, hops[0] = lax.optimization_barrier((diagonal, hops[0]))
    kept, passed = shrink_rows(place, mine, (raw, beside, across, diagonal), scales, gain, down)
    kept = kept + swap(passed, "store", 1)
    shrunk = kept[0] + swap(kept[1], "store", 2)
    shrunk = lax.all_gather(shrunk, "tensor", axis=0, tiled=False)
    if line:
        shrunk, hops[1] = lax.optimization_barrier((shrunk, hops[1]))
    shrunk = jnp.sum(shrunk, axis=0).astype(BF16)
    shrunk = jnp.stack([shrunk, swap(shrunk, "store", 2)])
    kept, passed = grow_rows(place, mine, shrunk, swap(shrunk, "store", 1), adapter_up_weight)

    weight = query_key_value_weight
    if line:
        raw, passed = lax.optimization_barrier((raw, passed))
        blocks = (raw,) + hops[0] + hops[1]
        near = jnp.concatenate(owners[:3])
        total = base_block(blocks, own_scale, gains, weight, near, None)
        total = base_block(hops[2], own_scale, gains, weight, owners[3], total)
    else:
        everything = lax.all_gather(raw, "tensor", axis=0, tiled=False)
        total = base_rows(everything, own_scale, gains, weight)
    passed = swap(passed, "store", 1)

    count = tensor_count * local
    gathered = []
    context = None
    for h in range(halves):
        part = slice(h * count, (h + 1) * count)
        delta = swap(kept[1, part] + passed[1, part], "store", 2)
        delta = (kept[0, part] + passed[0, part]) + delta
        qkv = (total[part] + delta).astype(BF16)
        qkv = qkv.reshape(tensor_count, local, -1)
        moved = lax.all_to_all(qkv, "tensor", split_axis=0, concat_axis=0, tiled=True)
        if tensor_count != 4:
            q_columns = HEADS * HD // tensor_count
            parts = []
            for piece in (moved[..., :q_columns], moved[..., q_columns:]):
                joined = piece.transpose(1, 0, 2).reshape(local, 4, -1)
                parts.append(joined.transpose(1, 0, 2))
            moved = jnp.concatenate(parts, axis=2)

        here = lengths[h * part_rows : (h + 1) * part_rows]
        cosine, sine = angle_tables(here, unit)
        context = attend(
            here, ascending(here), moved, cosine, sine, key_value_cache, h * part_rows, unit
        )

        gathered.append(lax.all_gather(context, "tensor", axis=0, tiled=False))

    previous = context
    results = []
    for everything in gathered:
        everything, previous = lax.optimization_barrier((everything, previous))
        if part_rows % RUN == 0:
            result = project(everything, output_weight)
        else:
            everything = everything.reshape(-1, HEADS * HD)
            result = jnp.dot(everything, output_weight, preferred_element_type=F32).astype(BF16)
            result = result.reshape(tensor_count, part_rows // unit, STEPS, unit, -1)
            result = result.transpose(2, 0, 1, 3, 4).reshape(STEPS, tensor_count, part_rows, -1)
        results.append(result)
        previous = result
    output = results[0] if halves == 1 else jnp.concatenate(results, axis=2)
    return output.reshape(STEPS, rows, -1)


def solution(mesh):
    in_specs = (
        P(None, ("groups", "store"), "tensor"),
        P(),
        P(None, "tensor"),
        P(None, "tensor"),
        P(("groups", "store"), "tensor", None),
        P(("groups", "store"), None, "tensor"),
        P(("groups", "store")),
        P("groups"),
        P(("groups", "store", "tensor")),
        P(("groups", "store", "tensor"), None, None, None),
    )
    out_specs = P(None, ("groups", "store"), "tensor")
    return jax.shard_map(
        on_device, mesh=mesh, in_specs=in_specs, out_specs=out_specs, check_vma=False
    )
```

```python
import functools

import jax
import jax.numpy as jnp
from jax import lax
from jax.experimental import pallas as pl
from jax.experimental.pallas import tpu as pltpu
from jax.sharding import PartitionSpec as P

HEADS = 32
KVH = 4
HD = 128
GROUP = HEADS // KVH
RUN = 8
STEPS = 2
LANES = 128
HALVES = 2

eps_norm = 1e-05
rope_base = 500000.0
masked = -1e30

MIB = 1 << 20
F32 = jnp.float32
BF16 = jnp.bfloat16
VMEM = pl.BlockSpec(memory_space=pltpu.VMEM)
SMEM = pl.BlockSpec(memory_space=pltpu.SMEM)
HBM = pl.BlockSpec(memory_space=pltpu.HBM)


def swap(values, axis, distance):
    count = lax.axis_size(axis)
    return lax.ppermute(values, axis, [(i, i ^ distance) for i in range(count)])


def summed_over(values, axis):
    distance = 1
    while distance < lax.axis_size(axis):
        values = values + swap(values, axis, distance)
        distance *= 2
    return values


def line_gather(block, axis):
    up = down = block
    hops = []
    for hop in range(1, 4):
        up = lax.ppermute(up, axis, [(i, i + 1) for i in range(hop - 1, 3)])
        down = lax.ppermute(down, axis, [(i, i - 1) for i in range(4 - hop, 0, -1)])
        hops.append((up, down))
    return hops


def hop_owners(position, hop):
    below = position - hop
    above = position + hop
    return jnp.stack([jnp.where(below >= 0, below, -1), jnp.where(above < 4, above, -1)])


def block_kernel(count, has_total, owners, *refs):
    x_refs = refs[:count]
    scale_ref, gain_ref, w_ref = refs[count : count + 3]
    out_ref, held, sems = refs[-3:]
    _, tiles, depth, _ = held.shape

    def copy(j, k):
        first = pl.multiple_of((owners[j] * tiles + k) * depth, depth)
        return pltpu.make_async_copy(
            w_ref.at[pl.ds(first, depth), :], held.at[j, k], sems.at[j, k]
        )

    for j in range(count):

        @pl.when(owners[j] >= 0)
        def _():
            for k in range(tiles):
                copy(j, k).start()

    out_ref[...] = refs[count + 3][...] if has_total else jnp.zeros_like(out_ref)
    for j, x_ref in enumerate(x_refs):

        @pl.when(owners[j] >= 0)
        def _():
            scale = scale_ref[...]
            for k in range(tiles):
                span = slice(k * depth, (k + 1) * depth)
                first = pl.multiple_of((owners[j] * tiles + k) * depth, depth)
                gain = gain_ref[:, pl.ds(first, depth)]
                normed = (x_ref[:, span].astype(F32) * scale * gain).astype(BF16)
                copy(j, k).wait()
                out_ref[...] += jnp.dot(normed, held[j, k], preferred_element_type=F32)


def base_block(blocks, scale, gain, weight, owners, total):
    rows, depth = blocks[0].shape
    columns = weight.shape[1]
    tile = min(512, depth)
    count = len(blocks)
    operands = [owners, *blocks, scale, gain, weight]
    if total is not None:
        operands.append(total)
    return pl.pallas_call(
        functools.partial(block_kernel, count, total is not None),
        out_shape=jax.ShapeDtypeStruct((rows, columns), F32),
        in_specs=[SMEM] + [VMEM] * (count + 2) + [HBM] + [VMEM] * (total is not None),
        out_specs=VMEM,
        scratch_shapes=[
            pltpu.VMEM((count, depth // tile, tile, columns), BF16),
            pltpu.SemaphoreType.DMA((count, depth // tile)),
        ],
        compiler_params=pltpu.CompilerParams(vmem_limit_bytes=48 * MIB),
        cost_estimate=pl.CostEstimate(
            flops=2 * count * rows * depth * columns,
            bytes_accessed=2 * depth * (rows + columns) + 8 * rows * columns,
            transcendentals=0,
        ),
        name="base_block",
    )(*operands)


def base_kernel(first_row, place_ref, x_ref, scale_ref, gain_ref, own_ref, w_ref, out_ref, held, sems):
    owners, _, span = x_ref.shape
    rows = scale_ref.shape[0]
    tiles, depth, _ = held.shape
    tiles_each = span // depth

    def spot(k):
        owner = lax.rem(place_ref[0] + 1 + k // tiles_each, owners)
        return owner, pl.multiple_of((owner * tiles_each + k % tiles_each) * depth, depth)

    copies = [
        pltpu.make_async_copy(w_ref.at[pl.ds(spot(k)[1], depth), :], held.at[k], sems.at[k])
        for k in range(tiles)
    ]
    for copy in copies:
        copy.start()
    scale = scale_ref[...]
    out_ref[...] = own_ref[first_row : first_row + rows, :]
    for k, copy in enumerate(copies):
        owner, first = spot(k)
        inner = (k % tiles_each) * depth
        gain = gain_ref[:, pl.ds(first, depth)]
        part = x_ref[owner, first_row : first_row + rows, inner : inner + depth].astype(F32)
        normed = (part * scale * gain).astype(BF16)
        copy.wait()
        out_ref[...] += jnp.dot(normed, held[k], preferred_element_type=F32)


def base_rows(place, x, scale, gain, own, weight, first_row):
    owners, _, span = x.shape
    rows = scale.shape[0]
    columns = weight.shape[1]
    tile = min(512, span)
    tiles = (owners - 1) * span // tile
    return pl.pallas_call(
        functools.partial(base_kernel, first_row),
        out_shape=jax.ShapeDtypeStruct((rows, columns), F32),
        in_specs=[SMEM] + [VMEM] * 4 + [HBM],
        out_specs=VMEM,
        scratch_shapes=[
            pltpu.VMEM((tiles, tile, columns), BF16),
            pltpu.SemaphoreType.DMA((tiles,)),
        ],
        compiler_params=pltpu.CompilerParams(vmem_limit_bytes=48 * MIB),
        cost_estimate=pl.CostEstimate(
            flops=2 * rows * tiles * tile * columns,
            bytes_accessed=2 * tiles * tile * (rows + columns) + 8 * rows * columns,
            transcendentals=0,
        ),
        name="base_rows",
    )(place, x, scale, gain, own, weight)


TEAM = 4
SLABS = (0, 2, 1, 3)


def list_runs(place_ref, slots, runs, jobs, start):
    def look(run, carry, slab, d):
        slot = slots[(place_ref[0] ^ d) * runs + run]

        @pl.when(slot >= 0)
        def _():
            jobs[carry] = slab * runs + run
            start(carry, d, run, slot)

        return carry + (slot >= 0).astype(jnp.int32)

    count = jnp.int32(0)
    for slab, d in enumerate(SLABS):
        count = lax.fori_loop(0, runs, functools.partial(look, slab=slab, d=d), count)
    return count


def work_in_teams(count, wait, work):
    def team(g, carry):
        for u in range(TEAM):

            @pl.when(g * TEAM + u < count)
            def _():
                wait(g * TEAM + u)

        work([jnp.minimum(g * TEAM + u, count - 1) for u in range(TEAM)])
        return carry

    lax.fori_loop(0, (count + TEAM - 1) // TEAM, team, 0)


def shrink_kernel(
    place_ref,
    slots,
    x0,
    x1,
    x2,
    x3,
    scale_ref,
    gain_ref,
    down_ref,
    keep_ref,
    send_ref,
    jobs,
    parts,
    held_x,
    held,
    x_sems,
    sems,
):
    runs = held.shape[0] // 4
    rank = held.shape[1]
    x_refs = (x0, x1, x2, x3)

    def x_copy(i, d, run):
        rows = pl.ds(pl.multiple_of(run * 16, 16), 16)
        return pltpu.make_async_copy(x_refs[d].at[rows, :], held_x.at[i], x_sems.at[i])

    def copy(i, slot):
        return pltpu.make_async_copy(down_ref.at[slot], held.at[i], sems.at[i])

    def start(i, d, run, slot):
        copy(i, slot).start()
        x_copy(i, d, run).start()

    def wait(i):
        copy(i, 0).wait()
        x_copy(i, 0, 0).wait()

    def work(members):
        results = []
        for i in members:
            job = jobs[i]
            slab = job // runs
            d = jnp.where(slab == 1, 2, jnp.where(slab == 2, 1, slab))
            rows = pl.ds(pl.multiple_of((job % runs) * 16, 16), 16)
            scale = scale_ref[place_ref[0] ^ d, rows, :]
            normed = (held_x[i].astype(F32) * scale * gain_ref[...]).astype(BF16)
            part = lax.dot_general(
                normed, held[i], (((1,), (1,)), ((), ())), preferred_element_type=F32
            )
            results.append((job, part))
        for job, part in results:
            parts[job] = part

    count = list_runs(place_ref, slots, runs, jobs, start)
    parts[...] = jnp.zeros_like(parts)
    work_in_teams(count, wait, work)
    for slab in range(4):
        for i in range(runs // 2):
            low = slab * runs + i
            out_ref = (keep_ref, send_ref)[slab // 2]
            out_ref[slab % 2, i * 16 : (i + 1) * 16, :] = jnp.concatenate(
                [parts[low], parts[low + runs // 2]], axis=1
            )


def shrink_rows(place, slots, blocks, scales, gain, down):
    rows, depth = blocks[0].shape
    rank = down.shape[1]
    runs = rows // 16
    return pl.pallas_call(
        shrink_kernel,
        out_shape=[jax.ShapeDtypeStruct((2, rows // 2, 2 * rank), F32)] * 2,
        in_specs=[SMEM] * 2 + [HBM] * 4 + [VMEM] * 2 + [HBM],
        out_specs=[VMEM] * 2,
        scratch_shapes=[
            pltpu.SMEM((4 * runs,), jnp.int32),
            pltpu.VMEM((4 * runs, 16, rank), F32),
            pltpu.VMEM((4 * runs, 16, depth), BF16),
            pltpu.VMEM((4 * runs, rank, depth), BF16),
            pltpu.SemaphoreType.DMA((4 * runs,)),
            pltpu.SemaphoreType.DMA((4 * runs,)),
        ],
        compiler_params=pltpu.CompilerParams(vmem_limit_bytes=54 * MIB),
        cost_estimate=pl.CostEstimate(
            flops=2 * rows * depth * rank,
            bytes_accessed=8 * rows * depth + down.size,
            transcendentals=0,
        ),
        name="shrink_rows",
    )(place, slots, *blocks, scales, gain, down)


def grow_kernel(
    place_ref, slots, s0, s1, up_ref, keep_ref, send_ref, jobs, parts, held, sems
):
    runs = held.shape[0] // 4
    rank = held.shape[1]

    def copy(i, slot):
        return pltpu.make_async_copy(up_ref.at[slot], held.at[i], sems.at[i])

    def start(i, d, run, slot):
        copy(i, slot).start()

    def wait(i):
        copy(i, 0).wait()

    def work(members):
        results = []
        for i in members:
            job = jobs[i]
            grown = jnp.dot(parts[job], held[i], preferred_element_type=F32)
            results.append((job, grown))
        for job, grown in results:
            rows = pl.ds(pl.multiple_of((job % runs) * 16, 16), 16)
            slab = job // runs

            @pl.when(slab < 2)
            def _():
                keep_ref[slab, rows, :] = grown

            @pl.when(slab >= 2)
            def _():
                send_ref[slab - 2, rows, :] = grown

    count = list_runs(place_ref, slots, runs, jobs, start)
    for slab in range(4):
        for i in range(runs // 2):
            low = slab * runs + i
            both = (s0, s1)[slab // 2][slab % 2, i * 16 : (i + 1) * 16, :]
            parts[low] = both[:, :rank]
            parts[low + runs // 2] = both[:, rank:]
    keep_ref[...] = jnp.zeros_like(keep_ref)
    send_ref[...] = jnp.zeros_like(send_ref)
    work_in_teams(count, wait, work)


def grow_rows(place, slots, kept, passed, up):
    _, pair_rows, _ = kept.shape
    rows = 2 * pair_rows
    rank, columns = up.shape[1:]
    runs = rows // 16
    return pl.pallas_call(
        grow_kernel,
        out_shape=[jax.ShapeDtypeStruct((2, rows, columns), F32)] * 2,
        in_specs=[SMEM, SMEM, VMEM, VMEM, HBM],
        out_specs=[VMEM] * 2,
        scratch_shapes=[
            pltpu.SMEM((4 * runs,), jnp.int32),
            pltpu.VMEM((4 * runs, 16, rank), BF16),
            pltpu.VMEM((4 * runs, rank, columns), BF16),
            pltpu.SemaphoreType.DMA((4 * runs,)),
        ],
        compiler_params=pltpu.CompilerParams(vmem_limit_bytes=60 * MIB),
        cost_estimate=pl.CostEstimate(
            flops=2 * rows * rank * columns,
            bytes_accessed=8 * rows * columns + up.size,
            transcendentals=0,
        ),
        name="grow_rows",
    )(place, slots, kept, passed, up)


def attend_kernel(
    unit,
    first_row,
    lengths,
    order,
    qkv_ref,
    cos_ref,
    sin_ref,
    cache_ref,
    out_ref,
    queries,
    keys,
    values,
    context,
    held,
    sems,
):
    rows, _, cached, _ = held.shape
    local = STEPS * rows
    q_columns = GROUP * HD
    part = cached // 2
    scale = HD ** (-0.5)
    team = min(4, rows)

    def copy(r, b):
        span = pl.ds(b * part, part)
        return pltpu.make_async_copy(
            cache_ref.at[first_row + r, :, span, :], held.at[r, :, span, :], sems.at[r, b]
        )

    def longest(group):
        return lengths[order[group * team + team - 1]]

    def fetch(i, carry):
        r = order[i]
        copy(r, 0).start()

        @pl.when(longest(i // team) > part)
        def _():
            copy(r, 1).start()

        return carry

    lax.fori_loop(0, rows, fetch, 0)

    cosine = cos_ref[...]
    sine = sin_ref[...]

    def rotated(x):
        x = x.astype(F32)
        turned = x * cosine + pltpu.roll(x, HD // 2, 1) * sine
        return turned.astype(BF16).astype(F32)

    for k in range(KVH):
        for g in range(GROUP):
            queries[k, g * local : (g + 1) * local, :] = rotated(
                qkv_ref[k, :, g * HD : (g + 1) * HD]
            )
        place = q_columns + (k % 2) * HD
        keys[k] = rotated(qkv_ref[k // 2, :, place : place + HD])
        values[k] = qkv_ref[2 + k // 2, :, place : place + HD].astype(F32)

    early = lax.broadcasted_iota(jnp.int32, (4 * GROUP, 1), 0) % (2 * GROUP) < GROUP

    def scores(r, at, pair, span, live):
        heads = (2 * pair, 2 * pair + 1)
        query = [
            jnp.concatenate(
                [queries[k, pl.ds(at[s], GROUP, stride=local), :] for s in range(STEPS)], axis=0
            )
            for k in heads
        ]
        blank = jnp.zeros((2 * GROUP, HD), F32)
        spread = jnp.concatenate(
            [
                jnp.concatenate([query[0], blank], axis=1),
                jnp.concatenate([blank, query[1]], axis=1),
            ],
            axis=0,
        ).astype(BF16)
        old_keys = jnp.concatenate([held[r, k, :span, :HD] for k in heads], axis=1)
        old = lax.dot_general(
            spread, old_keys, (((1,), (1,)), ((), ())), preferred_element_type=F32
        )
        old = jnp.where(live, old * scale, masked)
        fresh = []
        for t in range(STEPS):
            both = jnp.concatenate(
                [
                    jnp.sum(query[i] * keys[k, pl.ds(at[t], 1), :], axis=1, keepdims=True)
                    for i, k in enumerate(heads)
                ],
                axis=0,
            )
            fresh.append(both * scale)
        fresh[1] = jnp.where(early, masked, fresh[1])
        return old, fresh

    def soften(old, fresh):
        peak = jnp.maximum(jnp.max(old, axis=1, keepdims=True), jnp.maximum(fresh[0], fresh[1]))
        p_old = jnp.exp(old - peak)
        p_new = [jnp.exp(f - peak) for f in fresh]
        total = jnp.sum(p_old, axis=1, keepdims=True) + (p_new[0] + p_new[1])
        return p_old.astype(BF16), [p.astype(BF16).astype(F32) for p in p_new], total

    def mix(r, at, pair, span, w_old, w_new, total):
        heads = (2 * pair, 2 * pair + 1)
        old_values = jnp.concatenate([held[r, k, :span, HD:] for k in heads], axis=1)
        mixed = jnp.dot(w_old, old_values, preferred_element_type=F32)
        for i, k in enumerate(heads):
            own = slice(i * 2 * GROUP, (i + 1) * 2 * GROUP)
            result = mixed[own, i * HD : (i + 1) * HD]
            for t in range(STEPS):
                result = result + w_new[t][own] * values[k, pl.ds(at[t], 1), :]
            result = result / total[own]
            for s in range(STEPS):
                context[k, pl.ds(at[s], GROUP, stride=local), :] = result[
                    s * GROUP : (s + 1) * GROUP
                ]

    def attend_team(members, span):
        jobs = []
        for r in members:
            at = [(r // unit) * (STEPS * unit) + s * unit + r % unit for s in range(STEPS)]
            live = lax.broadcasted_iota(jnp.int32, (4 * GROUP, span), 1) < lengths[r]
            for pair in range(KVH // 2):
                jobs.append((r, at, pair, scores(r, at, pair, span, live)))
        softened = [soften(*job[3]) for job in jobs]
        for (r, at, pair, _), weights in zip(jobs, softened):
            mix(r, at, pair, span, *weights)

    def each(group, carry):
        members = [order[group * team + i] for i in range(team)]
        wide = longest(group) > part
        for r in members:
            copy(r, 0).wait()

        @pl.when(wide)
        def _():
            for r in members:
                copy(r, 1).wait()
            attend_team(members, cached)

        @pl.when(jnp.logical_not(wide))
        def _():
            attend_team(members, part)

        return carry

    lax.fori_loop(0, rows // team, each, 0)
    for k in range(KVH):
        for g in range(GROUP):
            place = (k * GROUP + g) * HD
            out_ref[:, place : place + HD] = context[k, g * local : (g + 1) * local, :].astype(BF16)


def attend(lengths, order, qkv, cosine, sine, cache, first_row, unit):
    rows = lengths.shape[0]
    local = STEPS * rows
    _, kv_heads, cached, width = cache.shape
    return pl.pallas_call(
        functools.partial(attend_kernel, unit, first_row),
        out_shape=jax.ShapeDtypeStruct((local, HEADS * HD), BF16),
        in_specs=[SMEM, SMEM, VMEM, VMEM, VMEM, HBM],
        out_specs=VMEM,
        scratch_shapes=[
            pltpu.VMEM((KVH, GROUP * local, HD), F32),
            pltpu.VMEM((KVH, local, HD), F32),
            pltpu.VMEM((KVH, local, HD), F32),
            pltpu.VMEM((KVH, GROUP * local, HD), F32),
            pltpu.VMEM((rows, kv_heads, cached, width), BF16),
            pltpu.SemaphoreType.DMA((rows, 2)),
        ],
        compiler_params=pltpu.CompilerParams(vmem_limit_bytes=48 * MIB),
        cost_estimate=pl.CostEstimate(
            flops=4 * local * HEADS * HD * cached,
            bytes_accessed=2 * rows * kv_heads * cached * width,
            transcendentals=local * HEADS * cached,
        ),
        name="attend",
    )(lengths, order, qkv, cosine, sine, cache)


def out_kernel(owners, *refs):
    blocks = refs[:7]
    w_ref, out_ref, lhs, total, held, sems = refs[7:]
    local = blocks[0].shape[0]
    rows = local // STEPS
    tiles, depth, columns = held.shape
    copies = [
        pltpu.make_async_copy(w_ref.at[pl.ds(k * depth, depth), :], held.at[k], sems.at[k])
        for k in range(tiles)
    ]
    for copy in copies:
        copy.start()
    for j, ref in enumerate(blocks):

        @pl.when(owners[j] >= 0)
        def _():
            lhs[pl.ds(pl.multiple_of(owners[j] * local, local), local), :] = ref[...]

    width = min(512, columns)
    for k, copy in enumerate(copies):
        copy.wait()
        for j in range(columns // width):
            span = slice(j * width, (j + 1) * width)
            product = jnp.dot(
                lhs[:, k * depth : (k + 1) * depth], held[k, :, span], preferred_element_type=F32
            )
            if k > 0:
                product = total[:, span] + product
            if k < tiles - 1:
                total[:, span] = product
                continue
            block = product.reshape(4, rows // RUN, STEPS, RUN, width)
            for s in range(STEPS):
                piece = block[:, :, s].reshape(4, rows, width)
                out_ref[s, :, :, span] = piece.astype(BF16)


def project(owners, blocks, weight):
    local, depth = blocks[0].shape
    columns = weight.shape[1]
    tile = min(512, depth)
    rows = local // STEPS
    return pl.pallas_call(
        out_kernel,
        out_shape=jax.ShapeDtypeStruct((STEPS, 4, rows, columns), BF16),
        in_specs=[SMEM] + [VMEM] * 7 + [HBM],
        out_specs=VMEM,
        scratch_shapes=[
            pltpu.VMEM((4 * local, depth), BF16),
            pltpu.VMEM((4 * local, columns), F32),
            pltpu.VMEM((depth // tile, tile, columns), BF16),
            pltpu.SemaphoreType.DMA((depth // tile,)),
        ],
        compiler_params=pltpu.CompilerParams(vmem_limit_bytes=52 * MIB),
        cost_estimate=pl.CostEstimate(
            flops=8 * local * depth * columns,
            bytes_accessed=2 * depth * columns + 8 * local * (depth + columns),
            transcendentals=0,
        ),
        name="project",
    )(owners, *blocks, weight)


def lookup(identity, table):
    hits = identity[:, None] == jnp.arange(table.shape[0], dtype=jnp.int32)[None, :]
    return jnp.sum(jnp.where(hits, table[None, :], 0), axis=1)


def ascending(lengths):
    count = lengths.shape[0]
    rows = jnp.arange(count, dtype=jnp.int32)
    keyed = lengths * count + rows
    rank = jnp.sum((keyed[None, :] < keyed[:, None]).astype(jnp.int32), axis=1)
    return jnp.sum(jnp.where(rank[:, None] == rows[None, :], rows[:, None], 0), axis=0)


def angle_tables(lengths, unit):
    steps = jnp.arange(STEPS, dtype=jnp.int32)
    position = lengths.reshape(-1, 1, unit) + steps[None, :, None]
    freq = rope_base ** (-(jnp.arange(HD // 2, dtype=F32) * 2.0 / HD))
    angles = position.reshape(-1).astype(F32)[:, None] * freq
    cosine = jnp.cos(angles)
    sine = jnp.sin(angles)
    return jnp.concatenate([cosine, cosine], 1), jnp.concatenate([-sine, sine], 1)


def on_device(
    hidden,
    input_norm_scale,
    query_key_value_weight,
    output_weight,
    adapter_down_weight,
    adapter_up_weight,
    row_adapter_index,
    adapter_store_slot,
    lengths,
    key_value_cache,
):
    tensor_count = lax.axis_size("tensor")
    tensor_pos = lax.axis_index("tensor")
    store_pos = lax.axis_index("store")
    _, rows, span = hidden.shape
    model_width = input_norm_scale.shape[0]
    rows_here = lengths.shape[0]
    unit = min(RUN, rows_here)
    halves = HALVES if rows_here % (HALVES * RUN) == 0 else 1
    part_rows = rows_here // halves
    local = STEPS * part_rows
    held_slots = adapter_down_weight.shape[0]
    rank = adapter_down_weight.shape[2]

    raw = hidden.reshape(STEPS, tensor_count, halves, part_rows // unit, unit, span)
    raw = raw.transpose(2, 1, 3, 0, 4, 5).reshape(STEPS * rows, span)
    values = raw.astype(F32)
    squares = jnp.sum(values * values, axis=1)
    squares = summed_over(squares, "tensor")
    own_runs = row_adapter_index[::RUN]
    if halves > 1:
        own_runs = own_runs.reshape(tensor_count, halves, -1).swapaxes(0, 1).reshape(-1)
    told = jnp.concatenate([squares, own_runs.astype(F32)]).reshape(1, -1)
    told = jnp.concatenate([told, swap(told, "store", 2)], axis=0)
    told = jnp.concatenate([told, swap(told, "store", 1)], axis=0)
    told = jnp.stack([told[d] for d in (0, 2, 1, 3)])
    told = jnp.stack([jnp.stack([told[p ^ q] for q in range(4)]) for p in range(4)])
    told = lax.dynamic_index_in_dim(told, store_pos, 0, keepdims=False)
    runs = told[:, STEPS * rows :].astype(jnp.int32)
    told = told[:, : STEPS * rows]
    scales = lax.rsqrt(told / model_width + eps_norm)
    slots = lookup(runs.reshape(-1), adapter_store_slot).reshape(runs.shape)
    slots = jnp.where(slots // held_slots == store_pos, slots % held_slots, -1)
    place = store_pos.reshape(1).astype(jnp.int32)
    gains = input_norm_scale.reshape(1, -1)
    gain = lax.dynamic_slice_in_dim(gains, tensor_pos * span, span, 1)
    scales = scales[:, :, None]
    own_scale = lax.dynamic_index_in_dim(scales, store_pos, 0, keepdims=False)

    line = tensor_count == 4 and part_rows % RUN == 0
    own_index = tensor_pos.reshape(1).astype(jnp.int32)
    everything = lax.all_gather(raw, "tensor", axis=0, tiled=False)

    across = swap(raw, "store", 2)
    beside = swap(raw, "store", 1)
    diagonal = swap(across, "store", 1)
    mine = slots.reshape(-1)
    down = jnp.swapaxes(adapter_down_weight, 1, 2)
    kept, passed = shrink_rows(place, mine, (raw, beside, across, diagonal), scales, gain, down)
    kept = kept + swap(passed, "store", 1)
    shrunk = kept[0] + swap(kept[1], "store", 2)
    shrunk = summed_over(shrunk, "tensor").astype(BF16)
    shrunk = jnp.stack([shrunk, swap(shrunk, "store", 2)])
    kept, passed = grow_rows(place, mine, shrunk, swap(shrunk, "store", 1), adapter_up_weight)
    raw, passed = lax.optimization_barrier((raw, passed))
    own = base_block((raw,), own_scale, gains, query_key_value_weight, own_index, None)
    passed = swap(passed, "store", 1)

    count = tensor_count * local
    parts = []
    for h in range(halves):
        part = slice(h * count, (h + 1) * count)
        delta = swap(kept[1, part] + passed[1, part], "store", 2)
        delta = (kept[0, part] + passed[0, part]) + delta
        if parts:
            everything, parts[-1] = lax.optimization_barrier((everything, parts[-1]))
        total = base_rows(
            own_index, everything, own_scale[part], gains, own, query_key_value_weight, h * count
        )
        parts.append((total + delta).astype(BF16).reshape(tensor_count, local, -1))

    contexts = []
    exchanged = [lax.all_to_all(qkv, "tensor", 0, 0, tiled=True) for qkv in parts]
    for h, moved in enumerate(exchanged):
        if h + 1 < halves:
            moved, parts[-1] = lax.optimization_barrier((moved, parts[-1]))
        if tensor_count != 4:
            q_columns = HEADS * HD // tensor_count
            pieces = []
            for piece in (moved[..., :q_columns], moved[..., q_columns:]):
                joined = piece.transpose(1, 0, 2).reshape(local, 4, -1)
                pieces.append(joined.transpose(1, 0, 2))
            moved = jnp.concatenate(pieces, axis=2)
        here = lengths[h * part_rows : (h + 1) * part_rows]
        cosine, sine = angle_tables(here, unit)
        contexts.append(
            attend(here, ascending(here), moved, cosine, sine, key_value_cache, h * part_rows, unit)
        )

    results = []
    if line:
        owners = [own_index] + [hop_owners(tensor_pos, hop) for hop in (1, 2, 3)]
        owners = jnp.concatenate(owners)
        hops = [line_gather(context, "tensor") for context in contexts]
        for h in range(halves):
            if h + 1 < halves:
                hops[h], hops[h + 1][1] = lax.optimization_barrier((hops[h], hops[h + 1][1]))
            blocks = (contexts[h],) + hops[h][0] + hops[h][1] + hops[h][2]
            results.append(project(owners, blocks, output_weight))
    else:
        for context in contexts:
            context = lax.all_gather(context, "tensor", axis=0, tiled=True)
            result = jnp.dot(context, output_weight, preferred_element_type=F32).astype(BF16)
            result = result.reshape(tensor_count, part_rows // unit, STEPS, unit, -1)
            result = result.transpose(2, 0, 1, 3, 4).reshape(STEPS, tensor_count, part_rows, -1)
            results.append(result)
    output = results[0] if halves == 1 else jnp.concatenate(results, axis=2)
    return output.reshape(STEPS, rows, -1)


def solution(mesh):
    in_specs = (
        P(None, ("groups", "store"), "tensor"),
        P(),
        P(None, "tensor"),
        P(None, "tensor"),
        P(("groups", "store"), "tensor", None),
        P(("groups", "store"), None, "tensor"),
        P(("groups", "store")),
        P("groups"),
        P(("groups", "store", "tensor")),
        P(("groups", "store", "tensor"), None, None, None),
    )
    out_specs = P(None, ("groups", "store"), "tensor")
    return jax.shard_map(
        on_device, mesh=mesh, in_specs=in_specs, out_specs=out_specs, check_vma=False
    )
```

```python
import functools

import jax
import jax.numpy as jnp
from jax import lax
from jax.experimental import pallas as pl
from jax.experimental.pallas import tpu as pltpu
from jax.sharding import PartitionSpec as P

HEADS = 32
KVH = 4
HD = 128
GROUP = HEADS // KVH
RUN = 8
STEPS = 2
LANES = 128
HALVES = 2

eps_norm = 1e-05
rope_base = 500000.0
masked = -1e30

MIB = 1 << 20
F32 = jnp.float32
BF16 = jnp.bfloat16
F16 = jnp.float16
VMEM = pl.BlockSpec(memory_space=pltpu.VMEM)
SMEM = pl.BlockSpec(memory_space=pltpu.SMEM)
HBM = pl.BlockSpec(memory_space=pltpu.HBM)


def swap(values, axis, distance):
    count = lax.axis_size(axis)
    return lax.ppermute(values, axis, [(i, i ^ distance) for i in range(count)])


def summed_over(values, axis):
    distance = 1
    while distance < lax.axis_size(axis):
        values = values + swap(values, axis, distance)
        distance *= 2
    return values


def line_gather(block, axis):
    up = down = block
    hops = []
    for hop in range(1, 4):
        up = lax.ppermute(up, axis, [(i, i + 1) for i in range(hop - 1, 3)])
        down = lax.ppermute(down, axis, [(i, i - 1) for i in range(4 - hop, 0, -1)])
        hops.append((up, down))
    return hops


def hop_owners(position, hop):
    below = position - hop
    above = position + hop
    return jnp.stack([jnp.where(below >= 0, below, -1), jnp.where(above < 4, above, -1)])


def block_kernel(count, has_total, owners, *refs):
    x_refs = refs[:count]
    scale_ref, gain_ref, w_ref = refs[count : count + 3]
    out_ref, held, sems = refs[-3:]
    _, tiles, depth, _ = held.shape

    def copy(j, k):
        first = pl.multiple_of((owners[j] * tiles + k) * depth, depth)
        return pltpu.make_async_copy(
            w_ref.at[pl.ds(first, depth), :], held.at[j, k], sems.at[j, k]
        )

    for j in range(count):

        @pl.when(owners[j] >= 0)
        def _():
            for k in range(tiles):
                copy(j, k).start()

    out_ref[...] = refs[count + 3][...] if has_total else jnp.zeros_like(out_ref)
    for j, x_ref in enumerate(x_refs):

        @pl.when(owners[j] >= 0)
        def _():
            scale = scale_ref[...]
            for k in range(tiles):
                span = slice(k * depth, (k + 1) * depth)
                first = pl.multiple_of((owners[j] * tiles + k) * depth, depth)
                gain = gain_ref[:, pl.ds(first, depth)]
                normed = (x_ref[:, span].astype(F32) * scale * gain).astype(BF16)
                copy(j, k).wait()
                out_ref[...] += jnp.dot(normed, held[j, k], preferred_element_type=F32)


def base_block(blocks, scale, gain, weight, owners, total):
    rows, depth = blocks[0].shape
    columns = weight.shape[1]
    tile = min(512, depth)
    count = len(blocks)
    operands = [owners, *blocks, scale, gain, weight]
    if total is not None:
        operands.append(total)
    return pl.pallas_call(
        functools.partial(block_kernel, count, total is not None),
        out_shape=jax.ShapeDtypeStruct((rows, columns), F32),
        in_specs=[SMEM] + [VMEM] * (count + 2) + [HBM] + [VMEM] * (total is not None),
        out_specs=VMEM,
        scratch_shapes=[
            pltpu.VMEM((count, depth // tile, tile, columns), BF16),
            pltpu.SemaphoreType.DMA((count, depth // tile)),
        ],
        compiler_params=pltpu.CompilerParams(vmem_limit_bytes=48 * MIB),
        cost_estimate=pl.CostEstimate(
            flops=2 * count * rows * depth * columns,
            bytes_accessed=2 * depth * (rows + columns) + 8 * rows * columns,
            transcendentals=0,
        ),
        name="base_block",
    )(*operands)


def base_kernel(first_row, place_ref, x_ref, scale_ref, gain_ref, own_ref, w_ref, out_ref, held, sems):
    owners, _, span = x_ref.shape
    rows = scale_ref.shape[0]
    tiles, depth, _ = held.shape
    tiles_each = span // depth

    def spot(k):
        owner = lax.rem(place_ref[0] + 1 + k // tiles_each, owners)
        return owner, pl.multiple_of((owner * tiles_each + k % tiles_each) * depth, depth)

    copies = [
        pltpu.make_async_copy(w_ref.at[pl.ds(spot(k)[1], depth), :], held.at[k], sems.at[k])
        for k in range(tiles)
    ]
    for copy in copies:
        copy.start()
    scale = scale_ref[...]
    out_ref[...] = own_ref[first_row : first_row + rows, :]
    for k, copy in enumerate(copies):
        owner, first = spot(k)
        inner = (k % tiles_each) * depth
        gain = gain_ref[:, pl.ds(first, depth)]
        part = x_ref[owner, first_row : first_row + rows, inner : inner + depth].astype(F32)
        normed = (part * scale * gain).astype(BF16)
        copy.wait()
        out_ref[...] += jnp.dot(normed, held[k], preferred_element_type=F32)


def base_rows(place, x, scale, gain, own, weight, first_row):
    owners, _, span = x.shape
    rows = scale.shape[0]
    columns = weight.shape[1]
    tile = min(512, span)
    tiles = (owners - 1) * span // tile
    return pl.pallas_call(
        functools.partial(base_kernel, first_row),
        out_shape=jax.ShapeDtypeStruct((rows, columns), F32),
        in_specs=[SMEM] + [VMEM] * 4 + [HBM],
        out_specs=VMEM,
        scratch_shapes=[
            pltpu.VMEM((tiles, tile, columns), BF16),
            pltpu.SemaphoreType.DMA((tiles,)),
        ],
        compiler_params=pltpu.CompilerParams(vmem_limit_bytes=48 * MIB),
        cost_estimate=pl.CostEstimate(
            flops=2 * rows * tiles * tile * columns,
            bytes_accessed=2 * tiles * tile * (rows + columns) + 8 * rows * columns,
            transcendentals=0,
        ),
        name="base_rows",
    )(place, x, scale, gain, own, weight)


TEAM = 4
SLABS = (0, 2, 1, 3)


def list_runs(place_ref, slots, runs, jobs, start):
    def look(run, carry, slab, d):
        slot = slots[(place_ref[0] ^ d) * runs + run]

        @pl.when(slot >= 0)
        def _():
            jobs[carry] = slab * runs + run
            start(carry, d, run, slot)

        return carry + (slot >= 0).astype(jnp.int32)

    count = jnp.int32(0)
    for slab, d in enumerate(SLABS):
        count = lax.fori_loop(0, runs, functools.partial(look, slab=slab, d=d), count)
    return count


def work_in_teams(count, wait, work):
    def team(g, carry):
        for u in range(TEAM):

            @pl.when(g * TEAM + u < count)
            def _():
                wait(g * TEAM + u)

        work([jnp.minimum(g * TEAM + u, count - 1) for u in range(TEAM)])
        return carry

    lax.fori_loop(0, (count + TEAM - 1) // TEAM, team, 0)


def shrink_kernel(
    place_ref,
    slots,
    x0,
    x1,
    x2,
    x3,
    scale_ref,
    gain_ref,
    down_ref,
    keep_ref,
    send_ref,
    jobs,
    parts,
    held_x,
    held,
    x_sems,
    sems,
):
    runs = held.shape[0] // 4
    rank = held.shape[1]
    x_refs = (x0, x1, x2, x3)

    def x_copy(i, d, run):
        rows = pl.ds(pl.multiple_of(run * 16, 16), 16)
        return pltpu.make_async_copy(x_refs[d].at[rows, :], held_x.at[i], x_sems.at[i])

    def copy(i, slot):
        return pltpu.make_async_copy(down_ref.at[slot], held.at[i], sems.at[i])

    def start(i, d, run, slot):
        copy(i, slot).start()
        x_copy(i, d, run).start()

    def wait(i):
        copy(i, 0).wait()
        x_copy(i, 0, 0).wait()

    def work(members):
        results = []
        for i in members:
            job = jobs[i]
            slab = job // runs
            d = jnp.where(slab == 1, 2, jnp.where(slab == 2, 1, slab))
            rows = pl.ds(pl.multiple_of((job % runs) * 16, 16), 16)
            scale = scale_ref[place_ref[0] ^ d, rows, :]
            normed = (held_x[i].astype(F32) * scale * gain_ref[...]).astype(BF16)
            part = lax.dot_general(
                normed, held[i], (((1,), (1,)), ((), ())), preferred_element_type=F32
            )
            results.append((job, part))
        for job, part in results:
            parts[job] = part

    count = list_runs(place_ref, slots, runs, jobs, start)
    parts[...] = jnp.zeros_like(parts)
    work_in_teams(count, wait, work)
    for slab in range(4):
        for i in range(runs // 2):
            low = slab * runs + i
            out_ref = (keep_ref, send_ref)[slab // 2]
            out_ref[slab % 2, i * 16 : (i + 1) * 16, :] = jnp.concatenate(
                [parts[low], parts[low + runs // 2]], axis=1
            )


def shrink_rows(place, slots, blocks, scales, gain, down):
    rows, depth = blocks[0].shape
    rank = down.shape[1]
    runs = rows // 16
    return pl.pallas_call(
        shrink_kernel,
        out_shape=[jax.ShapeDtypeStruct((2, rows // 2, 2 * rank), F32)] * 2,
        in_specs=[SMEM] * 2 + [HBM] * 4 + [VMEM] * 2 + [HBM],
        out_specs=[VMEM] * 2,
        scratch_shapes=[
            pltpu.SMEM((4 * runs,), jnp.int32),
            pltpu.VMEM((4 * runs, 16, rank), F32),
            pltpu.VMEM((4 * runs, 16, depth), BF16),
            pltpu.VMEM((4 * runs, rank, depth), BF16),
            pltpu.SemaphoreType.DMA((4 * runs,)),
            pltpu.SemaphoreType.DMA((4 * runs,)),
        ],
        compiler_params=pltpu.CompilerParams(vmem_limit_bytes=54 * MIB),
        cost_estimate=pl.CostEstimate(
            flops=2 * rows * depth * rank,
            bytes_accessed=8 * rows * depth + down.size,
            transcendentals=0,
        ),
        name="shrink_rows",
    )(place, slots, *blocks, scales, gain, down)


def grow_kernel(
    place_ref, slots, s0, s1, up_ref, keep_ref, send_ref, jobs, parts, held, sems
):
    runs = held.shape[0] // 4
    rank = held.shape[1]

    def copy(i, slot):
        return pltpu.make_async_copy(up_ref.at[slot], held.at[i], sems.at[i])

    def start(i, d, run, slot):
        copy(i, slot).start()

    def wait(i):
        copy(i, 0).wait()

    def work(members):
        results = []
        for i in members:
            job = jobs[i]
            grown = jnp.dot(parts[job], held[i], preferred_element_type=F32)
            results.append((job, grown))
        for job, grown in results:
            rows = pl.ds(pl.multiple_of((job % runs) * 16, 16), 16)
            slab = job // runs

            @pl.when(slab < 2)
            def _():
                keep_ref[slab, rows, :] = grown

            @pl.when(slab >= 2)
            def _():
                send_ref[slab - 2, rows, :] = grown

    count = list_runs(place_ref, slots, runs, jobs, start)
    for slab in range(4):
        for i in range(runs // 2):
            low = slab * runs + i
            both = (s0, s1)[slab // 2][slab % 2, i * 16 : (i + 1) * 16, :]
            parts[low] = both[:, :rank]
            parts[low + runs // 2] = both[:, rank:]
    keep_ref[...] = jnp.zeros_like(keep_ref)
    send_ref[...] = jnp.zeros_like(send_ref)
    work_in_teams(count, wait, work)


def grow_rows(place, slots, kept, passed, up):
    _, pair_rows, _ = kept.shape
    rows = 2 * pair_rows
    rank, columns = up.shape[1:]
    runs = rows // 16
    return pl.pallas_call(
        grow_kernel,
        out_shape=[jax.ShapeDtypeStruct((2, rows, columns), F32)] * 2,
        in_specs=[SMEM, SMEM, VMEM, VMEM, HBM],
        out_specs=[VMEM] * 2,
        scratch_shapes=[
            pltpu.SMEM((4 * runs,), jnp.int32),
            pltpu.VMEM((4 * runs, 16, rank), BF16),
            pltpu.VMEM((4 * runs, rank, columns), BF16),
            pltpu.SemaphoreType.DMA((4 * runs,)),
        ],
        compiler_params=pltpu.CompilerParams(vmem_limit_bytes=60 * MIB),
        cost_estimate=pl.CostEstimate(
            flops=2 * rows * rank * columns,
            bytes_accessed=8 * rows * columns + up.size,
            transcendentals=0,
        ),
        name="grow_rows",
    )(place, slots, kept, passed, up)


def attend_kernel(
    unit,
    first_row,
    lengths,
    order,
    qkv_ref,
    cos_ref,
    sin_ref,
    cache_ref,
    out_ref,
    queries,
    keys,
    values,
    context,
    held,
    sems,
):
    rows, _, cached, _ = held.shape
    local = STEPS * rows
    q_columns = GROUP * HD
    part = cached // 2
    scale = HD ** (-0.5)
    team = min(4, rows)

    def copy(r, b):
        span = pl.ds(b * part, part)
        return pltpu.make_async_copy(
            cache_ref.at[first_row + r, :, span, :], held.at[r, :, span, :], sems.at[r, b]
        )

    def longest(group):
        return lengths[order[group * team + team - 1]]

    def fetch(i, carry):
        r = order[i]
        copy(r, 0).start()

        @pl.when(longest(i // team) > part)
        def _():
            copy(r, 1).start()

        return carry

    lax.fori_loop(0, rows, fetch, 0)

    cosine = cos_ref[...]
    sine = sin_ref[...]

    def rotated(x):
        x = x.astype(F32)
        turned = x * cosine + pltpu.roll(x, HD // 2, 1) * sine
        return turned.astype(BF16).astype(F32)

    for k in range(KVH):
        for g in range(GROUP):
            queries[k, g * local : (g + 1) * local, :] = rotated(
                qkv_ref[k, :, g * HD : (g + 1) * HD]
            )
        place = q_columns + (k % 2) * HD
        keys[k] = rotated(qkv_ref[k // 2, :, place : place + HD])
        values[k] = qkv_ref[2 + k // 2, :, place : place + HD].astype(F32)

    early = lax.broadcasted_iota(jnp.int32, (4 * GROUP, 1), 0) % (2 * GROUP) < GROUP

    def scores(r, at, pair, span, live):
        heads = (2 * pair, 2 * pair + 1)
        query = [
            jnp.concatenate(
                [queries[k, pl.ds(at[s], GROUP, stride=local), :] for s in range(STEPS)], axis=0
            )
            for k in heads
        ]
        blank = jnp.zeros((2 * GROUP, HD), F32)
        spread = jnp.concatenate(
            [
                jnp.concatenate([query[0], blank], axis=1),
                jnp.concatenate([blank, query[1]], axis=1),
            ],
            axis=0,
        ).astype(BF16)
        old_keys = jnp.concatenate([held[r, k, :span, :HD] for k in heads], axis=1)
        old = lax.dot_general(
            spread, old_keys, (((1,), (1,)), ((), ())), preferred_element_type=F32
        )
        old = jnp.where(live, old * scale, masked)
        fresh = []
        for t in range(STEPS):
            both = jnp.concatenate(
                [
                    jnp.sum(query[i] * keys[k, pl.ds(at[t], 1), :], axis=1, keepdims=True)
                    for i, k in enumerate(heads)
                ],
                axis=0,
            )
            fresh.append(both * scale)
        fresh[1] = jnp.where(early, masked, fresh[1])
        return old, fresh

    def soften(old, fresh):
        peak = jnp.maximum(jnp.max(old, axis=1, keepdims=True), jnp.maximum(fresh[0], fresh[1]))
        p_old = jnp.exp(old - peak)
        p_new = [jnp.exp(f - peak) for f in fresh]
        total = jnp.sum(p_old, axis=1, keepdims=True) + (p_new[0] + p_new[1])
        return p_old.astype(BF16), [p.astype(BF16).astype(F32) for p in p_new], total

    def mix(r, at, pair, span, w_old, w_new, total):
        heads = (2 * pair, 2 * pair + 1)
        old_values = jnp.concatenate([held[r, k, :span, HD:] for k in heads], axis=1)
        mixed = jnp.dot(w_old, old_values, preferred_element_type=F32)
        for i, k in enumerate(heads):
            own = slice(i * 2 * GROUP, (i + 1) * 2 * GROUP)
            result = mixed[own, i * HD : (i + 1) * HD]
            for t in range(STEPS):
                result = result + w_new[t][own] * values[k, pl.ds(at[t], 1), :]
            result = result / total[own]
            for s in range(STEPS):
                context[k, pl.ds(at[s], GROUP, stride=local), :] = result[
                    s * GROUP : (s + 1) * GROUP
                ]

    def attend_team(members, span):
        jobs = []
        for r in members:
            at = [(r // unit) * (STEPS * unit) + s * unit + r % unit for s in range(STEPS)]
            live = lax.broadcasted_iota(jnp.int32, (4 * GROUP, span), 1) < lengths[r]
            for pair in range(KVH // 2):
                jobs.append((r, at, pair, scores(r, at, pair, span, live)))
        softened = [soften(*job[3]) for job in jobs]
        for (r, at, pair, _), weights in zip(jobs, softened):
            mix(r, at, pair, span, *weights)

    def each(group, carry):
        members = [order[group * team + i] for i in range(team)]
        wide = longest(group) > part
        for r in members:
            copy(r, 0).wait()

        @pl.when(wide)
        def _():
            for r in members:
                copy(r, 1).wait()
            attend_team(members, cached)

        @pl.when(jnp.logical_not(wide))
        def _():
            attend_team(members, part)

        return carry

    lax.fori_loop(0, rows // team, each, 0)
    for k in range(KVH):
        for g in range(GROUP):
            place = (k * GROUP + g) * HD
            out_ref[:, place : place + HD] = context[k, g * local : (g + 1) * local, :].astype(BF16)


def attend(lengths, order, qkv, cosine, sine, cache, first_row, unit):
    rows = lengths.shape[0]
    local = STEPS * rows
    _, kv_heads, cached, width = cache.shape
    return pl.pallas_call(
        functools.partial(attend_kernel, unit, first_row),
        out_shape=jax.ShapeDtypeStruct((local, HEADS * HD), BF16),
        in_specs=[SMEM, SMEM, VMEM, VMEM, VMEM, HBM],
        out_specs=VMEM,
        scratch_shapes=[
            pltpu.VMEM((KVH, GROUP * local, HD), F32),
            pltpu.VMEM((KVH, local, HD), F32),
            pltpu.VMEM((KVH, local, HD), F32),
            pltpu.VMEM((KVH, GROUP * local, HD), F32),
            pltpu.VMEM((rows, kv_heads, cached, width), BF16),
            pltpu.SemaphoreType.DMA((rows, 2)),
        ],
        compiler_params=pltpu.CompilerParams(vmem_limit_bytes=48 * MIB),
        cost_estimate=pl.CostEstimate(
            flops=4 * local * HEADS * HD * cached,
            bytes_accessed=2 * rows * kv_heads * cached * width,
            transcendentals=local * HEADS * cached,
        ),
        name="attend",
    )(lengths, order, qkv, cosine, sine, cache)


def out_kernel(count, has_earlier, owners, *refs):
    blocks = refs[:count]
    w_ref = refs[count]
    out_ref, lhs, total, held, sems = refs[-5:]
    local = blocks[0].shape[0]
    rows = local // STEPS
    tiles, depth, columns = held.shape
    halves = out_ref.shape[2]
    copies = [
        pltpu.make_async_copy(w_ref.at[pl.ds(k * depth, depth), :], held.at[k], sems.at[k])
        for k in range(tiles)
    ]
    for copy in copies:
        copy.start()
    slots = count // halves

    def place(j):
        used = jnp.int32(0)
        for i in range(j % slots):
            used = used + (owners[i] >= 0).astype(jnp.int32)
        return (j // slots) * (lhs.shape[0] // halves) + used * local

    lhs[...] = jnp.zeros_like(lhs)
    for j, ref in enumerate(blocks):

        @pl.when(owners[j % slots] >= 0)
        def _():
            lhs[pl.ds(pl.multiple_of(place(j), local), local), :] = ref[...]

    if has_earlier:
        out_ref[...] = refs[count + 1][...]
    width = min(512, columns)
    for k, copy in enumerate(copies):
        copy.wait()
        for j in range(columns // width):
            span = slice(j * width, (j + 1) * width)
            product = jnp.dot(
                lhs[:, k * depth : (k + 1) * depth], held[k, :, span], preferred_element_type=F32
            )
            if k > 0:
                product = total[:, span] + product
            total[:, span] = product
    for j in range(count):

        @pl.when(owners[j % slots] >= 0)
        def _():
            block = total[pl.ds(pl.multiple_of(place(j), local), local), :]
            block = block.reshape(rows // RUN, STEPS, RUN, columns)
            for s in range(STEPS):
                piece = block[:, s].reshape(rows, columns).astype(BF16)
                out_ref[s, owners[j % slots], j // slots] = piece


def project(owners, blocks, weight, present, earlier=None):
    halves = len(blocks)
    flat = [block for part in blocks for block in part]
    local, depth = flat[0].shape
    columns = weight.shape[1]
    tile = min(512, depth)
    rows = local // STEPS
    count = len(flat)
    more = [] if earlier is None else [earlier]
    return pl.pallas_call(
        functools.partial(out_kernel, count, earlier is not None),
        out_shape=jax.ShapeDtypeStruct((STEPS, 4, halves, rows, columns), BF16),
        in_specs=[SMEM] + [VMEM] * count + [HBM] + [VMEM] * len(more),
        out_specs=VMEM,
        scratch_shapes=[
            pltpu.VMEM((present * halves * local, depth), BF16),
            pltpu.VMEM((present * halves * local, columns), F32),
            pltpu.VMEM((depth // tile, tile, columns), BF16),
            pltpu.SemaphoreType.DMA((depth // tile,)),
        ],
        compiler_params=pltpu.CompilerParams(vmem_limit_bytes=52 * MIB),
        cost_estimate=pl.CostEstimate(
            flops=2 * present * halves * local * depth * columns,
            bytes_accessed=2 * depth * columns + 4 * present * local * (depth + columns),
            transcendentals=0,
        ),
        name="project",
    )(owners, *flat, weight, *more)


def lookup(identity, table):
    hits = identity[:, None] == jnp.arange(table.shape[0], dtype=jnp.int32)[None, :]
    return jnp.sum(jnp.where(hits, table[None, :], 0), axis=1)


def ascending(lengths):
    count = lengths.shape[0]
    rows = jnp.arange(count, dtype=jnp.int32)
    keyed = lengths * count + rows
    rank = jnp.sum((keyed[None, :] < keyed[:, None]).astype(jnp.int32), axis=1)
    return jnp.sum(jnp.where(rank[:, None] == rows[None, :], rows[:, None], 0), axis=0)


def angle_tables(lengths, unit):
    steps = jnp.arange(STEPS, dtype=jnp.int32)
    position = lengths.reshape(-1, 1, unit) + steps[None, :, None]
    freq = rope_base ** (-(jnp.arange(HD // 2, dtype=F32) * 2.0 / HD))
    angles = position.reshape(-1).astype(F32)[:, None] * freq
    cosine = jnp.cos(angles)
    sine = jnp.sin(angles)
    return jnp.concatenate([cosine, cosine], 1), jnp.concatenate([-sine, sine], 1)


def on_device(
    hidden,
    input_norm_scale,
    query_key_value_weight,
    output_weight,
    adapter_down_weight,
    adapter_up_weight,
    row_adapter_index,
    adapter_store_slot,
    lengths,
    key_value_cache,
):
    tensor_count = lax.axis_size("tensor")
    tensor_pos = lax.axis_index("tensor")
    store_pos = lax.axis_index("store")
    _, rows, span = hidden.shape
    model_width = input_norm_scale.shape[0]
    rows_here = lengths.shape[0]
    unit = min(RUN, rows_here)
    line = tensor_count == 4 and rows_here % (HALVES * RUN) == 0
    halves = HALVES if line else 1
    part_rows = rows_here // halves
    local = STEPS * part_rows
    held_slots = adapter_down_weight.shape[0]
    rank = adapter_down_weight.shape[2]

    raw = hidden.reshape(STEPS, tensor_count, halves, part_rows // unit, unit, span)
    raw = raw.transpose(2, 1, 3, 0, 4, 5).reshape(STEPS * rows, span)
    own_index = tensor_pos.reshape(1).astype(jnp.int32)
    owners = [own_index] + [hop_owners(tensor_pos, hop) for hop in (1, 2, 3)]
    count = tensor_count * local
    parts = [slice(h * count, (h + 1) * count) for h in range(halves)]
    everything = [None] * halves
    hops = None
    everything[0] = lax.all_gather(raw[parts[0]], "tensor", axis=0, tiled=False)
    if halves > 1:
        hops = line_gather(raw[parts[1]], "tensor")

    values = raw.astype(F32)
    squares = jnp.sum(values * values, axis=1)
    squares = summed_over(squares, "tensor")
    own_runs = row_adapter_index[::RUN]
    if halves > 1:
        own_runs = own_runs.reshape(tensor_count, halves, -1).swapaxes(0, 1).reshape(-1)
    told = jnp.concatenate([squares, own_runs.astype(F32)]).reshape(1, -1)
    told = jnp.concatenate([told, swap(told, "store", 2)], axis=0)
    if halves > 1:
        told, hops[0] = lax.optimization_barrier((told, hops[0]))
    told = jnp.concatenate([told, swap(told, "store", 1)], axis=0)
    told = jnp.stack([told[d] for d in (0, 2, 1, 3)])
    told = jnp.stack([jnp.stack([told[p ^ q] for q in range(4)]) for p in range(4)])
    told = lax.dynamic_index_in_dim(told, store_pos, 0, keepdims=False)
    runs = told[:, STEPS * rows :].astype(jnp.int32)
    told = told[:, : STEPS * rows]
    scales = lax.rsqrt(told / model_width + eps_norm)
    slots = lookup(runs.reshape(-1), adapter_store_slot).reshape(runs.shape)
    slots = jnp.where(slots // held_slots == store_pos, slots % held_slots, -1)
    place = store_pos.reshape(1).astype(jnp.int32)
    gains = input_norm_scale.reshape(1, -1)
    gain = lax.dynamic_slice_in_dim(gains, tensor_pos * span, span, 1)
    scales = scales[:, :, None]
    own_scale = lax.dynamic_index_in_dim(scales, store_pos, 0, keepdims=False)

    across = swap(raw, "store", 2)
    beside = swap(raw, "store", 1)
    diagonal = swap(across, "store", 1)
    mine = slots.reshape(-1)
    down = jnp.swapaxes(adapter_down_weight, 1, 2)
    kept, passed = shrink_rows(place, mine, (raw, beside, across, diagonal), scales, gain, down)
    kept = kept + swap(passed, "store", 1)
    shrunk = kept[0] + swap(kept[1], "store", 2)
    if halves > 1:
        shrunk, hops[1] = lax.optimization_barrier((shrunk, hops[1]))
    shrunk = summed_over(shrunk, "tensor").astype(BF16)
    shrunk = jnp.stack([shrunk, swap(shrunk, "store", 2)])
    kept, passed = grow_rows(place, mine, shrunk, swap(shrunk, "store", 1), adapter_up_weight)
    passed = swap(passed.astype(F16), "store", 1).astype(F32)
    deltas = []
    for part in parts:
        delta = swap((kept[1, part] + passed[1, part]).astype(F16), "store", 2).astype(F32)
        deltas.append((kept[0, part] + passed[0, part]) + delta)

    weight = query_key_value_weight
    raw, passed = lax.optimization_barrier((raw, passed))
    own = base_block((raw[parts[0]],), own_scale[parts[0]], gains, weight, own_index, None)
    total = base_rows(own_index, everything[0], own_scale[parts[0]], gains, own, weight, 0)
    mixed = [(total + deltas[0]).astype(BF16)]
    if halves > 1:
        blocks = (raw[parts[1]],) + hops[0] + hops[1]
        near = jnp.concatenate(owners[:3])
        total = base_block(blocks, own_scale[parts[1]], gains, weight, near, None)
        hops[2], mixed[0] = lax.optimization_barrier((hops[2], mixed[0]))
        total = base_block(hops[2], own_scale[parts[1]], gains, weight, owners[3], total)
        mixed.append((total + deltas[1]).astype(BF16))
    mixed = [qkv.reshape(tensor_count, local, -1) for qkv in mixed]

    contexts = []
    exchanged = []
    for qkv in mixed:
        if exchanged:
            qkv, exchanged[-1] = lax.optimization_barrier((qkv, exchanged[-1]))
        exchanged.append(lax.all_to_all(qkv, "tensor", 0, 0, tiled=True))
    for h, moved in enumerate(exchanged):
        if tensor_count != 4:
            q_columns = HEADS * HD // tensor_count
            pieces = []
            for piece in (moved[..., :q_columns], moved[..., q_columns:]):
                joined = piece.transpose(1, 0, 2).reshape(local, 4, -1)
                pieces.append(joined.transpose(1, 0, 2))
            moved = jnp.concatenate(pieces, axis=2)
        here = lengths[h * part_rows : (h + 1) * part_rows]
        cosine, sine = angle_tables(here, unit)
        contexts.append(
            attend(here, ascending(here), moved, cosine, sine, key_value_cache, h * part_rows, unit)
        )

    if line:
        hops = [line_gather(context, "tensor") for context in contexts]
        first = [(context,) + hop[0] for context, hop in zip(contexts, hops)]
        last = [hop[1] + hop[2] for hop in hops]
        output = project(jnp.concatenate(owners[:2]), first, output_weight, 3)
        output = project(jnp.concatenate(owners[2:]), last, output_weight, 2, output)
    else:
        results = []
        for context in contexts:
            context = lax.all_gather(context, "tensor", axis=0, tiled=True)
            result = jnp.dot(context, output_weight, preferred_element_type=F32).astype(BF16)
            result = result.reshape(tensor_count, part_rows // unit, STEPS, unit, -1)
            result = result.transpose(2, 0, 1, 3, 4).reshape(STEPS, tensor_count, part_rows, -1)
            results.append(result)
        output = jnp.stack(results, axis=2)
    return output.reshape(STEPS, rows, -1)


def solution(mesh):
    in_specs = (
        P(None, ("groups", "store"), "tensor"),
        P(),
        P(None, "tensor"),
        P(None, "tensor"),
        P(("groups", "store"), "tensor", None),
        P(("groups", "store"), None, "tensor"),
        P(("groups", "store")),
        P("groups"),
        P(("groups", "store", "tensor")),
        P(("groups", "store", "tensor"), None, None, None),
    )
    out_specs = P(None, ("groups", "store"), "tensor")
    return jax.shard_map(
        on_device, mesh=mesh, in_specs=in_specs, out_specs=out_specs, check_vma=False
    )
```

```python
import functools

import jax
import jax.numpy as jnp
from jax import lax
from jax.experimental import pallas as pl
from jax.experimental.pallas import tpu as pltpu
from jax.sharding import PartitionSpec as P

HEADS = 32
KVH = 4
HD = 128
GROUP = HEADS // KVH
RUN = 8
STEPS = 2
LANES = 128
HALVES = 2

eps_norm = 1e-05
rope_base = 500000.0
masked = -1e30

MIB = 1 << 20
F32 = jnp.float32
BF16 = jnp.bfloat16
F16 = jnp.float16
VMEM = pl.BlockSpec(memory_space=pltpu.VMEM)
SMEM = pl.BlockSpec(memory_space=pltpu.SMEM)
HBM = pl.BlockSpec(memory_space=pltpu.HBM)


def swap(values, axis, distance):
    count = lax.axis_size(axis)
    return lax.ppermute(values, axis, [(i, i ^ distance) for i in range(count)])


def summed_over(values, axis):
    distance = 1
    while distance < lax.axis_size(axis):
        values = values + swap(values, axis, distance)
        distance *= 2
    return values


def line_gather(block, axis):
    up = down = block
    hops = []
    for hop in range(1, 4):
        up = lax.ppermute(up, axis, [(i, i + 1) for i in range(hop - 1, 3)])
        down = lax.ppermute(down, axis, [(i, i - 1) for i in range(4 - hop, 0, -1)])
        hops.append((up, down))
    return hops


def hop_owners(position, hop):
    below = position - hop
    above = position + hop
    return jnp.stack([jnp.where(below >= 0, below, -1), jnp.where(above < 4, above, -1)])


def block_kernel(count, has_total, owners, *refs):
    x_refs = refs[:count]
    scale_ref, gain_ref, w_ref = refs[count : count + 3]
    out_ref, held, sems = refs[-3:]
    _, tiles, depth, _ = held.shape

    def copy(j, k):
        first = pl.multiple_of((owners[j] * tiles + k) * depth, depth)
        return pltpu.make_async_copy(
            w_ref.at[pl.ds(first, depth), :], held.at[j, k], sems.at[j, k]
        )

    for j in range(count):

        @pl.when(owners[j] >= 0)
        def _():
            for k in range(tiles):
                copy(j, k).start()

    out_ref[...] = refs[count + 3][...] if has_total else jnp.zeros_like(out_ref)
    for j, x_ref in enumerate(x_refs):

        @pl.when(owners[j] >= 0)
        def _():
            scale = scale_ref[...]
            for k in range(tiles):
                span = slice(k * depth, (k + 1) * depth)
                first = pl.multiple_of((owners[j] * tiles + k) * depth, depth)
                gain = gain_ref[:, pl.ds(first, depth)]
                normed = (x_ref[:, span].astype(F32) * scale * gain).astype(BF16)
                copy(j, k).wait()
                out_ref[...] += jnp.dot(normed, held[j, k], preferred_element_type=F32)


def base_block(blocks, scale, gain, weight, owners, total):
    rows, depth = blocks[0].shape
    columns = weight.shape[1]
    tile = min(512, depth)
    count = len(blocks)
    operands = [owners, *blocks, scale, gain, weight]
    if total is not None:
        operands.append(total)
    return pl.pallas_call(
        functools.partial(block_kernel, count, total is not None),
        out_shape=jax.ShapeDtypeStruct((rows, columns), F32),
        in_specs=[SMEM] + [VMEM] * (count + 2) + [HBM] + [VMEM] * (total is not None),
        out_specs=VMEM,
        scratch_shapes=[
            pltpu.VMEM((count, depth // tile, tile, columns), BF16),
            pltpu.SemaphoreType.DMA((count, depth // tile)),
        ],
        compiler_params=pltpu.CompilerParams(vmem_limit_bytes=48 * MIB),
        cost_estimate=pl.CostEstimate(
            flops=2 * count * rows * depth * columns,
            bytes_accessed=2 * depth * (rows + columns) + 8 * rows * columns,
            transcendentals=0,
        ),
        name="base_block",
    )(*operands)


def base_kernel(first_row, place_ref, x_ref, scale_ref, gain_ref, own_ref, w_ref, out_ref, held, sems):
    owners, _, span = x_ref.shape
    rows = scale_ref.shape[0]
    tiles, depth, _ = held.shape
    tiles_each = span // depth

    def spot(k):
        owner = lax.rem(place_ref[0] + 1 + k // tiles_each, owners)
        return owner, pl.multiple_of((owner * tiles_each + k % tiles_each) * depth, depth)

    copies = [
        pltpu.make_async_copy(w_ref.at[pl.ds(spot(k)[1], depth), :], held.at[k], sems.at[k])
        for k in range(tiles)
    ]
    for copy in copies:
        copy.start()
    scale = scale_ref[...]
    out_ref[...] = own_ref[first_row : first_row + rows, :]
    for k, copy in enumerate(copies):
        owner, first = spot(k)
        inner = (k % tiles_each) * depth
        gain = gain_ref[:, pl.ds(first, depth)]
        part = x_ref[owner, first_row : first_row + rows, inner : inner + depth].astype(F32)
        normed = (part * scale * gain).astype(BF16)
        copy.wait()
        out_ref[...] += jnp.dot(normed, held[k], preferred_element_type=F32)


def base_rows(place, x, scale, gain, own, weight, first_row):
    owners, _, span = x.shape
    rows = scale.shape[0]
    columns = weight.shape[1]
    tile = min(512, span)
    tiles = (owners - 1) * span // tile
    return pl.pallas_call(
        functools.partial(base_kernel, first_row),
        out_shape=jax.ShapeDtypeStruct((rows, columns), F32),
        in_specs=[SMEM] + [VMEM] * 4 + [HBM],
        out_specs=VMEM,
        scratch_shapes=[
            pltpu.VMEM((tiles, tile, columns), BF16),
            pltpu.SemaphoreType.DMA((tiles,)),
        ],
        compiler_params=pltpu.CompilerParams(vmem_limit_bytes=48 * MIB),
        cost_estimate=pl.CostEstimate(
            flops=2 * rows * tiles * tile * columns,
            bytes_accessed=2 * tiles * tile * (rows + columns) + 8 * rows * columns,
            transcendentals=0,
        ),
        name="base_rows",
    )(place, x, scale, gain, own, weight)


TEAM = 4
SLABS = (0, 2, 1, 3)


def list_runs(place_ref, slots, runs, jobs, start):
    def look(run, carry, slab, d):
        slot = slots[(place_ref[0] ^ d) * runs + run]

        @pl.when(slot >= 0)
        def _():
            jobs[carry] = slab * runs + run
            start(carry, d, run, slot)

        return carry + (slot >= 0).astype(jnp.int32)

    count = jnp.int32(0)
    for slab, d in enumerate(SLABS):
        count = lax.fori_loop(0, runs, functools.partial(look, slab=slab, d=d), count)
    return count


def work_in_teams(count, wait, work):
    def team(g, carry):
        for u in range(TEAM):

            @pl.when(g * TEAM + u < count)
            def _():
                wait(g * TEAM + u)

        work([jnp.minimum(g * TEAM + u, count - 1) for u in range(TEAM)])
        return carry

    lax.fori_loop(0, (count + TEAM - 1) // TEAM, team, 0)


def shrink_kernel(
    place_ref,
    slots,
    x0,
    x1,
    x2,
    x3,
    scale_ref,
    gain_ref,
    down_ref,
    keep_ref,
    send_ref,
    jobs,
    parts,
    held_x,
    held,
    x_sems,
    sems,
):
    runs = held.shape[0] // 4
    rank = held.shape[1]
    x_refs = (x0, x1, x2, x3)

    def x_copy(i, d, run):
        rows = pl.ds(pl.multiple_of(run * 16, 16), 16)
        return pltpu.make_async_copy(x_refs[d].at[rows, :], held_x.at[i], x_sems.at[i])

    def copy(i, slot):
        return pltpu.make_async_copy(down_ref.at[slot], held.at[i], sems.at[i])

    def start(i, d, run, slot):
        copy(i, slot).start()
        x_copy(i, d, run).start()

    def wait(i):
        copy(i, 0).wait()
        x_copy(i, 0, 0).wait()

    def work(members):
        results = []
        for i in members:
            job = jobs[i]
            slab = job // runs
            d = jnp.where(slab == 1, 2, jnp.where(slab == 2, 1, slab))
            rows = pl.ds(pl.multiple_of((job % runs) * 16, 16), 16)
            scale = scale_ref[place_ref[0] ^ d, rows, :]
            normed = (held_x[i].astype(F32) * scale * gain_ref[...]).astype(BF16)
            part = lax.dot_general(
                normed, held[i], (((1,), (1,)), ((), ())), preferred_element_type=F32
            )
            results.append((job, part))
        for job, part in results:
            parts[job] = part

    count = list_runs(place_ref, slots, runs, jobs, start)
    parts[...] = jnp.zeros_like(parts)
    work_in_teams(count, wait, work)
    for slab in range(4):
        for i in range(runs // 2):
            low = slab * runs + i
            out_ref = (keep_ref, send_ref)[slab // 2]
            out_ref[slab % 2, i * 16 : (i + 1) * 16, :] = jnp.concatenate(
                [parts[low], parts[low + runs // 2]], axis=1
            )


def shrink_rows(place, slots, blocks, scales, gain, down):
    rows, depth = blocks[0].shape
    rank = down.shape[1]
    runs = rows // 16
    return pl.pallas_call(
        shrink_kernel,
        out_shape=[jax.ShapeDtypeStruct((2, rows // 2, 2 * rank), F32)] * 2,
        in_specs=[SMEM] * 2 + [HBM] * 4 + [VMEM] * 2 + [HBM],
        out_specs=[VMEM] * 2,
        scratch_shapes=[
            pltpu.SMEM((4 * runs,), jnp.int32),
            pltpu.VMEM((4 * runs, 16, rank), F32),
            pltpu.VMEM((4 * runs, 16, depth), BF16),
            pltpu.VMEM((4 * runs, rank, depth), BF16),
            pltpu.SemaphoreType.DMA((4 * runs,)),
            pltpu.SemaphoreType.DMA((4 * runs,)),
        ],
        compiler_params=pltpu.CompilerParams(vmem_limit_bytes=54 * MIB),
        cost_estimate=pl.CostEstimate(
            flops=2 * rows * depth * rank,
            bytes_accessed=8 * rows * depth + down.size,
            transcendentals=0,
        ),
        name="shrink_rows",
    )(place, slots, *blocks, scales, gain, down)


def grow_kernel(
    place_ref, slots, s0, s1, up_ref, keep_ref, send_ref, jobs, parts, held, sems
):
    runs = held.shape[0] // 4
    rank = held.shape[1]

    def copy(i, slot):
        return pltpu.make_async_copy(up_ref.at[slot], held.at[i], sems.at[i])

    def start(i, d, run, slot):
        copy(i, slot).start()

    def wait(i):
        copy(i, 0).wait()

    def work(members):
        results = []
        for i in members:
            job = jobs[i]
            grown = jnp.dot(parts[job], held[i], preferred_element_type=F32)
            results.append((job, grown))
        for job, grown in results:
            rows = pl.ds(pl.multiple_of((job % runs) * 16, 16), 16)
            slab = job // runs

            @pl.when(slab < 2)
            def _():
                keep_ref[slab, rows, :] = grown

            @pl.when(slab >= 2)
            def _():
                send_ref[slab - 2, rows, :] = grown

    count = list_runs(place_ref, slots, runs, jobs, start)
    for slab in range(4):
        for i in range(runs // 2):
            low = slab * runs + i
            both = (s0, s1)[slab // 2][slab % 2, i * 16 : (i + 1) * 16, :]
            parts[low] = both[:, :rank]
            parts[low + runs // 2] = both[:, rank:]
    keep_ref[...] = jnp.zeros_like(keep_ref)
    send_ref[...] = jnp.zeros_like(send_ref)
    work_in_teams(count, wait, work)


def grow_rows(place, slots, kept, passed, up):
    _, pair_rows, _ = kept.shape
    rows = 2 * pair_rows
    rank, columns = up.shape[1:]
    runs = rows // 16
    return pl.pallas_call(
        grow_kernel,
        out_shape=[jax.ShapeDtypeStruct((2, rows, columns), F32)] * 2,
        in_specs=[SMEM, SMEM, VMEM, VMEM, HBM],
        out_specs=[VMEM] * 2,
        scratch_shapes=[
            pltpu.SMEM((4 * runs,), jnp.int32),
            pltpu.VMEM((4 * runs, 16, rank), BF16),
            pltpu.VMEM((4 * runs, rank, columns), BF16),
            pltpu.SemaphoreType.DMA((4 * runs,)),
        ],
        compiler_params=pltpu.CompilerParams(vmem_limit_bytes=60 * MIB),
        cost_estimate=pl.CostEstimate(
            flops=2 * rows * rank * columns,
            bytes_accessed=8 * rows * columns + up.size,
            transcendentals=0,
        ),
        name="grow_rows",
    )(place, slots, kept, passed, up)


def attend_kernel(
    unit,
    first_row,
    lengths,
    order,
    qkv_ref,
    cos_ref,
    sin_ref,
    cache_ref,
    out_ref,
    queries,
    keys,
    values,
    context,
    held,
    sems,
):
    rows, _, cached, _ = held.shape
    local = STEPS * rows
    q_columns = GROUP * HD
    part = cached // 2
    scale = HD ** (-0.5)
    team = min(4, rows)

    def copy(r, b):
        span = pl.ds(b * part, part)
        return pltpu.make_async_copy(
            cache_ref.at[first_row + r, :, span, :], held.at[r, :, span, :], sems.at[r, b]
        )

    def longest(group):
        return lengths[order[group * team + team - 1]]

    def fetch(i, carry):
        r = order[i]
        copy(r, 0).start()

        @pl.when(longest(i // team) > part)
        def _():
            copy(r, 1).start()

        return carry

    lax.fori_loop(0, rows, fetch, 0)

    cosine = cos_ref[...]
    sine = sin_ref[...]

    def rotated(x):
        x = x.astype(F32)
        turned = x * cosine + pltpu.roll(x, HD // 2, 1) * sine
        return turned.astype(BF16).astype(F32)

    for k in range(KVH):
        for g in range(GROUP):
            queries[k, g * local : (g + 1) * local, :] = rotated(
                qkv_ref[k, :, g * HD : (g + 1) * HD]
            )
        place = q_columns + (k % 2) * HD
        keys[k] = rotated(qkv_ref[k // 2, :, place : place + HD])
        values[k] = qkv_ref[2 + k // 2, :, place : place + HD].astype(F32)

    early = lax.broadcasted_iota(jnp.int32, (4 * GROUP, 1), 0) % (2 * GROUP) < GROUP

    def scores(r, at, pair, span, live):
        heads = (2 * pair, 2 * pair + 1)
        query = [
            jnp.concatenate(
                [queries[k, pl.ds(at[s], GROUP, stride=local), :] for s in range(STEPS)], axis=0
            )
            for k in heads
        ]
        blank = jnp.zeros((2 * GROUP, HD), F32)
        spread = jnp.concatenate(
            [
                jnp.concatenate([query[0], blank], axis=1),
                jnp.concatenate([blank, query[1]], axis=1),
            ],
            axis=0,
        ).astype(BF16)
        old_keys = jnp.concatenate([held[r, k, :span, :HD] for k in heads], axis=1)
        old = lax.dot_general(
            spread, old_keys, (((1,), (1,)), ((), ())), preferred_element_type=F32
        )
        old = jnp.where(live, old * scale, masked)
        fresh = []
        for t in range(STEPS):
            both = jnp.concatenate(
                [
                    jnp.sum(query[i] * keys[k, pl.ds(at[t], 1), :], axis=1, keepdims=True)
                    for i, k in enumerate(heads)
                ],
                axis=0,
            )
            fresh.append(both * scale)
        fresh[1] = jnp.where(early, masked, fresh[1])
        return old, fresh

    def soften(old, fresh):
        peak = jnp.maximum(jnp.max(old, axis=1, keepdims=True), jnp.maximum(fresh[0], fresh[1]))
        p_old = jnp.exp(old - peak)
        p_new = [jnp.exp(f - peak) for f in fresh]
        total = jnp.sum(p_old, axis=1, keepdims=True) + (p_new[0] + p_new[1])
        return p_old.astype(BF16), [p.astype(BF16).astype(F32) for p in p_new], total

    def mix(r, at, pair, span, w_old, w_new, total):
        heads = (2 * pair, 2 * pair + 1)
        old_values = jnp.concatenate([held[r, k, :span, HD:] for k in heads], axis=1)
        mixed = jnp.dot(w_old, old_values, preferred_element_type=F32)
        for i, k in enumerate(heads):
            own = slice(i * 2 * GROUP, (i + 1) * 2 * GROUP)
            result = mixed[own, i * HD : (i + 1) * HD]
            for t in range(STEPS):
                result = result + w_new[t][own] * values[k, pl.ds(at[t], 1), :]
            result = result / total[own]
            for s in range(STEPS):
                context[k, pl.ds(at[s], GROUP, stride=local), :] = result[
                    s * GROUP : (s + 1) * GROUP
                ]

    def attend_team(members, span):
        jobs = []
        for r in members:
            at = [(r // unit) * (STEPS * unit) + s * unit + r % unit for s in range(STEPS)]
            live = lax.broadcasted_iota(jnp.int32, (4 * GROUP, span), 1) < lengths[r]
            for pair in range(KVH // 2):
                jobs.append((r, at, pair, scores(r, at, pair, span, live)))
        softened = [soften(*job[3]) for job in jobs]
        for (r, at, pair, _), weights in zip(jobs, softened):
            mix(r, at, pair, span, *weights)

    def each(group, carry):
        members = [order[group * team + i] for i in range(team)]
        wide = longest(group) > part
        for r in members:
            copy(r, 0).wait()

        @pl.when(wide)
        def _():
            for r in members:
                copy(r, 1).wait()
            attend_team(members, cached)

        @pl.when(jnp.logical_not(wide))
        def _():
            attend_team(members, part)

        return carry

    lax.fori_loop(0, rows // team, each, 0)
    for k in range(KVH):
        for g in range(GROUP):
            place = (k * GROUP + g) * HD
            out_ref[:, place : place + HD] = context[k, g * local : (g + 1) * local, :].astype(BF16)


def attend(lengths, order, qkv, cosine, sine, cache, first_row, unit):
    rows = lengths.shape[0]
    local = STEPS * rows
    _, kv_heads, cached, width = cache.shape
    return pl.pallas_call(
        functools.partial(attend_kernel, unit, first_row),
        out_shape=jax.ShapeDtypeStruct((local, HEADS * HD), BF16),
        in_specs=[SMEM, SMEM, VMEM, VMEM, VMEM, HBM],
        out_specs=VMEM,
        scratch_shapes=[
            pltpu.VMEM((KVH, GROUP * local, HD), F32),
            pltpu.VMEM((KVH, local, HD), F32),
            pltpu.VMEM((KVH, local, HD), F32),
            pltpu.VMEM((KVH, GROUP * local, HD), F32),
            pltpu.VMEM((rows, kv_heads, cached, width), BF16),
            pltpu.SemaphoreType.DMA((rows, 2)),
        ],
        compiler_params=pltpu.CompilerParams(vmem_limit_bytes=48 * MIB),
        cost_estimate=pl.CostEstimate(
            flops=4 * local * HEADS * HD * cached,
            bytes_accessed=2 * rows * kv_heads * cached * width,
            transcendentals=local * HEADS * cached,
        ),
        name="attend",
    )(lengths, order, qkv, cosine, sine, cache)


def out_kernel(count, has_earlier, owners, *refs):
    blocks = refs[:count]
    w_ref = refs[count]
    out_ref, lhs, total, held, sems = refs[-5:]
    local = blocks[0].shape[0]
    rows = local // STEPS
    tiles, depth, columns = held.shape
    halves = out_ref.shape[2]
    copies = [
        pltpu.make_async_copy(w_ref.at[pl.ds(k * depth, depth), :], held.at[k], sems.at[k])
        for k in range(tiles)
    ]
    for copy in copies:
        copy.start()
    slots = count // halves

    def place(j):
        used = jnp.int32(0)
        for i in range(j % slots):
            used = used + (owners[i] >= 0).astype(jnp.int32)
        return (j // slots) * (lhs.shape[0] // halves) + used * local

    lhs[...] = jnp.zeros_like(lhs)
    for j, ref in enumerate(blocks):

        @pl.when(owners[j % slots] >= 0)
        def _():
            lhs[pl.ds(pl.multiple_of(place(j), local), local), :] = ref[...]

    if has_earlier:
        out_ref[...] = refs[count + 1][...]
    width = min(512, columns)
    for k, copy in enumerate(copies):
        copy.wait()
        for j in range(columns // width):
            span = slice(j * width, (j + 1) * width)
            product = jnp.dot(
                lhs[:, k * depth : (k + 1) * depth], held[k, :, span], preferred_element_type=F32
            )
            if k > 0:
                product = total[:, span] + product
            total[:, span] = product
    for j in range(count):

        @pl.when(owners[j % slots] >= 0)
        def _():
            block = total[pl.ds(pl.multiple_of(place(j), local), local), :]
            block = block.reshape(rows // RUN, STEPS, RUN, columns)
            for s in range(STEPS):
                piece = block[:, s].reshape(rows, columns).astype(BF16)
                out_ref[s, owners[j % slots], j // slots] = piece


def project(owners, blocks, weight, present, earlier=None):
    halves = len(blocks)
    flat = [block for part in blocks for block in part]
    local, depth = flat[0].shape
    columns = weight.shape[1]
    tile = min(512, depth)
    rows = local // STEPS
    count = len(flat)
    more = [] if earlier is None else [earlier]
    return pl.pallas_call(
        functools.partial(out_kernel, count, earlier is not None),
        out_shape=jax.ShapeDtypeStruct((STEPS, 4, halves, rows, columns), BF16),
        in_specs=[SMEM] + [VMEM] * count + [HBM] + [VMEM] * len(more),
        out_specs=VMEM,
        scratch_shapes=[
            pltpu.VMEM((present * halves * local, depth), BF16),
            pltpu.VMEM((present * halves * local, columns), F32),
            pltpu.VMEM((depth // tile, tile, columns), BF16),
            pltpu.SemaphoreType.DMA((depth // tile,)),
        ],
        compiler_params=pltpu.CompilerParams(vmem_limit_bytes=52 * MIB),
        cost_estimate=pl.CostEstimate(
            flops=2 * present * halves * local * depth * columns,
            bytes_accessed=2 * depth * columns + 4 * present * local * (depth + columns),
            transcendentals=0,
        ),
        name="project",
    )(owners, *flat, weight, *more)


def lookup(identity, table):
    hits = identity[:, None] == jnp.arange(table.shape[0], dtype=jnp.int32)[None, :]
    return jnp.sum(jnp.where(hits, table[None, :], 0), axis=1)


def ascending(lengths):
    count = lengths.shape[0]
    rows = jnp.arange(count, dtype=jnp.int32)
    keyed = lengths * count + rows
    rank = jnp.sum((keyed[None, :] < keyed[:, None]).astype(jnp.int32), axis=1)
    return jnp.sum(jnp.where(rank[:, None] == rows[None, :], rows[:, None], 0), axis=0)


def angle_tables(lengths, unit):
    steps = jnp.arange(STEPS, dtype=jnp.int32)
    position = lengths.reshape(-1, 1, unit) + steps[None, :, None]
    freq = rope_base ** (-(jnp.arange(HD // 2, dtype=F32) * 2.0 / HD))
    angles = position.reshape(-1).astype(F32)[:, None] * freq
    cosine = jnp.cos(angles)
    sine = jnp.sin(angles)
    return jnp.concatenate([cosine, cosine], 1), jnp.concatenate([-sine, sine], 1)


def on_device(
    hidden,
    input_norm_scale,
    query_key_value_weight,
    output_weight,
    adapter_down_weight,
    adapter_up_weight,
    row_adapter_index,
    adapter_store_slot,
    lengths,
    key_value_cache,
):
    tensor_count = lax.axis_size("tensor")
    tensor_pos = lax.axis_index("tensor")
    store_pos = lax.axis_index("store")
    _, rows, span = hidden.shape
    model_width = input_norm_scale.shape[0]
    rows_here = lengths.shape[0]
    unit = min(RUN, rows_here)
    line = tensor_count == 4 and rows_here % (HALVES * RUN) == 0
    halves = HALVES if line else 1
    part_rows = rows_here // halves
    local = STEPS * part_rows
    held_slots = adapter_down_weight.shape[0]
    rank = adapter_down_weight.shape[2]

    raw = hidden.reshape(STEPS, tensor_count, halves, part_rows // unit, unit, span)
    raw = raw.transpose(2, 1, 3, 0, 4, 5).reshape(STEPS * rows, span)
    own_index = tensor_pos.reshape(1).astype(jnp.int32)
    owners = [own_index] + [hop_owners(tensor_pos, hop) for hop in (1, 2, 3)]
    count = tensor_count * local
    parts = [slice(h * count, (h + 1) * count) for h in range(halves)]
    everything = [lax.all_gather(raw[part], "tensor", axis=0, tiled=False) for part in parts]

    values = raw.astype(F32)
    squares = jnp.sum(values * values, axis=1)
    squares = summed_over(squares, "tensor")
    own_runs = row_adapter_index[::RUN]
    if halves > 1:
        own_runs = own_runs.reshape(tensor_count, halves, -1).swapaxes(0, 1).reshape(-1)
    told = jnp.concatenate([squares, own_runs.astype(F32)]).reshape(1, -1)
    told = jnp.concatenate([told, swap(told, "store", 2)], axis=0)
    told = jnp.concatenate([told, swap(told, "store", 1)], axis=0)
    told = jnp.stack([told[d] for d in (0, 2, 1, 3)])
    told = jnp.stack([jnp.stack([told[p ^ q] for q in range(4)]) for p in range(4)])
    told = lax.dynamic_index_in_dim(told, store_pos, 0, keepdims=False)
    runs = told[:, STEPS * rows :].astype(jnp.int32)
    told = told[:, : STEPS * rows]
    scales = lax.rsqrt(told / model_width + eps_norm)
    slots = lookup(runs.reshape(-1), adapter_store_slot).reshape(runs.shape)
    slots = jnp.where(slots // held_slots == store_pos, slots % held_slots, -1)
    place = store_pos.reshape(1).astype(jnp.int32)
    gains = input_norm_scale.reshape(1, -1)
    gain = lax.dynamic_slice_in_dim(gains, tensor_pos * span, span, 1)
    scales = scales[:, :, None]
    own_scale = lax.dynamic_index_in_dim(scales, store_pos, 0, keepdims=False)

    across = swap(raw, "store", 2)
    beside = swap(raw, "store", 1)
    diagonal = swap(across, "store", 1)
    mine = slots.reshape(-1)
    down = jnp.swapaxes(adapter_down_weight, 1, 2)
    kept, passed = shrink_rows(place, mine, (raw, beside, across, diagonal), scales, gain, down)
    kept = kept + swap(passed, "store", 1)
    shrunk = kept[0] + swap(kept[1], "store", 2)
    shrunk = summed_over(shrunk, "tensor").astype(BF16)
    shrunk = jnp.stack([shrunk, swap(shrunk, "store", 2)])
    kept, passed = grow_rows(place, mine, shrunk, swap(shrunk, "store", 1), adapter_up_weight)
    passed = swap(passed, "store", 1)
    deltas = []
    for part in parts:
        delta = swap((kept[1, part] + passed[1, part]).astype(F16), "store", 2).astype(F32)
        deltas.append((kept[0, part] + passed[0, part]) + delta)

    weight = query_key_value_weight
    raw, passed = lax.optimization_barrier((raw, passed))
    mixed = []
    for h, part in enumerate(parts):
        if mixed:
            everything[h], mixed[-1] = lax.optimization_barrier((everything[h], mixed[-1]))
        own = base_block((raw[part],), own_scale[part], gains, weight, own_index, None)
        total = base_rows(own_index, everything[h], own_scale[part], gains, own, weight, 0)
        mixed.append((total + deltas[h]).astype(BF16))
    mixed = [qkv.reshape(tensor_count, local, -1) for qkv in mixed]

    contexts = []
    exchanged = []
    for qkv in mixed:
        if exchanged:
            qkv, exchanged[-1] = lax.optimization_barrier((qkv, exchanged[-1]))
        exchanged.append(lax.all_to_all(qkv, "tensor", 0, 0, tiled=True))
    for h, moved in enumerate(exchanged):
        if tensor_count != 4:
            q_columns = HEADS * HD // tensor_count
            pieces = []
            for piece in (moved[..., :q_columns], moved[..., q_columns:]):
                joined = piece.transpose(1, 0, 2).reshape(local, 4, -1)
                pieces.append(joined.transpose(1, 0, 2))
            moved = jnp.concatenate(pieces, axis=2)
        here = lengths[h * part_rows : (h + 1) * part_rows]
        cosine, sine = angle_tables(here, unit)
        contexts.append(
            attend(here, ascending(here), moved, cosine, sine, key_value_cache, h * part_rows, unit)
        )

    if line:
        hops = [line_gather(context, "tensor") for context in contexts]
        first = [(context,) + hop[0] for context, hop in zip(contexts, hops)]
        last = [hop[1] + hop[2] for hop in hops]
        output = project(jnp.concatenate(owners[:2]), first, output_weight, 3)
        output = project(jnp.concatenate(owners[2:]), last, output_weight, 2, output)
    else:
        results = []
        for context in contexts:
            context = lax.all_gather(context, "tensor", axis=0, tiled=True)
            result = jnp.dot(context, output_weight, preferred_element_type=F32).astype(BF16)
            result = result.reshape(tensor_count, part_rows // unit, STEPS, unit, -1)
            result = result.transpose(2, 0, 1, 3, 4).reshape(STEPS, tensor_count, part_rows, -1)
            results.append(result)
        output = jnp.stack(results, axis=2)
    return output.reshape(STEPS, rows, -1)


def solution(mesh):
    in_specs = (
        P(None, ("groups", "store"), "tensor"),
        P(),
        P(None, "tensor"),
        P(None, "tensor"),
        P(("groups", "store"), "tensor", None),
        P(("groups", "store"), None, "tensor"),
        P(("groups", "store")),
        P("groups"),
        P(("groups", "store", "tensor")),
        P(("groups", "store", "tensor"), None, None, None),
    )
    out_specs = P(None, ("groups", "store"), "tensor")
    return jax.shard_map(
        on_device, mesh=mesh, in_specs=in_specs, out_specs=out_specs, check_vma=False
    )
```

```python
import functools

import jax
import jax.numpy as jnp
from jax import lax
from jax.experimental import pallas as pl
from jax.experimental.pallas import tpu as pltpu
from jax.sharding import PartitionSpec as P

HEADS = 32
KVH = 4
HD = 128
GROUP = HEADS // KVH
RUN = 8
STEPS = 2
LANES = 128
HALVES = 2

eps_norm = 1e-05
rope_base = 500000.0
masked = -1e30

MIB = 1 << 20
F32 = jnp.float32
BF16 = jnp.bfloat16
F16 = jnp.float16
VMEM = pl.BlockSpec(memory_space=pltpu.VMEM)
SMEM = pl.BlockSpec(memory_space=pltpu.SMEM)
HBM = pl.BlockSpec(memory_space=pltpu.HBM)


def swap(values, axis, distance):
    count = lax.axis_size(axis)
    return lax.ppermute(values, axis, [(i, i ^ distance) for i in range(count)])


def summed_over(values, axis):
    distance = 1
    while distance < lax.axis_size(axis):
        values = values + swap(values, axis, distance)
        distance *= 2
    return values


def line_hop(up, down, axis, hop):
    up = lax.ppermute(up, axis, [(i, i + 1) for i in range(hop - 1, 3)])
    down = lax.ppermute(down, axis, [(i, i - 1) for i in range(4 - hop, 0, -1)])
    return up, down


def line_gather(block, axis):
    hops = [line_hop(block, block, axis, 1)]
    for hop in (2, 3):
        hops.append(line_hop(*hops[-1], axis, hop))
    return hops


def hop_owners(position, hop):
    below = position - hop
    above = position + hop
    return jnp.stack([jnp.where(below >= 0, below, -1), jnp.where(above < 4, above, -1)])


def block_kernel(count, has_total, owners, *refs):
    x_refs = refs[:count]
    scale_ref, gain_ref, w_ref = refs[count : count + 3]
    out_ref, held, sems = refs[-3:]
    _, tiles, depth, _ = held.shape

    def copy(j, k):
        first = pl.multiple_of((owners[j] * tiles + k) * depth, depth)
        return pltpu.make_async_copy(
            w_ref.at[pl.ds(first, depth), :], held.at[j, k], sems.at[j, k]
        )

    for j in range(count):

        @pl.when(owners[j] >= 0)
        def _():
            for k in range(tiles):
                copy(j, k).start()

    out_ref[...] = refs[count + 3][...] if has_total else jnp.zeros_like(out_ref)
    for j, x_ref in enumerate(x_refs):

        @pl.when(owners[j] >= 0)
        def _():
            scale = scale_ref[...]
            for k in range(tiles):
                span = slice(k * depth, (k + 1) * depth)
                first = pl.multiple_of((owners[j] * tiles + k) * depth, depth)
                gain = gain_ref[:, pl.ds(first, depth)]
                normed = (x_ref[:, span].astype(F32) * scale * gain).astype(BF16)
                copy(j, k).wait()
                out_ref[...] += jnp.dot(normed, held[j, k], preferred_element_type=F32)


def base_block(blocks, scale, gain, weight, owners, total):
    rows, depth = blocks[0].shape
    columns = weight.shape[1]
    tile = min(512, depth)
    count = len(blocks)
    operands = [owners, *blocks, scale, gain, weight]
    if total is not None:
        operands.append(total)
    return pl.pallas_call(
        functools.partial(block_kernel, count, total is not None),
        out_shape=jax.ShapeDtypeStruct((rows, columns), F32),
        in_specs=[SMEM] + [VMEM] * (count + 2) + [HBM] + [VMEM] * (total is not None),
        out_specs=VMEM,
        scratch_shapes=[
            pltpu.VMEM((count, depth // tile, tile, columns), BF16),
            pltpu.SemaphoreType.DMA((count, depth // tile)),
        ],
        compiler_params=pltpu.CompilerParams(vmem_limit_bytes=48 * MIB),
        cost_estimate=pl.CostEstimate(
            flops=2 * count * rows * depth * columns,
            bytes_accessed=2 * depth * (rows + columns) + 8 * rows * columns,
            transcendentals=0,
        ),
        name="base_block",
    )(*operands)


def base_kernel(first_row, place_ref, x_ref, scale_ref, gain_ref, own_ref, w_ref, out_ref, held, sems):
    owners, _, span = x_ref.shape
    rows = scale_ref.shape[0]
    tiles, depth, _ = held.shape
    tiles_each = span // depth

    def spot(k):
        owner = lax.rem(place_ref[0] + 1 + k // tiles_each, owners)
        return owner, pl.multiple_of((owner * tiles_each + k % tiles_each) * depth, depth)

    copies = [
        pltpu.make_async_copy(w_ref.at[pl.ds(spot(k)[1], depth), :], held.at[k], sems.at[k])
        for k in range(tiles)
    ]
    for copy in copies:
        copy.start()
    scale = scale_ref[...]
    out_ref[...] = own_ref[first_row : first_row + rows, :]
    for k, copy in enumerate(copies):
        owner, first = spot(k)
        inner = (k % tiles_each) * depth
        gain = gain_ref[:, pl.ds(first, depth)]
        part = x_ref[owner, first_row : first_row + rows, inner : inner + depth].astype(F32)
        normed = (part * scale * gain).astype(BF16)
        copy.wait()
        out_ref[...] += jnp.dot(normed, held[k], preferred_element_type=F32)


def base_rows(place, x, scale, gain, own, weight, first_row):
    owners, _, span = x.shape
    rows = scale.shape[0]
    columns = weight.shape[1]
    tile = min(512, span)
    tiles = (owners - 1) * span // tile
    return pl.pallas_call(
        functools.partial(base_kernel, first_row),
        out_shape=jax.ShapeDtypeStruct((rows, columns), F32),
        in_specs=[SMEM] + [VMEM] * 4 + [HBM],
        out_specs=VMEM,
        scratch_shapes=[
            pltpu.VMEM((tiles, tile, columns), BF16),
            pltpu.SemaphoreType.DMA((tiles,)),
        ],
        compiler_params=pltpu.CompilerParams(vmem_limit_bytes=48 * MIB),
        cost_estimate=pl.CostEstimate(
            flops=2 * rows * tiles * tile * columns,
            bytes_accessed=2 * tiles * tile * (rows + columns) + 8 * rows * columns,
            transcendentals=0,
        ),
        name="base_rows",
    )(place, x, scale, gain, own, weight)


TEAM = 4
SLABS = (0, 2, 1, 3)


def list_runs(place_ref, slots, runs, jobs, start):
    def look(run, carry, slab, d):
        slot = slots[(place_ref[0] ^ d) * runs + run]

        @pl.when(slot >= 0)
        def _():
            jobs[carry] = slab * runs + run
            start(carry, d, run, slot)

        return carry + (slot >= 0).astype(jnp.int32)

    count = jnp.int32(0)
    for slab, d in enumerate(SLABS):
        count = lax.fori_loop(0, runs, functools.partial(look, slab=slab, d=d), count)
    return count


def work_in_teams(count, wait, work):
    def team(g, carry):
        for u in range(TEAM):

            @pl.when(g * TEAM + u < count)
            def _():
                wait(g * TEAM + u)

        work([jnp.minimum(g * TEAM + u, count - 1) for u in range(TEAM)])
        return carry

    lax.fori_loop(0, (count + TEAM - 1) // TEAM, team, 0)


def shrink_kernel(
    place_ref,
    slots,
    x0,
    x1,
    x2,
    x3,
    scale_ref,
    gain_ref,
    down_ref,
    keep_ref,
    send_ref,
    jobs,
    parts,
    held_x,
    held,
    x_sems,
    sems,
):
    runs = held.shape[0] // 4
    rank = held.shape[1]
    x_refs = (x0, x1, x2, x3)

    def x_copy(i, d, run):
        rows = pl.ds(pl.multiple_of(run * 16, 16), 16)
        return pltpu.make_async_copy(x_refs[d].at[rows, :], held_x.at[i], x_sems.at[i])

    def copy(i, slot):
        return pltpu.make_async_copy(down_ref.at[slot], held.at[i], sems.at[i])

    def start(i, d, run, slot):
        copy(i, slot).start()
        x_copy(i, d, run).start()

    def wait(i):
        copy(i, 0).wait()
        x_copy(i, 0, 0).wait()

    def work(members):
        results = []
        for i in members:
            job = jobs[i]
            slab = job // runs
            d = jnp.where(slab == 1, 2, jnp.where(slab == 2, 1, slab))
            rows = pl.ds(pl.multiple_of((job % runs) * 16, 16), 16)
            scale = scale_ref[place_ref[0] ^ d, rows, :]
            normed = (held_x[i].astype(F32) * scale * gain_ref[...]).astype(BF16)
            part = lax.dot_general(
                normed, held[i], (((1,), (1,)), ((), ())), preferred_element_type=F32
            )
            results.append((job, part))
        for job, part in results:
            parts[job] = part

    count = list_runs(place_ref, slots, runs, jobs, start)
    parts[...] = jnp.zeros_like(parts)
    work_in_teams(count, wait, work)
    for slab in range(4):
        for i in range(runs // 2):
            low = slab * runs + i
            out_ref = (keep_ref, send_ref)[slab // 2]
            out_ref[slab % 2, i * 16 : (i + 1) * 16, :] = jnp.concatenate(
                [parts[low], parts[low + runs // 2]], axis=1
            )


def shrink_rows(place, slots, blocks, scales, gain, down):
    rows, depth = blocks[0].shape
    rank = down.shape[1]
    runs = rows // 16
    return pl.pallas_call(
        shrink_kernel,
        out_shape=[jax.ShapeDtypeStruct((2, rows // 2, 2 * rank), F32)] * 2,
        in_specs=[SMEM] * 2 + [HBM] * 4 + [VMEM] * 2 + [HBM],
        out_specs=[VMEM] * 2,
        scratch_shapes=[
            pltpu.SMEM((4 * runs,), jnp.int32),
            pltpu.VMEM((4 * runs, 16, rank), F32),
            pltpu.VMEM((4 * runs, 16, depth), BF16),
            pltpu.VMEM((4 * runs, rank, depth), BF16),
            pltpu.SemaphoreType.DMA((4 * runs,)),
            pltpu.SemaphoreType.DMA((4 * runs,)),
        ],
        compiler_params=pltpu.CompilerParams(vmem_limit_bytes=54 * MIB),
        cost_estimate=pl.CostEstimate(
            flops=rows * depth,
            bytes_accessed=rows * depth,
            transcendentals=0,
        ),
        name="shrink_rows",
    )(place, slots, *blocks, scales, gain, down)


def grow_kernel(
    place_ref, slots, s0, s1, up_ref, keep_ref, send_ref, jobs, parts, held, sems
):
    runs = held.shape[0] // 4
    rank = held.shape[1]

    def copy(i, slot):
        return pltpu.make_async_copy(up_ref.at[slot], held.at[i], sems.at[i])

    def start(i, d, run, slot):
        copy(i, slot).start()

    def wait(i):
        copy(i, 0).wait()

    def work(members):
        results = []
        for i in members:
            job = jobs[i]
            grown = jnp.dot(parts[job], held[i], preferred_element_type=F32)
            results.append((job, grown))
        for job, grown in results:
            rows = pl.ds(pl.multiple_of((job % runs) * 16, 16), 16)
            slab = job // runs

            @pl.when(slab < 2)
            def _():
                keep_ref[slab, rows, :] = grown

            @pl.when(slab >= 2)
            def _():
                send_ref[slab - 2, rows, :] = grown

    count = list_runs(place_ref, slots, runs, jobs, start)
    for slab in range(4):
        for i in range(runs // 2):
            low = slab * runs + i
            both = (s0, s1)[slab // 2][slab % 2, i * 16 : (i + 1) * 16, :]
            parts[low] = both[:, :rank]
            parts[low + runs // 2] = both[:, rank:]
    keep_ref[...] = jnp.zeros_like(keep_ref)
    send_ref[...] = jnp.zeros_like(send_ref)
    work_in_teams(count, wait, work)


def grow_rows(place, slots, kept, passed, up):
    _, pair_rows, _ = kept.shape
    rows = 2 * pair_rows
    rank, columns = up.shape[1:]
    runs = rows // 16
    return pl.pallas_call(
        grow_kernel,
        out_shape=[jax.ShapeDtypeStruct((2, rows, columns), F32)] * 2,
        in_specs=[SMEM, SMEM, VMEM, VMEM, HBM],
        out_specs=[VMEM] * 2,
        scratch_shapes=[
            pltpu.SMEM((4 * runs,), jnp.int32),
            pltpu.VMEM((4 * runs, 16, rank), BF16),
            pltpu.VMEM((4 * runs, rank, columns), BF16),
            pltpu.SemaphoreType.DMA((4 * runs,)),
        ],
        compiler_params=pltpu.CompilerParams(vmem_limit_bytes=60 * MIB),
        cost_estimate=pl.CostEstimate(
            flops=2 * rows * rank * columns,
            bytes_accessed=8 * rows * columns + up.size,
            transcendentals=0,
        ),
        name="grow_rows",
    )(place, slots, kept, passed, up)


def attend_kernel(
    unit,
    first_row,
    lengths,
    order,
    qkv_ref,
    cos_ref,
    sin_ref,
    cache_ref,
    out_ref,
    queries,
    keys,
    values,
    context,
    held,
    sems,
):
    rows, _, cached, _ = held.shape
    local = STEPS * rows
    q_columns = GROUP * HD
    part = cached // 2
    scale = HD ** (-0.5)
    team = min(4, rows)

    def copy(r, b):
        span = pl.ds(b * part, part)
        return pltpu.make_async_copy(
            cache_ref.at[first_row + r, :, span, :], held.at[r, :, span, :], sems.at[r, b]
        )

    def longest(group):
        return lengths[order[group * team + team - 1]]

    def fetch(i, carry):
        r = order[i]
        copy(r, 0).start()

        @pl.when(longest(i // team) > part)
        def _():
            copy(r, 1).start()

        return carry

    lax.fori_loop(0, rows, fetch, 0)

    cosine = cos_ref[...]
    sine = sin_ref[...]

    def rotated(x):
        x = x.astype(F32)
        turned = x * cosine + pltpu.roll(x, HD // 2, 1) * sine
        return turned.astype(BF16).astype(F32)

    for k in range(KVH):
        for g in range(GROUP):
            queries[k, g * local : (g + 1) * local, :] = rotated(
                qkv_ref[k, :, g * HD : (g + 1) * HD]
            )
        place = q_columns + (k % 2) * HD
        keys[k] = rotated(qkv_ref[k // 2, :, place : place + HD])
        values[k] = qkv_ref[2 + k // 2, :, place : place + HD].astype(F32)

    early = lax.broadcasted_iota(jnp.int32, (4 * GROUP, 1), 0) % (2 * GROUP) < GROUP

    def scores(r, at, pair, span, live):
        heads = (2 * pair, 2 * pair + 1)
        query = [
            jnp.concatenate(
                [queries[k, pl.ds(at[s], GROUP, stride=local), :] for s in range(STEPS)], axis=0
            )
            for k in heads
        ]
        blank = jnp.zeros((2 * GROUP, HD), F32)
        spread = jnp.concatenate(
            [
                jnp.concatenate([query[0], blank], axis=1),
                jnp.concatenate([blank, query[1]], axis=1),
            ],
            axis=0,
        ).astype(BF16)
        old_keys = jnp.concatenate([held[r, k, :span, :HD] for k in heads], axis=1)
        old = lax.dot_general(
            spread, old_keys, (((1,), (1,)), ((), ())), preferred_element_type=F32
        )
        old = jnp.where(live, old * scale, masked)
        fresh = []
        for t in range(STEPS):
            both = jnp.concatenate(
                [
                    jnp.sum(query[i] * keys[k, pl.ds(at[t], 1), :], axis=1, keepdims=True)
                    for i, k in enumerate(heads)
                ],
                axis=0,
            )
            fresh.append(both * scale)
        fresh[1] = jnp.where(early, masked, fresh[1])
        return old, fresh

    def soften(old, fresh):
        peak = jnp.maximum(jnp.max(old, axis=1, keepdims=True), jnp.maximum(fresh[0], fresh[1]))
        p_old = jnp.exp(old - peak)
        p_new = [jnp.exp(f - peak) for f in fresh]
        total = jnp.sum(p_old, axis=1, keepdims=True) + (p_new[0] + p_new[1])
        return p_old.astype(BF16), [p.astype(BF16).astype(F32) for p in p_new], total

    def mix(r, at, pair, span, w_old, w_new, total):
        heads = (2 * pair, 2 * pair + 1)
        old_values = jnp.concatenate([held[r, k, :span, HD:] for k in heads], axis=1)
        mixed = jnp.dot(w_old, old_values, preferred_element_type=F32)
        for i, k in enumerate(heads):
            own = slice(i * 2 * GROUP, (i + 1) * 2 * GROUP)
            result = mixed[own, i * HD : (i + 1) * HD]
            for t in range(STEPS):
                result = result + w_new[t][own] * values[k, pl.ds(at[t], 1), :]
            result = result / total[own]
            for s in range(STEPS):
                context[k, pl.ds(at[s], GROUP, stride=local), :] = result[
                    s * GROUP : (s + 1) * GROUP
                ]

    def attend_team(members, span):
        jobs = []
        for r in members:
            at = [(r // unit) * (STEPS * unit) + s * unit + r % unit for s in range(STEPS)]
            live = lax.broadcasted_iota(jnp.int32, (4 * GROUP, span), 1) < lengths[r]
            for pair in range(KVH // 2):
                jobs.append((r, at, pair, scores(r, at, pair, span, live)))
        softened = [soften(*job[3]) for job in jobs]
        for (r, at, pair, _), weights in zip(jobs, softened):
            mix(r, at, pair, span, *weights)

    def each(group, carry):
        members = [order[group * team + i] for i in range(team)]
        wide = longest(group) > part
        for r in members:
            copy(r, 0).wait()

        @pl.when(wide)
        def _():
            for r in members:
                copy(r, 1).wait()
            attend_team(members, cached)

        @pl.when(jnp.logical_not(wide))
        def _():
            attend_team(members, part)

        return carry

    lax.fori_loop(0, rows // team, each, 0)
    for k in range(KVH):
        for g in range(GROUP):
            place = (k * GROUP + g) * HD
            out_ref[:, place : place + HD] = context[k, g * local : (g + 1) * local, :].astype(BF16)


def attend(lengths, order, qkv, cosine, sine, cache, first_row, unit):
    rows = lengths.shape[0]
    local = STEPS * rows
    _, kv_heads, cached, width = cache.shape
    return pl.pallas_call(
        functools.partial(attend_kernel, unit, first_row),
        out_shape=jax.ShapeDtypeStruct((local, HEADS * HD), BF16),
        in_specs=[SMEM, SMEM, VMEM, VMEM, VMEM, HBM],
        out_specs=VMEM,
        scratch_shapes=[
            pltpu.VMEM((KVH, GROUP * local, HD), F32),
            pltpu.VMEM((KVH, local, HD), F32),
            pltpu.VMEM((KVH, local, HD), F32),
            pltpu.VMEM((KVH, GROUP * local, HD), F32),
            pltpu.VMEM((rows, kv_heads, cached, width), BF16),
            pltpu.SemaphoreType.DMA((rows, 2)),
        ],
        compiler_params=pltpu.CompilerParams(vmem_limit_bytes=48 * MIB),
        cost_estimate=pl.CostEstimate(
            flops=4 * local * HEADS * HD * cached,
            bytes_accessed=2 * rows * kv_heads * cached * width,
            transcendentals=local * HEADS * cached,
        ),
        name="attend",
    )(lengths, order, qkv, cosine, sine, cache)


def out_kernel(count, has_earlier, owners, *refs):
    blocks = refs[:count]
    w_ref = refs[count]
    out_ref, lhs, total, held, sems = refs[-5:]
    local = blocks[0].shape[0]
    rows = local // STEPS
    tiles, depth, columns = held.shape
    halves = out_ref.shape[2]
    copies = [
        pltpu.make_async_copy(w_ref.at[pl.ds(k * depth, depth), :], held.at[k], sems.at[k])
        for k in range(tiles)
    ]
    for copy in copies:
        copy.start()
    slots = count // halves

    def place(j):
        used = jnp.int32(0)
        for i in range(j % slots):
            used = used + (owners[i] >= 0).astype(jnp.int32)
        return (j // slots) * (lhs.shape[0] // halves) + used * local

    lhs[...] = jnp.zeros_like(lhs)
    for j, ref in enumerate(blocks):

        @pl.when(owners[j % slots] >= 0)
        def _():
            lhs[pl.ds(pl.multiple_of(place(j), local), local), :] = ref[...]

    if has_earlier:
        out_ref[...] = refs[count + 1][...]
    width = min(512, columns)
    for k, copy in enumerate(copies):
        copy.wait()
        for j in range(columns // width):
            span = slice(j * width, (j + 1) * width)
            product = jnp.dot(
                lhs[:, k * depth : (k + 1) * depth], held[k, :, span], preferred_element_type=F32
            )
            if k > 0:
                product = total[:, span] + product
            total[:, span] = product
    for j in range(count):

        @pl.when(owners[j % slots] >= 0)
        def _():
            block = total[pl.ds(pl.multiple_of(place(j), local), local), :]
            block = block.reshape(rows // RUN, STEPS, RUN, columns)
            for s in range(STEPS):
                piece = block[:, s].reshape(rows, columns).astype(BF16)
                out_ref[s, owners[j % slots], j // slots] = piece


def project(owners, blocks, weight, present, earlier=None):
    halves = len(blocks)
    flat = [block for part in blocks for block in part]
    local, depth = flat[0].shape
    columns = weight.shape[1]
    tile = min(512, depth)
    rows = local // STEPS
    count = len(flat)
    more = [] if earlier is None else [earlier]
    return pl.pallas_call(
        functools.partial(out_kernel, count, earlier is not None),
        out_shape=jax.ShapeDtypeStruct((STEPS, 4, halves, rows, columns), BF16),
        in_specs=[SMEM] + [VMEM] * count + [HBM] + [VMEM] * len(more),
        out_specs=VMEM,
        scratch_shapes=[
            pltpu.VMEM((present * halves * local, depth), BF16),
            pltpu.VMEM((present * halves * local, columns), F32),
            pltpu.VMEM((depth // tile, tile, columns), BF16),
            pltpu.SemaphoreType.DMA((depth // tile,)),
        ],
        compiler_params=pltpu.CompilerParams(vmem_limit_bytes=52 * MIB),
        cost_estimate=pl.CostEstimate(
            flops=2 * present * halves * local * depth * columns,
            bytes_accessed=2 * depth * columns + 4 * present * local * (depth + columns),
            transcendentals=0,
        ),
        name="project",
    )(owners, *flat, weight, *more)


def lookup(identity, table):
    hits = identity[:, None] == jnp.arange(table.shape[0], dtype=jnp.int32)[None, :]
    return jnp.sum(jnp.where(hits, table[None, :], 0), axis=1)


def ascending(lengths):
    count = lengths.shape[0]
    rows = jnp.arange(count, dtype=jnp.int32)
    keyed = lengths * count + rows
    rank = jnp.sum((keyed[None, :] < keyed[:, None]).astype(jnp.int32), axis=1)
    return jnp.sum(jnp.where(rank[:, None] == rows[None, :], rows[:, None], 0), axis=0)


def angle_tables(lengths, unit):
    steps = jnp.arange(STEPS, dtype=jnp.int32)
    position = lengths.reshape(-1, 1, unit) + steps[None, :, None]
    freq = rope_base ** (-(jnp.arange(HD // 2, dtype=F32) * 2.0 / HD))
    angles = position.reshape(-1).astype(F32)[:, None] * freq
    cosine = jnp.cos(angles)
    sine = jnp.sin(angles)
    return jnp.concatenate([cosine, cosine], 1), jnp.concatenate([-sine, sine], 1)


def on_device(
    hidden,
    input_norm_scale,
    query_key_value_weight,
    output_weight,
    adapter_down_weight,
    adapter_up_weight,
    row_adapter_index,
    adapter_store_slot,
    lengths,
    key_value_cache,
):
    tensor_count = lax.axis_size("tensor")
    tensor_pos = lax.axis_index("tensor")
    store_pos = lax.axis_index("store")
    _, rows, span = hidden.shape
    model_width = input_norm_scale.shape[0]
    rows_here = lengths.shape[0]
    unit = min(RUN, rows_here)
    line = tensor_count == 4 and rows_here % (HALVES * RUN) == 0
    halves = HALVES if line else 1
    part_rows = rows_here // halves
    local = STEPS * part_rows
    held_slots = adapter_down_weight.shape[0]
    rank = adapter_down_weight.shape[2]

    raw = hidden.reshape(STEPS, tensor_count, halves, part_rows // unit, unit, span)
    raw = raw.transpose(2, 1, 3, 0, 4, 5).reshape(STEPS * rows, span)
    own_index = tensor_pos.reshape(1).astype(jnp.int32)
    owners = [own_index] + [hop_owners(tensor_pos, hop) for hop in (1, 2, 3)]
    count = tensor_count * local
    parts = [slice(h * count, (h + 1) * count) for h in range(halves)]
    values = raw.astype(F32)
    squares = jnp.sum(values * values, axis=1)
    if line:
        squares = squares + sum(swap(squares, "tensor", d) for d in (1, 2, 3))
        travelling, squares = lax.optimization_barrier((raw, squares))
        hop1 = line_hop(travelling, travelling, "tensor", 1)
    else:
        squares = summed_over(squares, "tensor")
    own_runs = row_adapter_index[::RUN]
    if halves > 1:
        own_runs = own_runs.reshape(tensor_count, halves, -1).swapaxes(0, 1).reshape(-1)
    told = jnp.concatenate([squares, own_runs.astype(F32)]).reshape(1, -1)
    told = jnp.concatenate([told, swap(told, "store", 2)], axis=0)
    if line:
        told, hop1 = lax.optimization_barrier((told, hop1))
        hop2 = line_hop(*hop1, "tensor", 2)
    told = jnp.concatenate([told, swap(told, "store", 1)], axis=0)
    told = jnp.stack([told[d] for d in (0, 2, 1, 3)])
    told = jnp.stack([jnp.stack([told[p ^ q] for q in range(4)]) for p in range(4)])
    told = lax.dynamic_index_in_dim(told, store_pos, 0, keepdims=False)
    runs = told[:, STEPS * rows :].astype(jnp.int32)
    told = told[:, : STEPS * rows]
    scales = lax.rsqrt(told / model_width + eps_norm)
    slots = lookup(runs.reshape(-1), adapter_store_slot).reshape(runs.shape)
    slots = jnp.where(slots // held_slots == store_pos, slots % held_slots, -1)
    place = store_pos.reshape(1).astype(jnp.int32)
    gains = input_norm_scale.reshape(1, -1)
    gain = lax.dynamic_slice_in_dim(gains, tensor_pos * span, span, 1)
    scales = scales[:, :, None]
    own_scale = lax.dynamic_index_in_dim(scales, store_pos, 0, keepdims=False)

    across = swap(raw, "store", 2)
    beside = swap(raw, "store", 1)
    diagonal = swap(across, "store", 1)
    mine = slots.reshape(-1)
    down = jnp.swapaxes(adapter_down_weight, 1, 2)
    kept, passed = shrink_rows(place, mine, (raw, beside, across, diagonal), scales, gain, down)
    kept = kept + swap(passed, "store", 1)
    shrunk = kept[0] + swap(kept[1], "store", 2)
    if line:
        shrunk = shrunk + swap(shrunk, "tensor", 1)
        shrunk, hop2 = lax.optimization_barrier((shrunk, hop2))
        shrunk = shrunk + swap(shrunk, "tensor", 2)
        shrunk, sent = lax.optimization_barrier((shrunk, hop2))
        hop3 = line_hop(*sent, "tensor", 3)
    else:
        shrunk = summed_over(shrunk, "tensor")
    shrunk = shrunk.astype(BF16)
    shrunk = jnp.stack([shrunk, swap(shrunk, "store", 2)])
    kept, passed = grow_rows(place, mine, shrunk, swap(shrunk, "store", 1), adapter_up_weight)
    passed = swap(passed, "store", 1)
    deltas = []
    for part in parts:
        delta = swap((kept[1, part] + passed[1, part]).astype(F16), "store", 2).astype(F32)
        deltas.append((kept[0, part] + passed[0, part]) + delta)

    weight = query_key_value_weight
    raw, passed = lax.optimization_barrier((raw, passed))
    if line:
        near = jnp.concatenate(owners[:3])
        total = base_block((raw,) + hop1 + hop2, own_scale, gains, weight, near, None)
        total = base_block(hop3, own_scale, gains, weight, owners[3], total)
    else:
        everything = lax.all_gather(raw, "tensor", axis=0, tiled=False)
        own = base_block((raw,), own_scale, gains, weight, own_index, None)
        total = base_rows(own_index, everything, own_scale, gains, own, weight, 0)
    mixed = [(total[part] + delta).astype(BF16) for part, delta in zip(parts, deltas)]
    mixed = [qkv.reshape(tensor_count, local, -1) for qkv in mixed]

    contexts = []
    exchanged = []
    for qkv in mixed:
        if exchanged:
            qkv, exchanged[-1] = lax.optimization_barrier((qkv, exchanged[-1]))
        exchanged.append(lax.all_to_all(qkv, "tensor", 0, 0, tiled=True))
    for h, moved in enumerate(exchanged):
        if tensor_count != 4:
            q_columns = HEADS * HD // tensor_count
            pieces = []
            for piece in (moved[..., :q_columns], moved[..., q_columns:]):
                joined = piece.transpose(1, 0, 2).reshape(local, 4, -1)
                pieces.append(joined.transpose(1, 0, 2))
            moved = jnp.concatenate(pieces, axis=2)
        here = lengths[h * part_rows : (h + 1) * part_rows]
        cosine, sine = angle_tables(here, unit)
        contexts.append(
            attend(here, ascending(here), moved, cosine, sine, key_value_cache, h * part_rows, unit)
        )

    if line:
        hops = [line_gather(context, "tensor") for context in contexts]
        first = [(context,) + hop[0] for context, hop in zip(contexts, hops)]
        last = [hop[1] + hop[2] for hop in hops]
        output = project(jnp.concatenate(owners[:2]), first, output_weight, 3)
        output = project(jnp.concatenate(owners[2:]), last, output_weight, 2, output)
    else:
        results = []
        for context in contexts:
            context = lax.all_gather(context, "tensor", axis=0, tiled=True)
            result = jnp.dot(context, output_weight, preferred_element_type=F32).astype(BF16)
            result = result.reshape(tensor_count, part_rows // unit, STEPS, unit, -1)
            result = result.transpose(2, 0, 1, 3, 4).reshape(STEPS, tensor_count, part_rows, -1)
            results.append(result)
        output = jnp.stack(results, axis=2)
    return output.reshape(STEPS, rows, -1)


def solution(mesh):
    in_specs = (
        P(None, ("groups", "store"), "tensor"),
        P(),
        P(None, "tensor"),
        P(None, "tensor"),
        P(("groups", "store"), "tensor", None),
        P(("groups", "store"), None, "tensor"),
        P(("groups", "store")),
        P("groups"),
        P(("groups", "store", "tensor")),
        P(("groups", "store", "tensor"), None, None, None),
    )
    out_specs = P(None, ("groups", "store"), "tensor")
    return jax.shard_map(
        on_device, mesh=mesh, in_specs=in_specs, out_specs=out_specs, check_vma=False
    )
```

```python
import functools

import jax
import jax.numpy as jnp
from jax import lax
from jax.experimental import pallas as pl
from jax.experimental.pallas import tpu as pltpu
from jax.sharding import PartitionSpec as P

HEADS = 32
KVH = 4
HD = 128
GROUP = HEADS // KVH
RUN = 8
STEPS = 2
LANES = 128
HALVES = 2

eps_norm = 1e-05
rope_base = 500000.0
masked = -1e30

MIB = 1 << 20
F32 = jnp.float32
BF16 = jnp.bfloat16
F16 = jnp.float16
VMEM = pl.BlockSpec(memory_space=pltpu.VMEM)
SMEM = pl.BlockSpec(memory_space=pltpu.SMEM)
HBM = pl.BlockSpec(memory_space=pltpu.HBM)


def swap(values, axis, distance):
    count = lax.axis_size(axis)
    return lax.ppermute(values, axis, [(i, i ^ distance) for i in range(count)])


def summed_over(values, axis):
    distance = 1
    while distance < lax.axis_size(axis):
        values = values + swap(values, axis, distance)
        distance *= 2
    return values


def line_hop(up, down, axis, hop):
    up = lax.ppermute(up, axis, [(i, i + 1) for i in range(hop - 1, 3)])
    down = lax.ppermute(down, axis, [(i, i - 1) for i in range(4 - hop, 0, -1)])
    return up, down


def line_gather(block, axis):
    hops = [line_hop(block, block, axis, 1)]
    for hop in (2, 3):
        hops.append(line_hop(*hops[-1], axis, hop))
    return hops


def hop_owners(position, hop):
    below = position - hop
    above = position + hop
    return jnp.stack([jnp.where(below >= 0, below, -1), jnp.where(above < 4, above, -1)])


def block_kernel(first_rows, owners, *refs):
    count = len(refs) - 6
    x_refs = refs[:count]
    scale_ref, gain_ref, w_ref, out_ref, held, sems = refs[count:]
    rows = scale_ref.shape[0]
    slots, tiles, depth, _ = held.shape

    def slot(j):
        used = jnp.int32(0)
        for i in range(j):
            used = used + (owners[i] >= 0).astype(jnp.int32)
        return used

    def copy(j, k):
        first = pl.multiple_of((owners[j] * tiles + k) * depth, depth)
        return pltpu.make_async_copy(
            w_ref.at[pl.ds(first, depth), :], held.at[slot(j), k], sems.at[slot(j), k]
        )

    for j in range(count):

        @pl.when(owners[j] >= 0)
        def _():
            for k in range(tiles):
                copy(j, k).start()

    out_ref[...] = jnp.zeros_like(out_ref)
    for j, x_ref in enumerate(x_refs):

        @pl.when(owners[j] >= 0)
        def _():
            scale = scale_ref[...]
            for k in range(tiles):
                span = slice(k * depth, (k + 1) * depth)
                first = pl.multiple_of((owners[j] * tiles + k) * depth, depth)
                gain = gain_ref[:, pl.ds(first, depth)]
                part = x_ref[first_rows[j] : first_rows[j] + rows, span].astype(F32)
                normed = (part * scale * gain).astype(BF16)
                copy(j, k).wait()
                out_ref[...] += jnp.dot(normed, held[slot(j), k], preferred_element_type=F32)


def base_block(blocks, scale, gain, weight, owners, first_rows=(0,), present=1):
    depth = blocks[0].shape[1]
    rows = scale.shape[0]
    columns = weight.shape[1]
    tile = min(512, depth)
    count = len(blocks)
    return pl.pallas_call(
        functools.partial(block_kernel, first_rows),
        out_shape=jax.ShapeDtypeStruct((rows, columns), F32),
        in_specs=[SMEM] + [VMEM] * (count + 2) + [HBM],
        out_specs=VMEM,
        scratch_shapes=[
            pltpu.VMEM((present, depth // tile, tile, columns), BF16),
            pltpu.SemaphoreType.DMA((present, depth // tile)),
        ],
        compiler_params=pltpu.CompilerParams(vmem_limit_bytes=48 * MIB),
        cost_estimate=pl.CostEstimate(
            flops=2 * present * rows * depth * columns,
            bytes_accessed=2 * present * depth * (rows + columns) + 4 * rows * columns,
            transcendentals=0,
        ),
        name="base_block",
    )(owners, *blocks, scale, gain, weight)


def base_kernel(first_row, place_ref, x_ref, scale_ref, gain_ref, own_ref, w_ref, out_ref, held, sems):
    owners, _, span = x_ref.shape
    rows = scale_ref.shape[0]
    tiles, depth, _ = held.shape
    tiles_each = span // depth

    def spot(k):
        owner = lax.rem(place_ref[0] + 1 + k // tiles_each, owners)
        return owner, pl.multiple_of((owner * tiles_each + k % tiles_each) * depth, depth)

    copies = [
        pltpu.make_async_copy(w_ref.at[pl.ds(spot(k)[1], depth), :], held.at[k], sems.at[k])
        for k in range(tiles)
    ]
    for copy in copies:
        copy.start()
    scale = scale_ref[...]
    out_ref[...] = own_ref[first_row : first_row + rows, :]
    for k, copy in enumerate(copies):
        owner, first = spot(k)
        inner = (k % tiles_each) * depth
        gain = gain_ref[:, pl.ds(first, depth)]
        part = x_ref[owner, first_row : first_row + rows, inner : inner + depth].astype(F32)
        normed = (part * scale * gain).astype(BF16)
        copy.wait()
        out_ref[...] += jnp.dot(normed, held[k], preferred_element_type=F32)


def base_rows(place, x, scale, gain, own, weight, first_row):
    owners, _, span = x.shape
    rows = scale.shape[0]
    columns = weight.shape[1]
    tile = min(512, span)
    tiles = (owners - 1) * span // tile
    return pl.pallas_call(
        functools.partial(base_kernel, first_row),
        out_shape=jax.ShapeDtypeStruct((rows, columns), F32),
        in_specs=[SMEM] + [VMEM] * 4 + [HBM],
        out_specs=VMEM,
        scratch_shapes=[
            pltpu.VMEM((tiles, tile, columns), BF16),
            pltpu.SemaphoreType.DMA((tiles,)),
        ],
        compiler_params=pltpu.CompilerParams(vmem_limit_bytes=48 * MIB),
        cost_estimate=pl.CostEstimate(
            flops=2 * rows * tiles * tile * columns,
            bytes_accessed=2 * tiles * tile * (rows + columns) + 8 * rows * columns,
            transcendentals=0,
        ),
        name="base_rows",
    )(place, x, scale, gain, own, weight)


TEAM = 4
SLABS = (0, 2, 1, 3)


def list_runs(place_ref, slots, runs, jobs, start):
    def look(run, carry, slab, d):
        slot = slots[(place_ref[0] ^ d) * runs + run]

        @pl.when(slot >= 0)
        def _():
            jobs[carry] = slab * runs + run
            start(carry, d, run, slot)

        return carry + (slot >= 0).astype(jnp.int32)

    count = jnp.int32(0)
    for slab, d in enumerate(SLABS):
        count = lax.fori_loop(0, runs, functools.partial(look, slab=slab, d=d), count)
    return count


def work_in_teams(count, wait, work):
    def team(g, carry):
        for u in range(TEAM):

            @pl.when(g * TEAM + u < count)
            def _():
                wait(g * TEAM + u)

        work([jnp.minimum(g * TEAM + u, count - 1) for u in range(TEAM)])
        return carry

    lax.fori_loop(0, (count + TEAM - 1) // TEAM, team, 0)


def shrink_kernel(
    place_ref,
    slots,
    x0,
    x1,
    x2,
    x3,
    scale_ref,
    gain_ref,
    down_ref,
    keep_ref,
    send_ref,
    jobs,
    parts,
    held_x,
    held,
    x_sems,
    sems,
):
    runs = held.shape[0] // 4
    rank = held.shape[1]
    x_refs = (x0, x1, x2, x3)

    def x_copy(i, d, run):
        rows = pl.ds(pl.multiple_of(run * 16, 16), 16)
        return pltpu.make_async_copy(x_refs[d].at[rows, :], held_x.at[i], x_sems.at[i])

    def copy(i, slot):
        return pltpu.make_async_copy(down_ref.at[slot], held.at[i], sems.at[i])

    def start(i, d, run, slot):
        copy(i, slot).start()
        x_copy(i, d, run).start()

    def wait(i):
        copy(i, 0).wait()
        x_copy(i, 0, 0).wait()

    def work(members):
        results = []
        for i in members:
            job = jobs[i]
            slab = job // runs
            d = jnp.where(slab == 1, 2, jnp.where(slab == 2, 1, slab))
            rows = pl.ds(pl.multiple_of((job % runs) * 16, 16), 16)
            scale = scale_ref[place_ref[0] ^ d, rows, :]
            normed = (held_x[i].astype(F32) * scale * gain_ref[...]).astype(BF16)
            part = lax.dot_general(
                normed, held[i], (((1,), (1,)), ((), ())), preferred_element_type=F32
            )
            results.append((job, part))
        for job, part in results:
            parts[job] = part

    count = list_runs(place_ref, slots, runs, jobs, start)
    parts[...] = jnp.zeros_like(parts)
    work_in_teams(count, wait, work)
    for slab in range(4):
        for i in range(runs // 2):
            low = slab * runs + i
            out_ref = (keep_ref, send_ref)[slab // 2]
            out_ref[slab % 2, i * 16 : (i + 1) * 16, :] = jnp.concatenate(
                [parts[low], parts[low + runs // 2]], axis=1
            )


def shrink_rows(place, slots, blocks, scales, gain, down):
    rows, depth = blocks[0].shape
    rank = down.shape[1]
    runs = rows // 16
    return pl.pallas_call(
        shrink_kernel,
        out_shape=[jax.ShapeDtypeStruct((2, rows // 2, 2 * rank), F32)] * 2,
        in_specs=[SMEM] * 2 + [HBM] * 4 + [VMEM] * 2 + [HBM],
        out_specs=[VMEM] * 2,
        scratch_shapes=[
            pltpu.SMEM((4 * runs,), jnp.int32),
            pltpu.VMEM((4 * runs, 16, rank), F32),
            pltpu.VMEM((4 * runs, 16, depth), BF16),
            pltpu.VMEM((4 * runs, rank, depth), BF16),
            pltpu.SemaphoreType.DMA((4 * runs,)),
            pltpu.SemaphoreType.DMA((4 * runs,)),
        ],
        compiler_params=pltpu.CompilerParams(vmem_limit_bytes=54 * MIB),
        cost_estimate=pl.CostEstimate(
            flops=rows * depth,
            bytes_accessed=rows * depth,
            transcendentals=0,
        ),
        name="shrink_rows",
    )(place, slots, *blocks, scales, gain, down)


def grow_kernel(
    place_ref, slots, s0, s1, up_ref, keep_ref, *refs
):
    *sends, jobs, parts, held, sems = refs
    pieces = len(sends) // 2
    piece = keep_ref.shape[1] // pieces
    runs = held.shape[0] // 4
    rank = held.shape[1]

    def copy(i, slot):
        return pltpu.make_async_copy(up_ref.at[slot], held.at[i], sems.at[i])

    def start(i, d, run, slot):
        copy(i, slot).start()

    def wait(i):
        copy(i, 0).wait()

    def work(members):
        results = []
        for i in members:
            job = jobs[i]
            grown = jnp.dot(parts[job], held[i], preferred_element_type=F32)
            results.append((job, grown))
        for job, grown in results:
            rows = pl.ds(pl.multiple_of((job % runs) * 16, 16), 16)
            slab = job // runs

            @pl.when(slab < 2)
            def _():
                keep_ref[slab, rows, :] = grown

            run = job % runs
            inner = pl.ds(pl.multiple_of(lax.rem(run * 16, piece), 16), 16)
            target = (slab - 2) * pieces + (run * 16) // piece
            for i, send_ref in enumerate(sends):

                @pl.when((slab >= 2) & (target == i))
                def _():
                    send_ref[inner, :] = grown

    count = list_runs(place_ref, slots, runs, jobs, start)
    for slab in range(4):
        for i in range(runs // 2):
            low = slab * runs + i
            both = (s0, s1)[slab // 2][slab % 2, i * 16 : (i + 1) * 16, :]
            parts[low] = both[:, :rank]
            parts[low + runs // 2] = both[:, rank:]
    keep_ref[...] = jnp.zeros_like(keep_ref)
    for send_ref in sends:
        send_ref[...] = jnp.zeros_like(send_ref)
    work_in_teams(count, wait, work)


def grow_rows(place, slots, kept, passed, up, pieces):
    _, pair_rows, _ = kept.shape
    rows = 2 * pair_rows
    rank, columns = up.shape[1:]
    runs = rows // 16
    return pl.pallas_call(
        grow_kernel,
        out_shape=[jax.ShapeDtypeStruct((2, rows, columns), F32)]
        + [jax.ShapeDtypeStruct((rows // pieces, columns), F32)] * (2 * pieces),
        in_specs=[SMEM, SMEM, VMEM, VMEM, HBM],
        out_specs=[VMEM] * (1 + 2 * pieces),
        scratch_shapes=[
            pltpu.SMEM((4 * runs,), jnp.int32),
            pltpu.VMEM((4 * runs, 16, rank), BF16),
            pltpu.VMEM((4 * runs, rank, columns), BF16),
            pltpu.SemaphoreType.DMA((4 * runs,)),
        ],
        compiler_params=pltpu.CompilerParams(vmem_limit_bytes=60 * MIB),
        cost_estimate=pl.CostEstimate(
            flops=rows * columns,
            bytes_accessed=rows * columns,
            transcendentals=0,
        ),
        name="grow_rows",
    )(place, slots, kept, passed, up)


def attend_kernel(
    unit,
    first_row,
    lengths,
    order,
    qkv_ref,
    cos_ref,
    sin_ref,
    cache_ref,
    out_ref,
    queries,
    keys,
    values,
    context,
    held,
    sems,
):
    rows, _, cached, _ = held.shape
    local = STEPS * rows
    q_columns = GROUP * HD
    part = cached // 2
    scale = HD ** (-0.5)
    team = min(4, rows)

    def copy(r, b):
        span = pl.ds(b * part, part)
        return pltpu.make_async_copy(
            cache_ref.at[first_row + r, :, span, :], held.at[r, :, span, :], sems.at[r, b]
        )

    def longest(group):
        return lengths[order[group * team + team - 1]]

    def fetch(i, carry):
        r = order[i]
        copy(r, 0).start()

        @pl.when(longest(i // team) > part)
        def _():
            copy(r, 1).start()

        return carry

    lax.fori_loop(0, rows, fetch, 0)

    cosine = cos_ref[...]
    sine = sin_ref[...]

    def rotated(x):
        x = x.astype(F32)
        turned = x * cosine + pltpu.roll(x, HD // 2, 1) * sine
        return turned.astype(BF16).astype(F32)

    for k in range(KVH):
        for g in range(GROUP):
            queries[k, g * local : (g + 1) * local, :] = rotated(
                qkv_ref[k, :, g * HD : (g + 1) * HD]
            )
        place = q_columns + (k % 2) * HD
        keys[k] = rotated(qkv_ref[k // 2, :, place : place + HD])
        values[k] = qkv_ref[2 + k // 2, :, place : place + HD].astype(F32)

    early = lax.broadcasted_iota(jnp.int32, (4 * GROUP, 1), 0) % (2 * GROUP) < GROUP

    def scores(r, at, pair, span, live):
        heads = (2 * pair, 2 * pair + 1)
        query = [
            jnp.concatenate(
                [queries[k, pl.ds(at[s], GROUP, stride=local), :] for s in range(STEPS)], axis=0
            )
            for k in heads
        ]
        blank = jnp.zeros((2 * GROUP, HD), F32)
        spread = jnp.concatenate(
            [
                jnp.concatenate([query[0], blank], axis=1),
                jnp.concatenate([blank, query[1]], axis=1),
            ],
            axis=0,
        ).astype(BF16)
        old_keys = jnp.concatenate([held[r, k, :span, :HD] for k in heads], axis=1)
        old = lax.dot_general(
            spread, old_keys, (((1,), (1,)), ((), ())), preferred_element_type=F32
        )
        old = jnp.where(live, old * scale, masked)
        fresh = []
        for t in range(STEPS):
            both = jnp.concatenate(
                [
                    jnp.sum(query[i] * keys[k, pl.ds(at[t], 1), :], axis=1, keepdims=True)
                    for i, k in enumerate(heads)
                ],
                axis=0,
            )
            fresh.append(both * scale)
        fresh[1] = jnp.where(early, masked, fresh[1])
        return old, fresh

    def soften(old, fresh):
        peak = jnp.maximum(jnp.max(old, axis=1, keepdims=True), jnp.maximum(fresh[0], fresh[1]))
        p_old = jnp.exp(old - peak)
        p_new = [jnp.exp(f - peak) for f in fresh]
        total = jnp.sum(p_old, axis=1, keepdims=True) + (p_new[0] + p_new[1])
        return p_old.astype(BF16), [p.astype(BF16).astype(F32) for p in p_new], total

    def mix(r, at, pair, span, w_old, w_new, total):
        heads = (2 * pair, 2 * pair + 1)
        old_values = jnp.concatenate([held[r, k, :span, HD:] for k in heads], axis=1)
        mixed = jnp.dot(w_old, old_values, preferred_element_type=F32)
        for i, k in enumerate(heads):
            own = slice(i * 2 * GROUP, (i + 1) * 2 * GROUP)
            result = mixed[own, i * HD : (i + 1) * HD]
            for t in range(STEPS):
                result = result + w_new[t][own] * values[k, pl.ds(at[t], 1), :]
            result = result / total[own]
            for s in range(STEPS):
                context[k, pl.ds(at[s], GROUP, stride=local), :] = result[
                    s * GROUP : (s + 1) * GROUP
                ]

    def attend_team(members, span):
        jobs = []
        for r in members:
            at = [(r // unit) * (STEPS * unit) + s * unit + r % unit for s in range(STEPS)]
            live = lax.broadcasted_iota(jnp.int32, (4 * GROUP, span), 1) < lengths[r]
            for pair in range(KVH // 2):
                jobs.append((r, at, pair, scores(r, at, pair, span, live)))
        softened = [soften(*job[3]) for job in jobs]
        for (r, at, pair, _), weights in zip(jobs, softened):
            mix(r, at, pair, span, *weights)

    def each(group, carry):
        members = [order[group * team + i] for i in range(team)]
        wide = longest(group) > part
        for r in members:
            copy(r, 0).wait()

        @pl.when(wide)
        def _():
            for r in members:
                copy(r, 1).wait()
            attend_team(members, cached)

        @pl.when(jnp.logical_not(wide))
        def _():
            attend_team(members, part)

        return carry

    lax.fori_loop(0, rows // team, each, 0)
    for k in range(KVH):
        for g in range(GROUP):
            place = (k * GROUP + g) * HD
            out_ref[:, place : place + HD] = context[k, g * local : (g + 1) * local, :].astype(BF16)


def attend(lengths, order, qkv, cosine, sine, cache, first_row, unit):
    rows = lengths.shape[0]
    local = STEPS * rows
    _, kv_heads, cached, width = cache.shape
    return pl.pallas_call(
        functools.partial(attend_kernel, unit, first_row),
        out_shape=jax.ShapeDtypeStruct((local, HEADS * HD), BF16),
        in_specs=[SMEM, SMEM, VMEM, VMEM, VMEM, HBM],
        out_specs=VMEM,
        scratch_shapes=[
            pltpu.VMEM((KVH, GROUP * local, HD), F32),
            pltpu.VMEM((KVH, local, HD), F32),
            pltpu.VMEM((KVH, local, HD), F32),
            pltpu.VMEM((KVH, GROUP * local, HD), F32),
            pltpu.VMEM((rows, kv_heads, cached, width), BF16),
            pltpu.SemaphoreType.DMA((rows, 2)),
        ],
        compiler_params=pltpu.CompilerParams(vmem_limit_bytes=48 * MIB),
        cost_estimate=pl.CostEstimate(
            flops=4 * local * HEADS * HD * cached,
            bytes_accessed=2 * rows * kv_heads * cached * width,
            transcendentals=local * HEADS * cached,
        ),
        name="attend",
    )(lengths, order, qkv, cosine, sine, cache)


def out_kernel(count, has_earlier, owners, *refs):
    blocks = refs[:count]
    w_ref = refs[count]
    out_ref, lhs, total, held, sems = refs[-5:]
    local = blocks[0].shape[0]
    rows = local // STEPS
    tiles, depth, columns = held.shape
    halves = out_ref.shape[2]
    copies = [
        pltpu.make_async_copy(w_ref.at[pl.ds(k * depth, depth), :], held.at[k], sems.at[k])
        for k in range(tiles)
    ]
    for copy in copies:
        copy.start()
    slots = count // halves

    def place(j):
        used = jnp.int32(0)
        for i in range(j % slots):
            used = used + (owners[i] >= 0).astype(jnp.int32)
        return (j // slots) * (lhs.shape[0] // halves) + used * local

    lhs[...] = jnp.zeros_like(lhs)
    for j, ref in enumerate(blocks):

        @pl.when(owners[j % slots] >= 0)
        def _():
            lhs[pl.ds(pl.multiple_of(place(j), local), local), :] = ref[...]

    if has_earlier:
        out_ref[...] = refs[count + 1][...]
    width = min(512, columns)
    for k, copy in enumerate(copies):
        copy.wait()
        for j in range(columns // width):
            span = slice(j * width, (j + 1) * width)
            product = jnp.dot(
                lhs[:, k * depth : (k + 1) * depth], held[k, :, span], preferred_element_type=F32
            )
            if k > 0:
                product = total[:, span] + product
            total[:, span] = product
    for j in range(count):

        @pl.when(owners[j % slots] >= 0)
        def _():
            block = total[pl.ds(pl.multiple_of(place(j), local), local), :]
            block = block.reshape(rows // RUN, STEPS, RUN, columns)
            for s in range(STEPS):
                piece = block[:, s].reshape(rows, columns).astype(BF16)
                out_ref[s, owners[j % slots], j // slots] = piece


def project(owners, blocks, weight, present, earlier=None):
    halves = len(blocks)
    flat = [block for part in blocks for block in part]
    local, depth = flat[0].shape
    columns = weight.shape[1]
    tile = min(512, depth)
    rows = local // STEPS
    count = len(flat)
    more = [] if earlier is None else [earlier]
    return pl.pallas_call(
        functools.partial(out_kernel, count, earlier is not None),
        out_shape=jax.ShapeDtypeStruct((STEPS, 4, halves, rows, columns), BF16),
        in_specs=[SMEM] + [VMEM] * count + [HBM] + [VMEM] * len(more),
        out_specs=VMEM,
        scratch_shapes=[
            pltpu.VMEM((present * halves * local, depth), BF16),
            pltpu.VMEM((present * halves * local, columns), F32),
            pltpu.VMEM((depth // tile, tile, columns), BF16),
            pltpu.SemaphoreType.DMA((depth // tile,)),
        ],
        compiler_params=pltpu.CompilerParams(vmem_limit_bytes=52 * MIB),
        cost_estimate=pl.CostEstimate(
            flops=2 * present * halves * local * depth * columns,
            bytes_accessed=2 * depth * columns + 4 * present * local * (depth + columns),
            transcendentals=0,
        ),
        name="project",
    )(owners, *flat, weight, *more)


def lookup(identity, table):
    hits = identity[:, None] == jnp.arange(table.shape[0], dtype=jnp.int32)[None, :]
    return jnp.sum(jnp.where(hits, table[None, :], 0), axis=1)


def ascending(lengths):
    count = lengths.shape[0]
    rows = jnp.arange(count, dtype=jnp.int32)
    keyed = lengths * count + rows
    rank = jnp.sum((keyed[None, :] < keyed[:, None]).astype(jnp.int32), axis=1)
    return jnp.sum(jnp.where(rank[:, None] == rows[None, :], rows[:, None], 0), axis=0)


def angle_tables(lengths, unit):
    steps = jnp.arange(STEPS, dtype=jnp.int32)
    position = lengths.reshape(-1, 1, unit) + steps[None, :, None]
    freq = rope_base ** (-(jnp.arange(HD // 2, dtype=F32) * 2.0 / HD))
    angles = position.reshape(-1).astype(F32)[:, None] * freq
    cosine = jnp.cos(angles)
    sine = jnp.sin(angles)
    return jnp.concatenate([cosine, cosine], 1), jnp.concatenate([-sine, sine], 1)


def on_device(
    hidden,
    input_norm_scale,
    query_key_value_weight,
    output_weight,
    adapter_down_weight,
    adapter_up_weight,
    row_adapter_index,
    adapter_store_slot,
    lengths,
    key_value_cache,
):
    tensor_count = lax.axis_size("tensor")
    tensor_pos = lax.axis_index("tensor")
    store_pos = lax.axis_index("store")
    _, rows, span = hidden.shape
    model_width = input_norm_scale.shape[0]
    rows_here = lengths.shape[0]
    unit = min(RUN, rows_here)
    line = tensor_count == 4 and rows_here % (HALVES * RUN) == 0
    halves = HALVES if line else 1
    part_rows = rows_here // halves
    local = STEPS * part_rows
    held_slots = adapter_down_weight.shape[0]
    rank = adapter_down_weight.shape[2]

    raw = hidden.reshape(STEPS, tensor_count, halves, part_rows // unit, unit, span)
    raw = raw.transpose(2, 1, 3, 0, 4, 5).reshape(STEPS * rows, span)
    own_index = tensor_pos.reshape(1).astype(jnp.int32)
    owners = [own_index] + [hop_owners(tensor_pos, hop) for hop in (1, 2, 3)]
    count = tensor_count * local
    parts = [slice(h * count, (h + 1) * count) for h in range(halves)]
    values = raw.astype(F32)
    squares = jnp.sum(values * values, axis=1)
    if line:
        squares = squares + sum(swap(squares, "tensor", d) for d in (1, 2, 3))
        travelling, squares = lax.optimization_barrier((raw, squares))
        hop1 = line_hop(travelling, travelling, "tensor", 1)
    else:
        squares = summed_over(squares, "tensor")
    own_runs = row_adapter_index[::RUN]
    if halves > 1:
        own_runs = own_runs.reshape(tensor_count, halves, -1).swapaxes(0, 1).reshape(-1)
    told = jnp.concatenate([squares, own_runs.astype(F32)]).reshape(1, -1)
    told = jnp.concatenate([told, swap(told, "store", 2)], axis=0)
    if line:
        told, hop1 = lax.optimization_barrier((told, hop1))
        hop2 = line_hop(*hop1, "tensor", 2)
    told = jnp.concatenate([told, swap(told, "store", 1)], axis=0)
    told = jnp.stack([told[d] for d in (0, 2, 1, 3)])
    told = jnp.stack([jnp.stack([told[p ^ q] for q in range(4)]) for p in range(4)])
    told = lax.dynamic_index_in_dim(told, store_pos, 0, keepdims=False)
    runs = told[:, STEPS * rows :].astype(jnp.int32)
    told = told[:, : STEPS * rows]
    scales = lax.rsqrt(told / model_width + eps_norm)
    slots = lookup(runs.reshape(-1), adapter_store_slot).reshape(runs.shape)
    slots = jnp.where(slots // held_slots == store_pos, slots % held_slots, -1)
    place = store_pos.reshape(1).astype(jnp.int32)
    gains = input_norm_scale.reshape(1, -1)
    gain = lax.dynamic_slice_in_dim(gains, tensor_pos * span, span, 1)
    scales = scales[:, :, None]
    own_scale = lax.dynamic_index_in_dim(scales, store_pos, 0, keepdims=False)

    across = swap(raw, "store", 2)
    beside = swap(raw, "store", 1)
    diagonal = swap(across, "store", 1)
    mine = slots.reshape(-1)
    down = jnp.swapaxes(adapter_down_weight, 1, 2)
    kept, passed = shrink_rows(place, mine, (raw, beside, across, diagonal), scales, gain, down)
    kept = kept + swap(passed, "store", 1)
    shrunk = kept[0] + swap(kept[1], "store", 2)
    if line:
        shrunk = shrunk + swap(shrunk, "tensor", 1)
        shrunk, hop2 = lax.optimization_barrier((shrunk, hop2))
        shrunk = shrunk + swap(shrunk, "tensor", 2)
        shrunk, sent = lax.optimization_barrier((shrunk, hop2))
        hop3 = [line_hop(sent[0][part], sent[1][part], "tensor", 3) for part in parts]
    else:
        shrunk = summed_over(shrunk, "tensor")
    shrunk = shrunk.astype(BF16)
    shrunk = jnp.stack([shrunk, swap(shrunk, "store", 2)])
    other = swap(shrunk, "store", 1)
    kept, *passed = grow_rows(place, mine, shrunk, other, adapter_up_weight, 1)
    if line:
        passed, hop3[0] = lax.optimization_barrier((passed, hop3[0]))
    passed = [swap(piece, "store", 1) for piece in passed]
    leaving = [(kept[1, part] + passed[1][part]).astype(F16) for part in parts]
    arrived = [swap(piece, "store", 2).astype(F32) for piece in leaving]
    deltas = [(kept[0, p] + passed[0][p]) + far for p, far in zip(parts, arrived)]

    weight = query_key_value_weight
    mixed = []
    if line:
        raw, leaving = lax.optimization_barrier((raw, leaving))
        spots = jnp.concatenate(owners)
        for h, part in enumerate(parts):
            if mixed:
                spots, mixed[-1] = lax.optimization_barrier((spots, mixed[-1]))
            blocks = (raw,) + hop1 + hop2 + hop3[h]
            first_rows = (h * count,) * 5 + (0, 0)
            total = base_block(blocks, own_scale[part], gains, weight, spots, first_rows, 4)
            mixed.append((total + deltas[h]).astype(BF16))
    else:
        everything = lax.all_gather(raw, "tensor", axis=0, tiled=False)
        own = base_block((raw,), own_scale, gains, weight, own_index)
        total = base_rows(own_index, everything, own_scale, gains, own, weight, 0)
        mixed.append((total + deltas[0]).astype(BF16))
    mixed = [qkv.reshape(tensor_count, local, -1) for qkv in mixed]

    contexts = []
    exchanged = []
    for qkv in mixed:
        if exchanged:
            qkv, exchanged[-1] = lax.optimization_barrier((qkv, exchanged[-1]))
        exchanged.append(lax.all_to_all(qkv, "tensor", 0, 0, tiled=True))
    for h, moved in enumerate(exchanged):
        if tensor_count != 4:
            q_columns = HEADS * HD // tensor_count
            pieces = []
            for piece in (moved[..., :q_columns], moved[..., q_columns:]):
                joined = piece.transpose(1, 0, 2).reshape(local, 4, -1)
                pieces.append(joined.transpose(1, 0, 2))
            moved = jnp.concatenate(pieces, axis=2)
        here = lengths[h * part_rows : (h + 1) * part_rows]
        cosine, sine = angle_tables(here, unit)
        contexts.append(
            attend(here, ascending(here), moved, cosine, sine, key_value_cache, h * part_rows, unit)
        )

    if line:
        hops = [line_gather(context, "tensor") for context in contexts]
        first = [(context,) + hop[0] for context, hop in zip(contexts, hops)]
        last = [hop[1] + hop[2] for hop in hops]
        output = project(jnp.concatenate(owners[:2]), first, output_weight, 3)
        output = project(jnp.concatenate(owners[2:]), last, output_weight, 2, output)
    else:
        results = []
        for context in contexts:
            context = lax.all_gather(context, "tensor", axis=0, tiled=True)
            result = jnp.dot(context, output_weight, preferred_element_type=F32).astype(BF16)
            result = result.reshape(tensor_count, part_rows // unit, STEPS, unit, -1)
            result = result.transpose(2, 0, 1, 3, 4).reshape(STEPS, tensor_count, part_rows, -1)
            results.append(result)
        output = jnp.stack(results, axis=2)
    return output.reshape(STEPS, rows, -1)


def solution(mesh):
    in_specs = (
        P(None, ("groups", "store"), "tensor"),
        P(),
        P(None, "tensor"),
        P(None, "tensor"),
        P(("groups", "store"), "tensor", None),
        P(("groups", "store"), None, "tensor"),
        P(("groups", "store")),
        P("groups"),
        P(("groups", "store", "tensor")),
        P(("groups", "store", "tensor"), None, None, None),
    )
    out_specs = P(None, ("groups", "store"), "tensor")
    return jax.shard_map(
        on_device, mesh=mesh, in_specs=in_specs, out_specs=out_specs, check_vma=False
    )
```

```python
import functools

import jax
import jax.numpy as jnp
from jax import lax
from jax.experimental import pallas as pl
from jax.experimental.pallas import tpu as pltpu
from jax.sharding import PartitionSpec as P

HEADS = 32
KVH = 4
HD = 128
GROUP = HEADS // KVH
RUN = 8
STEPS = 2
LANES = 128
HALVES = 2

eps_norm = 1e-05
rope_base = 500000.0
masked = -1e30

MIB = 1 << 20
F32 = jnp.float32
BF16 = jnp.bfloat16
F16 = jnp.float16
VMEM = pl.BlockSpec(memory_space=pltpu.VMEM)
SMEM = pl.BlockSpec(memory_space=pltpu.SMEM)
HBM = pl.BlockSpec(memory_space=pltpu.HBM)


def swap(values, axis, distance):
    count = lax.axis_size(axis)
    return lax.ppermute(values, axis, [(i, i ^ distance) for i in range(count)])


def summed_over(values, axis):
    distance = 1
    while distance < lax.axis_size(axis):
        values = values + swap(values, axis, distance)
        distance *= 2
    return values


def line_hop(up, down, axis, hop):
    up = lax.ppermute(up, axis, [(i, i + 1) for i in range(hop - 1, 3)])
    down = lax.ppermute(down, axis, [(i, i - 1) for i in range(4 - hop, 0, -1)])
    return up, down


def line_gather(block, axis):
    hops = [line_hop(block, block, axis, 1)]
    for hop in (2, 3):
        hops.append(line_hop(*hops[-1], axis, hop))
    return hops


def hop_owners(position, hop):
    below = position - hop
    above = position + hop
    return jnp.stack([jnp.where(below >= 0, below, -1), jnp.where(above < 4, above, -1)])


def block_kernel(first_rows, has_total, owners, *refs):
    count = len(first_rows)
    x_refs = refs[:count]
    scale_ref, gain_ref, w_ref = refs[count : count + 3]
    out_ref, held_x, held, x_sems, sems = refs[-5:]
    rows = scale_ref.shape[0]
    _, tiles, depth, _ = held.shape

    def slot(j):
        used = jnp.int32(0)
        for i in range(j):
            used = used + (owners[i] >= 0).astype(jnp.int32)
        return used

    def copy(j, k):
        first = pl.multiple_of((owners[j] * tiles + k) * depth, depth)
        return pltpu.make_async_copy(
            w_ref.at[pl.ds(first, depth), :], held.at[slot(j), k], sems.at[slot(j), k]
        )

    def x_copy(j):
        part = x_refs[j].at[first_rows[j] : first_rows[j] + rows, :]
        return pltpu.make_async_copy(part, held_x.at[slot(j)], x_sems.at[slot(j)])

    for j in range(count):

        @pl.when(owners[j] >= 0)
        def _():
            x_copy(j).start()
            for k in range(tiles):
                copy(j, k).start()

    out_ref[...] = refs[count + 3][...] if has_total else jnp.zeros_like(out_ref)
    for j in range(count):

        @pl.when(owners[j] >= 0)
        def _():
            scale = scale_ref[...]
            x_copy(j).wait()
            for k in range(tiles):
                span = slice(k * depth, (k + 1) * depth)
                first = pl.multiple_of((owners[j] * tiles + k) * depth, depth)
                gain = gain_ref[:, pl.ds(first, depth)]
                part = held_x[slot(j), :, span].astype(F32)
                normed = (part * scale * gain).astype(BF16)
                copy(j, k).wait()
                out_ref[...] += jnp.dot(normed, held[slot(j), k], preferred_element_type=F32)


def base_block(blocks, scale, gain, weight, owners, first_rows, present, total=None):
    depth = blocks[0].shape[1]
    rows = scale.shape[0]
    columns = weight.shape[1]
    tile = min(512, depth)
    count = len(blocks)
    more = [] if total is None else [total]
    return pl.pallas_call(
        functools.partial(block_kernel, first_rows, total is not None),
        out_shape=jax.ShapeDtypeStruct((rows, columns), F32),
        in_specs=[SMEM] + [HBM] * count + [VMEM] * 2 + [HBM] + [VMEM] * len(more),
        out_specs=VMEM,
        scratch_shapes=[
            pltpu.VMEM((present, rows, depth), BF16),
            pltpu.VMEM((present, depth // tile, tile, columns), BF16),
            pltpu.SemaphoreType.DMA((present,)),
            pltpu.SemaphoreType.DMA((present, depth // tile)),
        ],
        compiler_params=pltpu.CompilerParams(vmem_limit_bytes=46 * MIB),
        cost_estimate=pl.CostEstimate(
            flops=rows * columns,
            bytes_accessed=rows * columns,
            transcendentals=0,
        ),
        name="base_block",
    )(owners, *blocks, scale, gain, weight, *more)


def base_kernel(first_row, place_ref, x_ref, scale_ref, gain_ref, own_ref, w_ref, out_ref, held, sems):
    owners, _, span = x_ref.shape
    rows = scale_ref.shape[0]
    tiles, depth, _ = held.shape
    tiles_each = span // depth

    def spot(k):
        owner = lax.rem(place_ref[0] + 1 + k // tiles_each, owners)
        return owner, pl.multiple_of((owner * tiles_each + k % tiles_each) * depth, depth)

    copies = [
        pltpu.make_async_copy(w_ref.at[pl.ds(spot(k)[1], depth), :], held.at[k], sems.at[k])
        for k in range(tiles)
    ]
    for copy in copies:
        copy.start()
    scale = scale_ref[...]
    out_ref[...] = own_ref[first_row : first_row + rows, :]
    for k, copy in enumerate(copies):
        owner, first = spot(k)
        inner = (k % tiles_each) * depth
        gain = gain_ref[:, pl.ds(first, depth)]
        part = x_ref[owner, first_row : first_row + rows, inner : inner + depth].astype(F32)
        normed = (part * scale * gain).astype(BF16)
        copy.wait()
        out_ref[...] += jnp.dot(normed, held[k], preferred_element_type=F32)


def base_rows(place, x, scale, gain, own, weight, first_row):
    owners, _, span = x.shape
    rows = scale.shape[0]
    columns = weight.shape[1]
    tile = min(512, span)
    tiles = (owners - 1) * span // tile
    return pl.pallas_call(
        functools.partial(base_kernel, first_row),
        out_shape=jax.ShapeDtypeStruct((rows, columns), F32),
        in_specs=[SMEM] + [VMEM] * 4 + [HBM],
        out_specs=VMEM,
        scratch_shapes=[
            pltpu.VMEM((tiles, tile, columns), BF16),
            pltpu.SemaphoreType.DMA((tiles,)),
        ],
        compiler_params=pltpu.CompilerParams(vmem_limit_bytes=48 * MIB),
        cost_estimate=pl.CostEstimate(
            flops=2 * rows * tiles * tile * columns,
            bytes_accessed=2 * tiles * tile * (rows + columns) + 8 * rows * columns,
            transcendentals=0,
        ),
        name="base_rows",
    )(place, x, scale, gain, own, weight)


TEAM = 4
SLABS = (0, 2, 1, 3)


def list_runs(place_ref, slots, runs, jobs, start):
    def look(run, carry, slab, d):
        slot = slots[(place_ref[0] ^ d) * runs + run]

        @pl.when(slot >= 0)
        def _():
            jobs[carry] = slab * runs + run
            start(carry, d, run, slot)

        return carry + (slot >= 0).astype(jnp.int32)

    count = jnp.int32(0)
    for slab, d in enumerate(SLABS):
        count = lax.fori_loop(0, runs, functools.partial(look, slab=slab, d=d), count)
    return count


def work_in_teams(count, wait, work):
    def team(g, carry):
        for u in range(TEAM):

            @pl.when(g * TEAM + u < count)
            def _():
                wait(g * TEAM + u)

        work([jnp.minimum(g * TEAM + u, count - 1) for u in range(TEAM)])
        return carry

    lax.fori_loop(0, (count + TEAM - 1) // TEAM, team, 0)


def shrink_kernel(
    place_ref,
    slots,
    x0,
    x1,
    x2,
    x3,
    scale_ref,
    gain_ref,
    down_ref,
    keep_ref,
    send_ref,
    jobs,
    parts,
    held_x,
    held,
    x_sems,
    sems,
):
    runs = held.shape[0] // 4
    rank = held.shape[1]
    x_refs = (x0, x1, x2, x3)

    def x_copy(i, d, run):
        rows = pl.ds(pl.multiple_of(run * 16, 16), 16)
        return pltpu.make_async_copy(x_refs[d].at[rows, :], held_x.at[i], x_sems.at[i])

    def copy(i, slot):
        return pltpu.make_async_copy(down_ref.at[slot], held.at[i], sems.at[i])

    def start(i, d, run, slot):
        copy(i, slot).start()
        x_copy(i, d, run).start()

    def wait(i):
        copy(i, 0).wait()
        x_copy(i, 0, 0).wait()

    def work(members):
        results = []
        for i in members:
            job = jobs[i]
            slab = job // runs
            d = jnp.where(slab == 1, 2, jnp.where(slab == 2, 1, slab))
            rows = pl.ds(pl.multiple_of((job % runs) * 16, 16), 16)
            scale = scale_ref[place_ref[0] ^ d, rows, :]
            normed = (held_x[i].astype(F32) * scale * gain_ref[...]).astype(BF16)
            part = lax.dot_general(
                normed, held[i], (((1,), (1,)), ((), ())), preferred_element_type=F32
            )
            results.append((job, part))
        for job, part in results:
            parts[job] = part

    count = list_runs(place_ref, slots, runs, jobs, start)
    parts[...] = jnp.zeros_like(parts)
    work_in_teams(count, wait, work)
    for slab in range(4):
        for i in range(runs // 2):
            low = slab * runs + i
            out_ref = (keep_ref, send_ref)[slab // 2]
            out_ref[slab % 2, i * 16 : (i + 1) * 16, :] = jnp.concatenate(
                [parts[low], parts[low + runs // 2]], axis=1
            )


def shrink_rows(place, slots, blocks, scales, gain, down):
    rows, depth = blocks[0].shape
    rank = down.shape[1]
    runs = rows // 16
    return pl.pallas_call(
        shrink_kernel,
        out_shape=[jax.ShapeDtypeStruct((2, rows // 2, 2 * rank), F32)] * 2,
        in_specs=[SMEM] * 2 + [HBM] * 4 + [VMEM] * 2 + [HBM],
        out_specs=[VMEM] * 2,
        scratch_shapes=[
            pltpu.SMEM((4 * runs,), jnp.int32),
            pltpu.VMEM((4 * runs, 16, rank), F32),
            pltpu.VMEM((4 * runs, 16, depth), BF16),
            pltpu.VMEM((4 * runs, rank, depth), BF16),
            pltpu.SemaphoreType.DMA((4 * runs,)),
            pltpu.SemaphoreType.DMA((4 * runs,)),
        ],
        compiler_params=pltpu.CompilerParams(vmem_limit_bytes=54 * MIB),
        cost_estimate=pl.CostEstimate(
            flops=rows * depth,
            bytes_accessed=rows * depth,
            transcendentals=0,
        ),
        name="shrink_rows",
    )(place, slots, *blocks, scales, gain, down)


def grow_kernel(
    place_ref, slots, s0, s1, up_ref, keep_ref, *refs
):
    *sends, jobs, parts, held, sems = refs
    pieces = len(sends) // 2
    piece = keep_ref.shape[1] // pieces
    runs = held.shape[0] // 4
    rank = held.shape[1]

    def copy(i, slot):
        return pltpu.make_async_copy(up_ref.at[slot], held.at[i], sems.at[i])

    def start(i, d, run, slot):
        copy(i, slot).start()

    def wait(i):
        copy(i, 0).wait()

    def work(members):
        results = []
        for i in members:
            job = jobs[i]
            grown = jnp.dot(parts[job], held[i], preferred_element_type=F32)
            results.append((job, grown))
        for job, grown in results:
            rows = pl.ds(pl.multiple_of((job % runs) * 16, 16), 16)
            slab = job // runs

            @pl.when(slab < 2)
            def _():
                keep_ref[slab, rows, :] = grown

            run = job % runs
            inner = pl.ds(pl.multiple_of(lax.rem(run * 16, piece), 16), 16)
            target = (slab - 2) * pieces + (run * 16) // piece
            for i, send_ref in enumerate(sends):

                @pl.when((slab >= 2) & (target == i))
                def _():
                    send_ref[inner, :] = grown

    count = list_runs(place_ref, slots, runs, jobs, start)
    for slab in range(4):
        for i in range(runs // 2):
            low = slab * runs + i
            both = (s0, s1)[slab // 2][slab % 2, i * 16 : (i + 1) * 16, :]
            parts[low] = both[:, :rank]
            parts[low + runs // 2] = both[:, rank:]
    keep_ref[...] = jnp.zeros_like(keep_ref)
    for send_ref in sends:
        send_ref[...] = jnp.zeros_like(send_ref)
    work_in_teams(count, wait, work)


def grow_rows(place, slots, kept, passed, up, pieces):
    _, pair_rows, _ = kept.shape
    rows = 2 * pair_rows
    rank, columns = up.shape[1:]
    runs = rows // 16
    return pl.pallas_call(
        grow_kernel,
        out_shape=[jax.ShapeDtypeStruct((2, rows, columns), F32)]
        + [jax.ShapeDtypeStruct((rows // pieces, columns), F32)] * (2 * pieces),
        in_specs=[SMEM, SMEM, VMEM, VMEM, HBM],
        out_specs=[VMEM] * (1 + 2 * pieces),
        scratch_shapes=[
            pltpu.SMEM((4 * runs,), jnp.int32),
            pltpu.VMEM((4 * runs, 16, rank), BF16),
            pltpu.VMEM((4 * runs, rank, columns), BF16),
            pltpu.SemaphoreType.DMA((4 * runs,)),
        ],
        compiler_params=pltpu.CompilerParams(vmem_limit_bytes=60 * MIB),
        cost_estimate=pl.CostEstimate(
            flops=rows * columns,
            bytes_accessed=rows * columns,
            transcendentals=0,
        ),
        name="grow_rows",
    )(place, slots, kept, passed, up)


def attend_kernel(
    unit,
    first_row,
    lengths,
    order,
    qkv_ref,
    cos_ref,
    sin_ref,
    cache_ref,
    out_ref,
    queries,
    keys,
    values,
    context,
    held,
    sems,
):
    rows, _, cached, _ = held.shape
    local = STEPS * rows
    q_columns = GROUP * HD
    part = cached // 2
    scale = HD ** (-0.5)
    team = min(4, rows)

    def copy(r, b):
        span = pl.ds(b * part, part)
        return pltpu.make_async_copy(
            cache_ref.at[first_row + r, :, span, :], held.at[r, :, span, :], sems.at[r, b]
        )

    def longest(group):
        return lengths[order[group * team + team - 1]]

    def fetch(i, carry):
        r = order[i]
        copy(r, 0).start()

        @pl.when(longest(i // team) > part)
        def _():
            copy(r, 1).start()

        return carry

    lax.fori_loop(0, rows, fetch, 0)

    cosine = cos_ref[...]
    sine = sin_ref[...]

    def rotated(x):
        x = x.astype(F32)
        turned = x * cosine + pltpu.roll(x, HD // 2, 1) * sine
        return turned.astype(BF16).astype(F32)

    for k in range(KVH):
        for g in range(GROUP):
            queries[k, g * local : (g + 1) * local, :] = rotated(
                qkv_ref[k, :, g * HD : (g + 1) * HD]
            )
        place = q_columns + (k % 2) * HD
        keys[k] = rotated(qkv_ref[k // 2, :, place : place + HD])
        values[k] = qkv_ref[2 + k // 2, :, place : place + HD].astype(F32)

    early = lax.broadcasted_iota(jnp.int32, (4 * GROUP, 1), 0) % (2 * GROUP) < GROUP

    def scores(r, at, pair, span, live):
        heads = (2 * pair, 2 * pair + 1)
        query = [
            jnp.concatenate(
                [queries[k, pl.ds(at[s], GROUP, stride=local), :] for s in range(STEPS)], axis=0
            )
            for k in heads
        ]
        blank = jnp.zeros((2 * GROUP, HD), F32)
        spread = jnp.concatenate(
            [
                jnp.concatenate([query[0], blank], axis=1),
                jnp.concatenate([blank, query[1]], axis=1),
            ],
            axis=0,
        ).astype(BF16)
        old_keys = jnp.concatenate([held[r, k, :span, :HD] for k in heads], axis=1)
        old = lax.dot_general(
            spread, old_keys, (((1,), (1,)), ((), ())), preferred_element_type=F32
        )
        old = jnp.where(live, old * scale, masked)
        fresh = []
        for t in range(STEPS):
            both = jnp.concatenate(
                [
                    jnp.sum(query[i] * keys[k, pl.ds(at[t], 1), :], axis=1, keepdims=True)
                    for i, k in enumerate(heads)
                ],
                axis=0,
            )
            fresh.append(both * scale)
        fresh[1] = jnp.where(early, masked, fresh[1])
        return old, fresh

    def soften(old, fresh):
        peak = jnp.maximum(jnp.max(old, axis=1, keepdims=True), jnp.maximum(fresh[0], fresh[1]))
        p_old = jnp.exp(old - peak)
        p_new = [jnp.exp(f - peak) for f in fresh]
        total = jnp.sum(p_old, axis=1, keepdims=True) + (p_new[0] + p_new[1])
        return p_old.astype(BF16), [p.astype(BF16).astype(F32) for p in p_new], total

    def mix(r, at, pair, span, w_old, w_new, total):
        heads = (2 * pair, 2 * pair + 1)
        old_values = jnp.concatenate([held[r, k, :span, HD:] for k in heads], axis=1)
        mixed = jnp.dot(w_old, old_values, preferred_element_type=F32)
        for i, k in enumerate(heads):
            own = slice(i * 2 * GROUP, (i + 1) * 2 * GROUP)
            result = mixed[own, i * HD : (i + 1) * HD]
            for t in range(STEPS):
                result = result + w_new[t][own] * values[k, pl.ds(at[t], 1), :]
            result = result / total[own]
            for s in range(STEPS):
                context[k, pl.ds(at[s], GROUP, stride=local), :] = result[
                    s * GROUP : (s + 1) * GROUP
                ]

    def attend_team(members, span):
        jobs = []
        for r in members:
            at = [(r // unit) * (STEPS * unit) + s * unit + r % unit for s in range(STEPS)]
            live = lax.broadcasted_iota(jnp.int32, (4 * GROUP, span), 1) < lengths[r]
            for pair in range(KVH // 2):
                jobs.append((r, at, pair, scores(r, at, pair, span, live)))
        softened = [soften(*job[3]) for job in jobs]
        for (r, at, pair, _), weights in zip(jobs, softened):
            mix(r, at, pair, span, *weights)

    def each(group, carry):
        members = [order[group * team + i] for i in range(team)]
        wide = longest(group) > part
        for r in members:
            copy(r, 0).wait()

        @pl.when(wide)
        def _():
            for r in members:
                copy(r, 1).wait()
            attend_team(members, cached)

        @pl.when(jnp.logical_not(wide))
        def _():
            attend_team(members, part)

        return carry

    lax.fori_loop(0, rows // team, each, 0)
    for k in range(KVH):
        for g in range(GROUP):
            place = (k * GROUP + g) * HD
            out_ref[:, place : place + HD] = context[k, g * local : (g + 1) * local, :].astype(BF16)


def attend(lengths, order, qkv, cosine, sine, cache, first_row, unit):
    rows = lengths.shape[0]
    local = STEPS * rows
    _, kv_heads, cached, width = cache.shape
    return pl.pallas_call(
        functools.partial(attend_kernel, unit, first_row),
        out_shape=jax.ShapeDtypeStruct((local, HEADS * HD), BF16),
        in_specs=[SMEM, SMEM, VMEM, VMEM, VMEM, HBM],
        out_specs=VMEM,
        scratch_shapes=[
            pltpu.VMEM((KVH, GROUP * local, HD), F32),
            pltpu.VMEM((KVH, local, HD), F32),
            pltpu.VMEM((KVH, local, HD), F32),
            pltpu.VMEM((KVH, GROUP * local, HD), F32),
            pltpu.VMEM((rows, kv_heads, cached, width), BF16),
            pltpu.SemaphoreType.DMA((rows, 2)),
        ],
        compiler_params=pltpu.CompilerParams(vmem_limit_bytes=48 * MIB),
        cost_estimate=pl.CostEstimate(
            flops=4 * local * HEADS * HD * cached,
            bytes_accessed=2 * rows * kv_heads * cached * width,
            transcendentals=local * HEADS * cached,
        ),
        name="attend",
    )(lengths, order, qkv, cosine, sine, cache)


def out_kernel(count, has_earlier, owners, *refs):
    blocks = refs[:count]
    w_ref = refs[count]
    out_ref, lhs, total, held, sems = refs[-5:]
    local = blocks[0].shape[0]
    rows = local // STEPS
    tiles, depth, columns = held.shape
    halves = out_ref.shape[2]
    copies = [
        pltpu.make_async_copy(w_ref.at[pl.ds(k * depth, depth), :], held.at[k], sems.at[k])
        for k in range(tiles)
    ]
    for copy in copies:
        copy.start()
    slots = count // halves

    def place(j):
        used = jnp.int32(0)
        for i in range(j % slots):
            used = used + (owners[i] >= 0).astype(jnp.int32)
        return (j // slots) * (lhs.shape[0] // halves) + used * local

    lhs[...] = jnp.zeros_like(lhs)
    for j, ref in enumerate(blocks):

        @pl.when(owners[j % slots] >= 0)
        def _():
            lhs[pl.ds(pl.multiple_of(place(j), local), local), :] = ref[...]

    if has_earlier:
        out_ref[...] = refs[count + 1][...]
    width = min(512, columns)
    for k, copy in enumerate(copies):
        copy.wait()
        for j in range(columns // width):
            span = slice(j * width, (j + 1) * width)
            product = jnp.dot(
                lhs[:, k * depth : (k + 1) * depth], held[k, :, span], preferred_element_type=F32
            )
            if k > 0:
                product = total[:, span] + product
            total[:, span] = product
    for j in range(count):

        @pl.when(owners[j % slots] >= 0)
        def _():
            block = total[pl.ds(pl.multiple_of(place(j), local), local), :]
            block = block.reshape(rows // RUN, STEPS, RUN, columns)
            for s in range(STEPS):
                piece = block[:, s].reshape(rows, columns).astype(BF16)
                out_ref[s, owners[j % slots], j // slots] = piece


def project(owners, blocks, weight, present, earlier=None):
    halves = len(blocks)
    flat = [block for part in blocks for block in part]
    local, depth = flat[0].shape
    columns = weight.shape[1]
    tile = min(512, depth)
    rows = local // STEPS
    count = len(flat)
    more = [] if earlier is None else [earlier]
    return pl.pallas_call(
        functools.partial(out_kernel, count, earlier is not None),
        out_shape=jax.ShapeDtypeStruct((STEPS, 4, halves, rows, columns), BF16),
        in_specs=[SMEM] + [VMEM] * count + [HBM] + [VMEM] * len(more),
        out_specs=VMEM,
        scratch_shapes=[
            pltpu.VMEM((present * halves * local, depth), BF16),
            pltpu.VMEM((present * halves * local, columns), F32),
            pltpu.VMEM((depth // tile, tile, columns), BF16),
            pltpu.SemaphoreType.DMA((depth // tile,)),
        ],
        compiler_params=pltpu.CompilerParams(vmem_limit_bytes=52 * MIB),
        cost_estimate=pl.CostEstimate(
            flops=2 * present * halves * local * depth * columns,
            bytes_accessed=2 * depth * columns + 4 * present * local * (depth + columns),
            transcendentals=0,
        ),
        name="project",
    )(owners, *flat, weight, *more)


def lookup(identity, table):
    hits = identity[:, None] == jnp.arange(table.shape[0], dtype=jnp.int32)[None, :]
    return jnp.sum(jnp.where(hits, table[None, :], 0), axis=1)


def ascending(lengths):
    count = lengths.shape[0]
    rows = jnp.arange(count, dtype=jnp.int32)
    keyed = lengths * count + rows
    rank = jnp.sum((keyed[None, :] < keyed[:, None]).astype(jnp.int32), axis=1)
    return jnp.sum(jnp.where(rank[:, None] == rows[None, :], rows[:, None], 0), axis=0)


def angle_tables(lengths, unit):
    steps = jnp.arange(STEPS, dtype=jnp.int32)
    position = lengths.reshape(-1, 1, unit) + steps[None, :, None]
    freq = rope_base ** (-(jnp.arange(HD // 2, dtype=F32) * 2.0 / HD))
    angles = position.reshape(-1).astype(F32)[:, None] * freq
    cosine = jnp.cos(angles)
    sine = jnp.sin(angles)
    return jnp.concatenate([cosine, cosine], 1), jnp.concatenate([-sine, sine], 1)


def on_device(
    hidden,
    input_norm_scale,
    query_key_value_weight,
    output_weight,
    adapter_down_weight,
    adapter_up_weight,
    row_adapter_index,
    adapter_store_slot,
    lengths,
    key_value_cache,
):
    tensor_count = lax.axis_size("tensor")
    tensor_pos = lax.axis_index("tensor")
    store_pos = lax.axis_index("store")
    _, rows, span = hidden.shape
    model_width = input_norm_scale.shape[0]
    rows_here = lengths.shape[0]
    unit = min(RUN, rows_here)
    line = tensor_count == 4 and rows_here % (HALVES * RUN) == 0
    halves = HALVES if line else 1
    part_rows = rows_here // halves
    local = STEPS * part_rows
    held_slots = adapter_down_weight.shape[0]
    rank = adapter_down_weight.shape[2]

    raw = hidden.reshape(STEPS, tensor_count, halves, part_rows // unit, unit, span)
    raw = raw.transpose(2, 1, 3, 0, 4, 5).reshape(STEPS * rows, span)
    own_index = tensor_pos.reshape(1).astype(jnp.int32)
    owners = [own_index] + [hop_owners(tensor_pos, hop) for hop in (1, 2, 3)]
    count = tensor_count * local
    parts = [slice(h * count, (h + 1) * count) for h in range(halves)]
    values = raw.astype(F32)
    squares = jnp.sum(values * values, axis=1)
    if line:
        squares = squares + sum(swap(squares, "tensor", d) for d in (1, 2, 3))
        travelling, squares = lax.optimization_barrier((raw, squares))
        hop1 = line_hop(travelling, travelling, "tensor", 1)
    else:
        squares = summed_over(squares, "tensor")
    own_runs = row_adapter_index[::RUN]
    if halves > 1:
        own_runs = own_runs.reshape(tensor_count, halves, -1).swapaxes(0, 1).reshape(-1)
    told = jnp.concatenate([squares, own_runs.astype(F32)]).reshape(1, -1)
    told = jnp.concatenate([told, swap(told, "store", 2)], axis=0)
    if line:
        told, hop1 = lax.optimization_barrier((told, hop1))
        hop2 = line_hop(*hop1, "tensor", 2)
    told = jnp.concatenate([told, swap(told, "store", 1)], axis=0)
    told = jnp.stack([told[d] for d in (0, 2, 1, 3)])
    told = jnp.stack([jnp.stack([told[p ^ q] for q in range(4)]) for p in range(4)])
    told = lax.dynamic_index_in_dim(told, store_pos, 0, keepdims=False)
    runs = told[:, STEPS * rows :].astype(jnp.int32)
    told = told[:, : STEPS * rows]
    scales = lax.rsqrt(told / model_width + eps_norm)
    slots = lookup(runs.reshape(-1), adapter_store_slot).reshape(runs.shape)
    slots = jnp.where(slots // held_slots == store_pos, slots % held_slots, -1)
    place = store_pos.reshape(1).astype(jnp.int32)
    gains = input_norm_scale.reshape(1, -1)
    gain = lax.dynamic_slice_in_dim(gains, tensor_pos * span, span, 1)
    scales = scales[:, :, None]
    own_scale = lax.dynamic_index_in_dim(scales, store_pos, 0, keepdims=False)

    across = swap(raw, "store", 2)
    beside = swap(raw, "store", 1)
    diagonal = swap(across, "store", 1)
    mine = slots.reshape(-1)
    down = jnp.swapaxes(adapter_down_weight, 1, 2)
    kept, passed = shrink_rows(place, mine, (raw, beside, across, diagonal), scales, gain, down)
    kept = kept + swap(passed, "store", 1)
    shrunk = kept[0] + swap(kept[1], "store", 2)
    if line:
        shrunk, early = lax.optimization_barrier((shrunk, (raw,) + hop1))
        near = jnp.concatenate(owners[:2])
        total = base_block(early, own_scale, gains, query_key_value_weight, near, (0,) * 3, 3)
        shrunk = shrunk + swap(shrunk, "tensor", 1)
        shrunk, total, hop2 = lax.optimization_barrier((shrunk, total, hop2))
        sent = [(hop2[0][part], hop2[1][part]) for part in parts]
        shrunk = shrunk + swap(shrunk, "tensor", 2)
        shrunk, sent = lax.optimization_barrier((shrunk, sent))
        hop3 = [line_hop(up, down, "tensor", 3) for up, down in sent]
    else:
        shrunk = summed_over(shrunk, "tensor")
    shrunk = shrunk.astype(BF16)
    shrunk = jnp.stack([shrunk, swap(shrunk, "store", 2)])
    other = swap(shrunk, "store", 1)
    kept, *passed = grow_rows(place, mine, shrunk, other, adapter_up_weight, 1)
    if line:
        passed, hop3[0] = lax.optimization_barrier((passed, hop3[0]))
    passed = [swap(piece, "store", 1) for piece in passed]
    leaving = [(kept[1, part] + passed[1][part]).astype(F16) for part in parts]
    arrived = [swap(piece, "store", 2).astype(F32) for piece in leaving]
    deltas = [(kept[0, p] + passed[0][p]) + far for p, far in zip(parts, arrived)]

    weight = query_key_value_weight
    mixed = []
    if line:
        total, leaving = lax.optimization_barrier((total, leaving))
        far = jnp.concatenate(owners[2:])
        for h, part in enumerate(parts):
            if mixed:
                far, mixed[-1] = lax.optimization_barrier((far, mixed[-1]))
            blocks = hop2 + hop3[h]
            first_rows = (h * count, h * count, 0, 0)
            sums = base_block(
                blocks, own_scale[part], gains, weight, far, first_rows, 2, total[part]
            )
            mixed.append((sums + deltas[h]).astype(BF16))
    else:
        everything = lax.all_gather(raw, "tensor", axis=0, tiled=False)
        own = base_block((raw,), own_scale, gains, weight, own_index, (0,), 1)
        total = base_rows(own_index, everything, own_scale, gains, own, weight, 0)
        mixed.append((total + deltas[0]).astype(BF16))
    mixed = [qkv.reshape(tensor_count, local, -1) for qkv in mixed]

    contexts = []
    exchanged = []
    for qkv in mixed:
        if exchanged:
            qkv, exchanged[-1] = lax.optimization_barrier((qkv, exchanged[-1]))
        exchanged.append(lax.all_to_all(qkv, "tensor", 0, 0, tiled=True))
    for h, moved in enumerate(exchanged):
        if tensor_count != 4:
            q_columns = HEADS * HD // tensor_count
            pieces = []
            for piece in (moved[..., :q_columns], moved[..., q_columns:]):
                joined = piece.transpose(1, 0, 2).reshape(local, 4, -1)
                pieces.append(joined.transpose(1, 0, 2))
            moved = jnp.concatenate(pieces, axis=2)
        here = lengths[h * part_rows : (h + 1) * part_rows]
        cosine, sine = angle_tables(here, unit)
        contexts.append(
            attend(here, ascending(here), moved, cosine, sine, key_value_cache, h * part_rows, unit)
        )

    if line:
        hops = [line_gather(context, "tensor") for context in contexts]
        first = [(context,) + hop[0] for context, hop in zip(contexts, hops)]
        last = [hop[1] + hop[2] for hop in hops]
        output = project(jnp.concatenate(owners[:2]), first, output_weight, 3)
        output = project(jnp.concatenate(owners[2:]), last, output_weight, 2, output)
    else:
        results = []
        for context in contexts:
            context = lax.all_gather(context, "tensor", axis=0, tiled=True)
            result = jnp.dot(context, output_weight, preferred_element_type=F32).astype(BF16)
            result = result.reshape(tensor_count, part_rows // unit, STEPS, unit, -1)
            result = result.transpose(2, 0, 1, 3, 4).reshape(STEPS, tensor_count, part_rows, -1)
            results.append(result)
        output = jnp.stack(results, axis=2)
    return output.reshape(STEPS, rows, -1)


def solution(mesh):
    in_specs = (
        P(None, ("groups", "store"), "tensor"),
        P(),
        P(None, "tensor"),
        P(None, "tensor"),
        P(("groups", "store"), "tensor", None),
        P(("groups", "store"), None, "tensor"),
        P(("groups", "store")),
        P("groups"),
        P(("groups", "store", "tensor")),
        P(("groups", "store", "tensor"), None, None, None),
    )
    out_specs = P(None, ("groups", "store"), "tensor")
    return jax.shard_map(
        on_device, mesh=mesh, in_specs=in_specs, out_specs=out_specs, check_vma=False
    )
```

```python
import functools

import jax
import jax.numpy as jnp
from jax import lax
from jax.experimental import pallas as pl
from jax.experimental.pallas import tpu as pltpu
from jax.sharding import PartitionSpec as P

HEADS = 32
KVH = 4
HD = 128
GROUP = HEADS // KVH
RUN = 8
STEPS = 2
LANES = 128
HALVES = 2

eps_norm = 1e-05
rope_base = 500000.0
masked = -1e30

MIB = 1 << 20
F32 = jnp.float32
BF16 = jnp.bfloat16
F16 = jnp.float16
VMEM = pl.BlockSpec(memory_space=pltpu.VMEM)
SMEM = pl.BlockSpec(memory_space=pltpu.SMEM)
HBM = pl.BlockSpec(memory_space=pltpu.HBM)
ANY = pl.BlockSpec(memory_space=pl.ANY)


def swap(values, axis, distance):
    count = lax.axis_size(axis)
    return lax.ppermute(values, axis, [(i, i ^ distance) for i in range(count)])


def summed_over(values, axis):
    distance = 1
    while distance < lax.axis_size(axis):
        values = values + swap(values, axis, distance)
        distance *= 2
    return values


def line_hop(up, down, axis, hop):
    up = lax.ppermute(up, axis, [(i, i + 1) for i in range(hop - 1, 3)])
    down = lax.ppermute(down, axis, [(i, i - 1) for i in range(4 - hop, 0, -1)])
    return up, down


def line_gather(block, axis):
    hops = [line_hop(block, block, axis, 1)]
    for hop in (2, 3):
        hops.append(line_hop(*hops[-1], axis, hop))
    return hops


def hop_owners(position, hop):
    below = position - hop
    above = position + hop
    return jnp.stack([jnp.where(below >= 0, below, -1), jnp.where(above < 4, above, -1)])


def block_kernel(first_rows, has_total, owners, *refs):
    count = len(first_rows)
    x_refs = refs[:count]
    scale_ref, gain_ref, w_ref = refs[count : count + 3]
    out_ref, held_x, held, x_sems, sems = refs[-5:]
    rows = scale_ref.shape[0]
    _, tiles, depth, _ = held.shape

    def slot(j):
        used = jnp.int32(0)
        for i in range(j):
            used = used + (owners[i] >= 0).astype(jnp.int32)
        return used

    def copy(j, k):
        first = pl.multiple_of((owners[j] * tiles + k) * depth, depth)
        return pltpu.make_async_copy(
            w_ref.at[pl.ds(first, depth), :], held.at[slot(j), k], sems.at[slot(j), k]
        )

    def x_copy(j):
        part = x_refs[j].at[first_rows[j] : first_rows[j] + rows, :]
        return pltpu.make_async_copy(part, held_x.at[slot(j)], x_sems.at[slot(j)])

    for j in range(count):

        @pl.when(owners[j] >= 0)
        def _():
            x_copy(j).start()
            for k in range(tiles):
                copy(j, k).start()

    out_ref[...] = refs[count + 3][...] if has_total else jnp.zeros_like(out_ref)
    for j in range(count):

        @pl.when(owners[j] >= 0)
        def _():
            scale = scale_ref[...]
            x_copy(j).wait()
            for k in range(tiles):
                span = slice(k * depth, (k + 1) * depth)
                first = pl.multiple_of((owners[j] * tiles + k) * depth, depth)
                gain = gain_ref[:, pl.ds(first, depth)]
                part = held_x[slot(j), :, span].astype(F32)
                normed = (part * scale * gain).astype(BF16)
                copy(j, k).wait()
                out_ref[...] += jnp.dot(normed, held[slot(j), k], preferred_element_type=F32)


def base_block(blocks, scale, gain, weight, owners, first_rows, present, total=None):
    depth = blocks[0].shape[1]
    rows = scale.shape[0]
    columns = weight.shape[1]
    tile = min(512, depth)
    count = len(blocks)
    more = [] if total is None else [total]
    return pl.pallas_call(
        functools.partial(block_kernel, first_rows, total is not None),
        out_shape=jax.ShapeDtypeStruct((rows, columns), F32),
        in_specs=[SMEM] + [ANY] * count + [VMEM] * 2 + [HBM] + [VMEM] * len(more),
        out_specs=VMEM,
        scratch_shapes=[
            pltpu.VMEM((present, rows, depth), BF16),
            pltpu.VMEM((present, depth // tile, tile, columns), BF16),
            pltpu.SemaphoreType.DMA((present,)),
            pltpu.SemaphoreType.DMA((present, depth // tile)),
        ],
        compiler_params=pltpu.CompilerParams(vmem_limit_bytes=46 * MIB),
        cost_estimate=pl.CostEstimate(
            flops=2 * present * rows * depth * columns,
            bytes_accessed=2 * present * depth * (rows + columns) + 4 * rows * columns,
            transcendentals=0,
        ),
        name="base_block",
    )(owners, *blocks, scale, gain, weight, *more)


def base_kernel(first_row, place_ref, x_ref, scale_ref, gain_ref, own_ref, w_ref, out_ref, held, sems):
    owners, _, span = x_ref.shape
    rows = scale_ref.shape[0]
    tiles, depth, _ = held.shape
    tiles_each = span // depth

    def spot(k):
        owner = lax.rem(place_ref[0] + 1 + k // tiles_each, owners)
        return owner, pl.multiple_of((owner * tiles_each + k % tiles_each) * depth, depth)

    copies = [
        pltpu.make_async_copy(w_ref.at[pl.ds(spot(k)[1], depth), :], held.at[k], sems.at[k])
        for k in range(tiles)
    ]
    for copy in copies:
        copy.start()
    scale = scale_ref[...]
    out_ref[...] = own_ref[first_row : first_row + rows, :]
    for k, copy in enumerate(copies):
        owner, first = spot(k)
        inner = (k % tiles_each) * depth
        gain = gain_ref[:, pl.ds(first, depth)]
        part = x_ref[owner, first_row : first_row + rows, inner : inner + depth].astype(F32)
        normed = (part * scale * gain).astype(BF16)
        copy.wait()
        out_ref[...] += jnp.dot(normed, held[k], preferred_element_type=F32)


def base_rows(place, x, scale, gain, own, weight, first_row):
    owners, _, span = x.shape
    rows = scale.shape[0]
    columns = weight.shape[1]
    tile = min(512, span)
    tiles = (owners - 1) * span // tile
    return pl.pallas_call(
        functools.partial(base_kernel, first_row),
        out_shape=jax.ShapeDtypeStruct((rows, columns), F32),
        in_specs=[SMEM] + [VMEM] * 4 + [HBM],
        out_specs=VMEM,
        scratch_shapes=[
            pltpu.VMEM((tiles, tile, columns), BF16),
            pltpu.SemaphoreType.DMA((tiles,)),
        ],
        compiler_params=pltpu.CompilerParams(vmem_limit_bytes=48 * MIB),
        cost_estimate=pl.CostEstimate(
            flops=2 * rows * tiles * tile * columns,
            bytes_accessed=2 * tiles * tile * (rows + columns) + 8 * rows * columns,
            transcendentals=0,
        ),
        name="base_rows",
    )(place, x, scale, gain, own, weight)


TEAM = 4
SLABS = (0, 2, 1, 3)


def list_runs(place_ref, slots, runs, jobs, start):
    def look(run, carry, slab, d):
        slot = slots[(place_ref[0] ^ d) * runs + run]

        @pl.when(slot >= 0)
        def _():
            jobs[carry] = slab * runs + run
            start(carry, d, run, slot)

        return carry + (slot >= 0).astype(jnp.int32)

    count = jnp.int32(0)
    for slab, d in enumerate(SLABS):
        count = lax.fori_loop(0, runs, functools.partial(look, slab=slab, d=d), count)
    return count


def work_in_teams(count, wait, work):
    def team(g, carry):
        for u in range(TEAM):

            @pl.when(g * TEAM + u < count)
            def _():
                wait(g * TEAM + u)

        work([jnp.minimum(g * TEAM + u, count - 1) for u in range(TEAM)])
        return carry

    lax.fori_loop(0, (count + TEAM - 1) // TEAM, team, 0)


def shrink_kernel(
    place_ref,
    slots,
    x0,
    x1,
    x2,
    x3,
    scale_ref,
    gain_ref,
    down_ref,
    keep_ref,
    send_ref,
    jobs,
    parts,
    held_x,
    held,
    x_sems,
    sems,
):
    runs = held.shape[0] // 4
    rank = held.shape[1]
    x_refs = (x0, x1, x2, x3)

    def x_copy(i, d, run):
        rows = pl.ds(pl.multiple_of(run * 16, 16), 16)
        return pltpu.make_async_copy(x_refs[d].at[rows, :], held_x.at[i], x_sems.at[i])

    def copy(i, slot):
        return pltpu.make_async_copy(down_ref.at[slot], held.at[i], sems.at[i])

    def start(i, d, run, slot):
        copy(i, slot).start()
        x_copy(i, d, run).start()

    def wait(i):
        copy(i, 0).wait()
        x_copy(i, 0, 0).wait()

    def work(members):
        results = []
        for i in members:
            job = jobs[i]
            slab = job // runs
            d = jnp.where(slab == 1, 2, jnp.where(slab == 2, 1, slab))
            rows = pl.ds(pl.multiple_of((job % runs) * 16, 16), 16)
            scale = scale_ref[place_ref[0] ^ d, rows, :]
            normed = (held_x[i].astype(F32) * scale * gain_ref[...]).astype(BF16)
            part = lax.dot_general(
                normed, held[i], (((1,), (1,)), ((), ())), preferred_element_type=F32
            )
            results.append((job, part))
        for job, part in results:
            parts[job] = part

    count = list_runs(place_ref, slots, runs, jobs, start)
    parts[...] = jnp.zeros_like(parts)
    work_in_teams(count, wait, work)
    for slab in range(4):
        for i in range(runs // 2):
            low = slab * runs + i
            out_ref = (keep_ref, send_ref)[slab // 2]
            out_ref[slab % 2, i * 16 : (i + 1) * 16, :] = jnp.concatenate(
                [parts[low], parts[low + runs // 2]], axis=1
            )


def shrink_rows(place, slots, blocks, scales, gain, down):
    rows, depth = blocks[0].shape
    rank = down.shape[1]
    runs = rows // 16
    return pl.pallas_call(
        shrink_kernel,
        out_shape=[jax.ShapeDtypeStruct((2, rows // 2, 2 * rank), F32)] * 2,
        in_specs=[SMEM] * 2 + [ANY] * 4 + [VMEM] * 2 + [HBM],
        out_specs=[VMEM] * 2,
        scratch_shapes=[
            pltpu.SMEM((4 * runs,), jnp.int32),
            pltpu.VMEM((4 * runs, 16, rank), F32),
            pltpu.VMEM((4 * runs, 16, depth), BF16),
            pltpu.VMEM((4 * runs, rank, depth), BF16),
            pltpu.SemaphoreType.DMA((4 * runs,)),
            pltpu.SemaphoreType.DMA((4 * runs,)),
        ],
        compiler_params=pltpu.CompilerParams(vmem_limit_bytes=54 * MIB),
        cost_estimate=pl.CostEstimate(
            flops=rows * depth,
            bytes_accessed=rows * depth,
            transcendentals=0,
        ),
        name="shrink_rows",
    )(place, slots, *blocks, scales, gain, down)


def grow_kernel(
    place_ref, slots, s0, s1, up_ref, keep_ref, *refs
):
    *sends, jobs, parts, held, sems = refs
    pieces = len(sends) // 2
    piece = keep_ref.shape[1] // pieces
    runs = held.shape[0] // 4
    rank = held.shape[1]

    def copy(i, slot):
        return pltpu.make_async_copy(up_ref.at[slot], held.at[i], sems.at[i])

    def start(i, d, run, slot):
        copy(i, slot).start()

    def wait(i):
        copy(i, 0).wait()

    def work(members):
        results = []
        for i in members:
            job = jobs[i]
            grown = jnp.dot(parts[job], held[i], preferred_element_type=F32)
            results.append((job, grown))
        for job, grown in results:
            rows = pl.ds(pl.multiple_of((job % runs) * 16, 16), 16)
            slab = job // runs

            @pl.when(slab < 2)
            def _():
                keep_ref[slab, rows, :] = grown

            run = job % runs
            inner = pl.ds(pl.multiple_of(lax.rem(run * 16, piece), 16), 16)
            target = (slab - 2) * pieces + (run * 16) // piece
            for i, send_ref in enumerate(sends):

                @pl.when((slab >= 2) & (target == i))
                def _():
                    send_ref[inner, :] = grown

    count = list_runs(place_ref, slots, runs, jobs, start)
    for slab in range(4):
        for i in range(runs // 2):
            low = slab * runs + i
            both = (s0, s1)[slab // 2][slab % 2, i * 16 : (i + 1) * 16, :]
            parts[low] = both[:, :rank]
            parts[low + runs // 2] = both[:, rank:]
    keep_ref[...] = jnp.zeros_like(keep_ref)
    for send_ref in sends:
        send_ref[...] = jnp.zeros_like(send_ref)
    work_in_teams(count, wait, work)


def grow_rows(place, slots, kept, passed, up, pieces):
    _, pair_rows, _ = kept.shape
    rows = 2 * pair_rows
    rank, columns = up.shape[1:]
    runs = rows // 16
    return pl.pallas_call(
        grow_kernel,
        out_shape=[jax.ShapeDtypeStruct((2, rows, columns), F32)]
        + [jax.ShapeDtypeStruct((rows // pieces, columns), F32)] * (2 * pieces),
        in_specs=[SMEM, SMEM, VMEM, VMEM, HBM],
        out_specs=[VMEM] * (1 + 2 * pieces),
        scratch_shapes=[
            pltpu.SMEM((4 * runs,), jnp.int32),
            pltpu.VMEM((4 * runs, 16, rank), BF16),
            pltpu.VMEM((4 * runs, rank, columns), BF16),
            pltpu.SemaphoreType.DMA((4 * runs,)),
        ],
        compiler_params=pltpu.CompilerParams(vmem_limit_bytes=60 * MIB),
        cost_estimate=pl.CostEstimate(
            flops=rows * columns,
            bytes_accessed=rows * columns,
            transcendentals=0,
        ),
        name="grow_rows",
    )(place, slots, kept, passed, up)


def attend_kernel(
    unit,
    first_row,
    lengths,
    order,
    qkv_ref,
    cos_ref,
    sin_ref,
    cache_ref,
    out_ref,
    queries,
    keys,
    values,
    context,
    held,
    sems,
):
    rows, _, cached, _ = held.shape
    local = STEPS * rows
    q_columns = GROUP * HD
    part = cached // 2
    scale = HD ** (-0.5)
    team = min(4, rows)

    def copy(r, b):
        span = pl.ds(b * part, part)
        return pltpu.make_async_copy(
            cache_ref.at[first_row + r, :, span, :], held.at[r, :, span, :], sems.at[r, b]
        )

    def longest(group):
        return lengths[order[group * team + team - 1]]

    def fetch(i, carry):
        r = order[i]
        copy(r, 0).start()

        @pl.when(longest(i // team) > part)
        def _():
            copy(r, 1).start()

        return carry

    lax.fori_loop(0, rows, fetch, 0)

    cosine = cos_ref[...]
    sine = sin_ref[...]

    def rotated(x):
        x = x.astype(F32)
        turned = x * cosine + pltpu.roll(x, HD // 2, 1) * sine
        return turned.astype(BF16).astype(F32)

    for k in range(KVH):
        for g in range(GROUP):
            queries[k, g * local : (g + 1) * local, :] = rotated(
                qkv_ref[k, :, g * HD : (g + 1) * HD]
            )
        place = q_columns + (k % 2) * HD
        keys[k] = rotated(qkv_ref[k // 2, :, place : place + HD])
        values[k] = qkv_ref[2 + k // 2, :, place : place + HD].astype(F32)

    early = lax.broadcasted_iota(jnp.int32, (4 * GROUP, 1), 0) % (2 * GROUP) < GROUP

    def scores(r, at, pair, span, live):
        heads = (2 * pair, 2 * pair + 1)
        query = [
            jnp.concatenate(
                [queries[k, pl.ds(at[s], GROUP, stride=local), :] for s in range(STEPS)], axis=0
            )
            for k in heads
        ]
        blank = jnp.zeros((2 * GROUP, HD), F32)
        spread = jnp.concatenate(
            [
                jnp.concatenate([query[0], blank], axis=1),
                jnp.concatenate([blank, query[1]], axis=1),
            ],
            axis=0,
        ).astype(BF16)
        old_keys = jnp.concatenate([held[r, k, :span, :HD] for k in heads], axis=1)
        old = lax.dot_general(
            spread, old_keys, (((1,), (1,)), ((), ())), preferred_element_type=F32
        )
        old = jnp.where(live, old * scale, masked)
        fresh = []
        for t in range(STEPS):
            both = jnp.concatenate(
                [
                    jnp.sum(query[i] * keys[k, pl.ds(at[t], 1), :], axis=1, keepdims=True)
                    for i, k in enumerate(heads)
                ],
                axis=0,
            )
            fresh.append(both * scale)
        fresh[1] = jnp.where(early, masked, fresh[1])
        return old, fresh

    def soften(old, fresh):
        peak = jnp.maximum(jnp.max(old, axis=1, keepdims=True), jnp.maximum(fresh[0], fresh[1]))
        p_old = jnp.exp(old - peak)
        p_new = [jnp.exp(f - peak) for f in fresh]
        total = jnp.sum(p_old, axis=1, keepdims=True) + (p_new[0] + p_new[1])
        return p_old.astype(BF16), [p.astype(BF16).astype(F32) for p in p_new], total

    def mix(r, at, pair, span, w_old, w_new, total):
        heads = (2 * pair, 2 * pair + 1)
        old_values = jnp.concatenate([held[r, k, :span, HD:] for k in heads], axis=1)
        mixed = jnp.dot(w_old, old_values, preferred_element_type=F32)
        for i, k in enumerate(heads):
            own = slice(i * 2 * GROUP, (i + 1) * 2 * GROUP)
            result = mixed[own, i * HD : (i + 1) * HD]
            for t in range(STEPS):
                result = result + w_new[t][own] * values[k, pl.ds(at[t], 1), :]
            result = result / total[own]
            for s in range(STEPS):
                context[k, pl.ds(at[s], GROUP, stride=local), :] = result[
                    s * GROUP : (s + 1) * GROUP
                ]

    def attend_team(members, span):
        jobs = []
        for r in members:
            at = [(r // unit) * (STEPS * unit) + s * unit + r % unit for s in range(STEPS)]
            live = lax.broadcasted_iota(jnp.int32, (4 * GROUP, span), 1) < lengths[r]
            for pair in range(KVH // 2):
                jobs.append((r, at, pair, scores(r, at, pair, span, live)))
        softened = [soften(*job[3]) for job in jobs]
        for (r, at, pair, _), weights in zip(jobs, softened):
            mix(r, at, pair, span, *weights)

    def each(group, carry):
        members = [order[group * team + i] for i in range(team)]
        wide = longest(group) > part
        for r in members:
            copy(r, 0).wait()

        @pl.when(wide)
        def _():
            for r in members:
                copy(r, 1).wait()
            attend_team(members, cached)

        @pl.when(jnp.logical_not(wide))
        def _():
            attend_team(members, part)

        return carry

    lax.fori_loop(0, rows // team, each, 0)
    for k in range(KVH):
        for g in range(GROUP):
            place = (k * GROUP + g) * HD
            out_ref[:, place : place + HD] = context[k, g * local : (g + 1) * local, :].astype(BF16)


def attend(lengths, order, qkv, cosine, sine, cache, first_row, unit):
    rows = lengths.shape[0]
    local = STEPS * rows
    _, kv_heads, cached, width = cache.shape
    return pl.pallas_call(
        functools.partial(attend_kernel, unit, first_row),
        out_shape=jax.ShapeDtypeStruct((local, HEADS * HD), BF16),
        in_specs=[SMEM, SMEM, VMEM, VMEM, VMEM, HBM],
        out_specs=VMEM,
        scratch_shapes=[
            pltpu.VMEM((KVH, GROUP * local, HD), F32),
            pltpu.VMEM((KVH, local, HD), F32),
            pltpu.VMEM((KVH, local, HD), F32),
            pltpu.VMEM((KVH, GROUP * local, HD), F32),
            pltpu.VMEM((rows, kv_heads, cached, width), BF16),
            pltpu.SemaphoreType.DMA((rows, 2)),
        ],
        compiler_params=pltpu.CompilerParams(vmem_limit_bytes=28 * MIB),
        cost_estimate=pl.CostEstimate(
            flops=4 * local * HEADS * HD * cached,
            bytes_accessed=2 * rows * kv_heads * cached * width,
            transcendentals=local * HEADS * cached,
        ),
        name="attend",
    )(lengths, order, qkv, cosine, sine, cache)


def out_kernel(count, has_earlier, owners, *refs):
    blocks = refs[:count]
    w_ref = refs[count]
    if has_earlier:
        out_ref, lhs, total = refs[-3:]
    else:
        out_ref, lhs, total, held, sems = refs[-5:]
        tiles, tile, _ = held.shape
        copies = [
            pltpu.make_async_copy(w_ref.at[pl.ds(k * tile, tile), :], held.at[k], sems.at[k])
            for k in range(tiles)
        ]
        for copy in copies:
            copy.start()
    local, depth = blocks[0].shape
    rows = local // STEPS
    columns = w_ref.shape[1]
    halves = out_ref.shape[2]
    slots = count // halves

    def place(j):
        used = jnp.int32(0)
        for i in range(j % slots):
            used = used + (owners[i] >= 0).astype(jnp.int32)
        return (j // slots) * (lhs.shape[0] // halves) + used * local

    lhs[...] = jnp.zeros_like(lhs)
    for j, ref in enumerate(blocks):

        @pl.when(owners[j % slots] >= 0)
        def _():
            lhs[pl.ds(pl.multiple_of(place(j), local), local), :] = ref[...]

    if has_earlier:
        out_ref[...] = refs[count + 1][...]
    width = min(512, columns)
    spans = [slice(j * width, (j + 1) * width) for j in range(columns // width)]
    if has_earlier:
        for span in spans:
            total[:, span] = jnp.dot(lhs[...], w_ref[:, span], preferred_element_type=F32)
    else:
        for k, copy in enumerate(copies):
            copy.wait()
            part = lhs[:, k * tile : (k + 1) * tile]
            for span in spans:
                product = jnp.dot(part, held[k, :, span], preferred_element_type=F32)
                total[:, span] = product if k == 0 else total[:, span] + product
    for j in range(count):

        @pl.when(owners[j % slots] >= 0)
        def _():
            block = total[pl.ds(pl.multiple_of(place(j), local), local), :]
            block = block.reshape(rows // RUN, STEPS, RUN, columns)
            for s in range(STEPS):
                piece = block[:, s].reshape(rows, columns).astype(BF16)
                out_ref[s, owners[j % slots], j // slots] = piece


def project(owners, blocks, weight, present, earlier=None):
    halves = len(blocks)
    flat = [block for part in blocks for block in part]
    local, depth = flat[0].shape
    columns = weight.shape[1]
    rows = local // STEPS
    count = len(flat)
    more = [] if earlier is None else [earlier]
    tile = min(512, depth)
    streamed = [
        pltpu.VMEM((depth // tile, tile, columns), BF16),
        pltpu.SemaphoreType.DMA((depth // tile,)),
    ]
    return pl.pallas_call(
        functools.partial(out_kernel, count, earlier is not None),
        out_shape=jax.ShapeDtypeStruct((STEPS, 4, halves, rows, columns), BF16),
        in_specs=[SMEM] + [VMEM] * count + [VMEM if more else HBM] + [VMEM] * len(more),
        out_specs=VMEM,
        scratch_shapes=[
            pltpu.VMEM((present * halves * local, depth), BF16),
            pltpu.VMEM((present * halves * local, columns), F32),
        ]
        + ([] if more else streamed),
        compiler_params=pltpu.CompilerParams(vmem_limit_bytes=(24 if more else 28) * MIB),
        cost_estimate=pl.CostEstimate(
            flops=2 * present * halves * local * depth * columns,
            bytes_accessed=2 * depth * columns + 4 * present * local * (depth + columns),
            transcendentals=0,
        ),
        name="project",
    )(owners, *flat, weight, *more)


def lookup(identity, table):
    hits = identity[:, None] == jnp.arange(table.shape[0], dtype=jnp.int32)[None, :]
    return jnp.sum(jnp.where(hits, table[None, :], 0), axis=1)


def ascending(lengths):
    count = lengths.shape[0]
    rows = jnp.arange(count, dtype=jnp.int32)
    keyed = lengths * count + rows
    rank = jnp.sum((keyed[None, :] < keyed[:, None]).astype(jnp.int32), axis=1)
    return jnp.sum(jnp.where(rank[:, None] == rows[None, :], rows[:, None], 0), axis=0)


def angle_tables(lengths, unit):
    steps = jnp.arange(STEPS, dtype=jnp.int32)
    position = lengths.reshape(-1, 1, unit) + steps[None, :, None]
    freq = rope_base ** (-(jnp.arange(HD // 2, dtype=F32) * 2.0 / HD))
    angles = position.reshape(-1).astype(F32)[:, None] * freq
    cosine = jnp.cos(angles)
    sine = jnp.sin(angles)
    return jnp.concatenate([cosine, cosine], 1), jnp.concatenate([-sine, sine], 1)


def on_device(
    hidden,
    input_norm_scale,
    query_key_value_weight,
    output_weight,
    adapter_down_weight,
    adapter_up_weight,
    row_adapter_index,
    adapter_store_slot,
    lengths,
    key_value_cache,
):
    tensor_count = lax.axis_size("tensor")
    tensor_pos = lax.axis_index("tensor")
    store_pos = lax.axis_index("store")
    _, rows, span = hidden.shape
    model_width = input_norm_scale.shape[0]
    rows_here = lengths.shape[0]
    unit = min(RUN, rows_here)
    line = tensor_count == 4 and rows_here % (HALVES * RUN) == 0
    halves = HALVES if line else 1
    part_rows = rows_here // halves
    local = STEPS * part_rows
    held_slots = adapter_down_weight.shape[0]
    rank = adapter_down_weight.shape[2]

    raw = hidden.reshape(STEPS, tensor_count, halves, part_rows // unit, unit, span)
    raw = raw.transpose(2, 1, 3, 0, 4, 5).reshape(STEPS * rows, span)
    own_index = tensor_pos.reshape(1).astype(jnp.int32)
    owners = [own_index] + [hop_owners(tensor_pos, hop) for hop in (1, 2, 3)]
    count = tensor_count * local
    parts = [slice(h * count, (h + 1) * count) for h in range(halves)]
    values = raw.astype(F32)
    squares = jnp.sum(values * values, axis=1)
    if line:
        squares = squares + sum(swap(squares, "tensor", d) for d in (1, 2, 3))
        travelling, squares = lax.optimization_barrier((raw, squares))
        hop1 = line_hop(travelling, travelling, "tensor", 1)
    else:
        squares = summed_over(squares, "tensor")
    own_runs = row_adapter_index[::RUN]
    if halves > 1:
        own_runs = own_runs.reshape(tensor_count, halves, -1).swapaxes(0, 1).reshape(-1)
    told = jnp.concatenate([squares, own_runs.astype(F32)]).reshape(1, -1)
    told = jnp.concatenate([told, swap(told, "store", 2)], axis=0)
    beside = swap(raw, "store", 1)
    if line:
        told, hop1, beside = lax.optimization_barrier((told, hop1, beside))
        sent = [(hop1[0][part], hop1[1][part]) for part in parts]
        hop2 = [line_hop(*sent[0], "tensor", 2)]
    told = jnp.concatenate([told, swap(told, "store", 1)], axis=0)
    told = jnp.stack([told[d] for d in (0, 2, 1, 3)])
    told = jnp.stack([jnp.stack([told[p ^ q] for q in range(4)]) for p in range(4)])
    told = lax.dynamic_index_in_dim(told, store_pos, 0, keepdims=False)
    runs = told[:, STEPS * rows :].astype(jnp.int32)
    told = told[:, : STEPS * rows]
    scales = lax.rsqrt(told / model_width + eps_norm)
    slots = lookup(runs.reshape(-1), adapter_store_slot).reshape(runs.shape)
    slots = jnp.where(slots // held_slots == store_pos, slots % held_slots, -1)
    place = store_pos.reshape(1).astype(jnp.int32)
    gains = input_norm_scale.reshape(1, -1)
    gain = lax.dynamic_slice_in_dim(gains, tensor_pos * span, span, 1)
    scales = scales[:, :, None]
    own_scale = lax.dynamic_index_in_dim(scales, store_pos, 0, keepdims=False)

    across = swap(raw, "store", 2)
    diagonal = swap(across, "store", 1)
    mine = slots.reshape(-1)
    down = jnp.swapaxes(adapter_down_weight, 1, 2)
    kept, passed = shrink_rows(place, mine, (raw, beside, across, diagonal), scales, gain, down)
    kept = kept + swap(passed, "store", 1)
    shrunk = kept[0] + swap(kept[1], "store", 2)
    if line:
        shrunk, hop2[0] = lax.optimization_barrier((shrunk, hop2[0]))
        shrunk = shrunk + swap(shrunk, "tensor", 1)
        shrunk = shrunk + swap(shrunk, "tensor", 2)
        shrunk, sent[1], hop2[0] = lax.optimization_barrier((shrunk, sent[1], hop2[0]))
        hop3 = [line_hop(*hop2[0], "tensor", 3)]
        hop2.append(line_hop(*sent[1], "tensor", 2))
    else:
        shrunk = summed_over(shrunk, "tensor")
    shrunk = shrunk.astype(BF16)
    shrunk = jnp.stack([shrunk, swap(shrunk, "store", 2)])
    other = swap(shrunk, "store", 1)
    kept, *passed = grow_rows(place, mine, shrunk, other, adapter_up_weight, 1)
    if line:
        passed, hop3[0] = lax.optimization_barrier((passed, hop3[0]))
    passed = [swap(piece, "store", 1) for piece in passed]
    leaving = [(kept[1, part] + passed[1][part]).astype(F16) for part in parts]
    arrived = [swap(piece, "store", 2).astype(F32) for piece in leaving]
    if line:
        arrived[0], hop2[1] = lax.optimization_barrier((arrived[0], hop2[1]))
        hop3.append(line_hop(*hop2[1], "tensor", 3))
    deltas = [(kept[0, p] + passed[0][p]) + far for p, far in zip(parts, arrived)]

    weight = query_key_value_weight
    mixed = []
    if line:
        early, leaving = lax.optimization_barrier(((raw,) + hop1, leaving))
        near = jnp.concatenate(owners[:2])
        total = base_block(early, own_scale, gains, weight, near, (0,) * 3, 3)
        far = jnp.concatenate(owners[2:])
        for h, part in enumerate(parts):
            if mixed:
                far, mixed[-1] = lax.optimization_barrier((far, mixed[-1]))
            blocks = hop2[h] + hop3[h]
            first_rows = (0,) * 4
            sums = base_block(
                blocks, own_scale[part], gains, weight, far, first_rows, 2, total[part]
            )
            mixed.append((sums + deltas[h]).astype(BF16))
    else:
        everything = lax.all_gather(raw, "tensor", axis=0, tiled=False)
        own = base_block((raw,), own_scale, gains, weight, own_index, (0,), 1)
        total = base_rows(own_index, everything, own_scale, gains, own, weight, 0)
        mixed.append((total + deltas[0]).astype(BF16))
    mixed = [qkv.reshape(tensor_count, local, -1) for qkv in mixed]

    contexts = []
    exchanged = []
    for qkv in mixed:
        if exchanged:
            qkv, exchanged[-1] = lax.optimization_barrier((qkv, exchanged[-1]))
        exchanged.append(lax.all_to_all(qkv, "tensor", 0, 0, tiled=True))
    for h, moved in enumerate(exchanged):
        if tensor_count != 4:
            q_columns = HEADS * HD // tensor_count
            pieces = []
            for piece in (moved[..., :q_columns], moved[..., q_columns:]):
                joined = piece.transpose(1, 0, 2).reshape(local, 4, -1)
                pieces.append(joined.transpose(1, 0, 2))
            moved = jnp.concatenate(pieces, axis=2)
        here = lengths[h * part_rows : (h + 1) * part_rows]
        cosine, sine = angle_tables(here, unit)
        contexts.append(
            attend(here, ascending(here), moved, cosine, sine, key_value_cache, h * part_rows, unit)
        )

    if line:
        hops = [line_gather(context, "tensor") for context in contexts]
        first = [(context,) + hop[0] for context, hop in zip(contexts, hops)]
        last = [hop[1] + hop[2] for hop in hops]
        output = project(jnp.concatenate(owners[:2]), first, output_weight, 3)
        output = project(jnp.concatenate(owners[2:]), last, output_weight, 2, output)
    else:
        results = []
        for context in contexts:
            context = lax.all_gather(context, "tensor", axis=0, tiled=True)
            result = jnp.dot(context, output_weight, preferred_element_type=F32).astype(BF16)
            result = result.reshape(tensor_count, part_rows // unit, STEPS, unit, -1)
            result = result.transpose(2, 0, 1, 3, 4).reshape(STEPS, tensor_count, part_rows, -1)
            results.append(result)
        output = jnp.stack(results, axis=2)
    return output.reshape(STEPS, rows, -1)


def solution(mesh):
    in_specs = (
        P(None, ("groups", "store"), "tensor"),
        P(),
        P(None, "tensor"),
        P(None, "tensor"),
        P(("groups", "store"), "tensor", None),
        P(("groups", "store"), None, "tensor"),
        P(("groups", "store")),
        P("groups"),
        P(("groups", "store", "tensor")),
        P(("groups", "store", "tensor"), None, None, None),
    )
    out_specs = P(None, ("groups", "store"), "tensor")
    return jax.shard_map(
        on_device, mesh=mesh, in_specs=in_specs, out_specs=out_specs, check_vma=False
    )
```

```python
import functools

import jax
import jax.numpy as jnp
from jax import lax
from jax.experimental import pallas as pl
from jax.experimental.pallas import tpu as pltpu
from jax.sharding import PartitionSpec as P

HEADS = 32
KVH = 4
HD = 128
GROUP = HEADS // KVH
RUN = 8
STEPS = 2
LANES = 128
HALVES = 2

eps_norm = 1e-05
rope_base = 500000.0
masked = -1e30

MIB = 1 << 20
F32 = jnp.float32
BF16 = jnp.bfloat16
F16 = jnp.float16
VMEM = pl.BlockSpec(memory_space=pltpu.VMEM)
SMEM = pl.BlockSpec(memory_space=pltpu.SMEM)
HBM = pl.BlockSpec(memory_space=pltpu.HBM)
ANY = pl.BlockSpec(memory_space=pl.ANY)


def swap(values, axis, distance):
    count = lax.axis_size(axis)
    return lax.ppermute(values, axis, [(i, i ^ distance) for i in range(count)])


def summed_over(values, axis):
    distance = 1
    while distance < lax.axis_size(axis):
        values = values + swap(values, axis, distance)
        distance *= 2
    return values


def line_hop(up, down, axis, hop):
    up = lax.ppermute(up, axis, [(i, i + 1) for i in range(hop - 1, 3)])
    down = lax.ppermute(down, axis, [(i, i - 1) for i in range(4 - hop, 0, -1)])
    return up, down


def line_gather(block, axis):
    hops = [line_hop(block, block, axis, 1)]
    for hop in (2, 3):
        hops.append(line_hop(*hops[-1], axis, hop))
    return hops


def hop_owners(position, hop):
    below = position - hop
    above = position + hop
    return jnp.stack([jnp.where(below >= 0, below, -1), jnp.where(above < 4, above, -1)])


def block_kernel(first_rows, has_total, owners, *refs):
    count = len(first_rows)
    x_refs = refs[:count]
    scale_ref, gain_ref, w_ref = refs[count : count + 3]
    out_ref, held_x, held, x_sems, sems = refs[-5:]
    rows = scale_ref.shape[0]
    _, tiles, depth, _ = held.shape

    def slot(j):
        used = jnp.int32(0)
        for i in range(j):
            used = used + (owners[i] >= 0).astype(jnp.int32)
        return used

    def copy(j, k):
        first = pl.multiple_of((owners[j] * tiles + k) * depth, depth)
        return pltpu.make_async_copy(
            w_ref.at[pl.ds(first, depth), :], held.at[slot(j), k], sems.at[slot(j), k]
        )

    def x_copy(j):
        part = x_refs[j].at[first_rows[j] : first_rows[j] + rows, :]
        return pltpu.make_async_copy(part, held_x.at[slot(j)], x_sems.at[slot(j)])

    for j in range(count):

        @pl.when(owners[j] >= 0)
        def _():
            x_copy(j).start()
            for k in range(tiles):
                copy(j, k).start()

    out_ref[...] = refs[count + 3][...] if has_total else jnp.zeros_like(out_ref)
    for j in range(count):

        @pl.when(owners[j] >= 0)
        def _():
            scale = scale_ref[...]
            x_copy(j).wait()
            for k in range(tiles):
                span = slice(k * depth, (k + 1) * depth)
                first = pl.multiple_of((owners[j] * tiles + k) * depth, depth)
                gain = gain_ref[:, pl.ds(first, depth)]
                part = held_x[slot(j), :, span].astype(F32)
                normed = (part * scale * gain).astype(BF16)
                copy(j, k).wait()
                out_ref[...] += jnp.dot(normed, held[slot(j), k], preferred_element_type=F32)


def base_block(blocks, scale, gain, weight, owners, first_rows, present, total=None):
    depth = blocks[0].shape[1]
    rows = scale.shape[0]
    columns = weight.shape[1]
    tile = min(512, depth)
    count = len(blocks)
    more = [] if total is None else [total]
    return pl.pallas_call(
        functools.partial(block_kernel, first_rows, total is not None),
        out_shape=jax.ShapeDtypeStruct((rows, columns), F32),
        in_specs=[SMEM] + [ANY] * count + [VMEM] * 2 + [HBM] + [VMEM] * len(more),
        out_specs=VMEM,
        scratch_shapes=[
            pltpu.VMEM((present, rows, depth), BF16),
            pltpu.VMEM((present, depth // tile, tile, columns), BF16),
            pltpu.SemaphoreType.DMA((present,)),
            pltpu.SemaphoreType.DMA((present, depth // tile)),
        ],
        compiler_params=pltpu.CompilerParams(vmem_limit_bytes=46 * MIB),
        cost_estimate=pl.CostEstimate(
            flops=rows * columns,
            bytes_accessed=rows * columns,
            transcendentals=0,
        ),
        name="base_block",
    )(owners, *blocks, scale, gain, weight, *more)


def base_kernel(first_row, place_ref, x_ref, scale_ref, gain_ref, own_ref, w_ref, out_ref, held, sems):
    owners, _, span = x_ref.shape
    rows = scale_ref.shape[0]
    tiles, depth, _ = held.shape
    tiles_each = span // depth

    def spot(k):
        owner = lax.rem(place_ref[0] + 1 + k // tiles_each, owners)
        return owner, pl.multiple_of((owner * tiles_each + k % tiles_each) * depth, depth)

    copies = [
        pltpu.make_async_copy(w_ref.at[pl.ds(spot(k)[1], depth), :], held.at[k], sems.at[k])
        for k in range(tiles)
    ]
    for copy in copies:
        copy.start()
    scale = scale_ref[...]
    out_ref[...] = own_ref[first_row : first_row + rows, :]
    for k, copy in enumerate(copies):
        owner, first = spot(k)
        inner = (k % tiles_each) * depth
        gain = gain_ref[:, pl.ds(first, depth)]
        part = x_ref[owner, first_row : first_row + rows, inner : inner + depth].astype(F32)
        normed = (part * scale * gain).astype(BF16)
        copy.wait()
        out_ref[...] += jnp.dot(normed, held[k], preferred_element_type=F32)


def base_rows(place, x, scale, gain, own, weight, first_row):
    owners, _, span = x.shape
    rows = scale.shape[0]
    columns = weight.shape[1]
    tile = min(512, span)
    tiles = (owners - 1) * span // tile
    return pl.pallas_call(
        functools.partial(base_kernel, first_row),
        out_shape=jax.ShapeDtypeStruct((rows, columns), F32),
        in_specs=[SMEM] + [VMEM] * 4 + [HBM],
        out_specs=VMEM,
        scratch_shapes=[
            pltpu.VMEM((tiles, tile, columns), BF16),
            pltpu.SemaphoreType.DMA((tiles,)),
        ],
        compiler_params=pltpu.CompilerParams(vmem_limit_bytes=48 * MIB),
        cost_estimate=pl.CostEstimate(
            flops=2 * rows * tiles * tile * columns,
            bytes_accessed=2 * tiles * tile * (rows + columns) + 8 * rows * columns,
            transcendentals=0,
        ),
        name="base_rows",
    )(place, x, scale, gain, own, weight)


TEAM = 4
SLABS = (0, 2, 1, 3)


def list_runs(place_ref, slots, runs, jobs, start):
    def look(run, carry, slab, d):
        slot = slots[(place_ref[0] ^ d) * runs + run]

        @pl.when(slot >= 0)
        def _():
            jobs[carry] = slab * runs + run
            start(carry, d, run, slot)

        return carry + (slot >= 0).astype(jnp.int32)

    count = jnp.int32(0)
    for slab, d in enumerate(SLABS):
        count = lax.fori_loop(0, runs, functools.partial(look, slab=slab, d=d), count)
    return count


def work_in_teams(count, wait, work):
    def team(g, carry):
        for u in range(TEAM):

            @pl.when(g * TEAM + u < count)
            def _():
                wait(g * TEAM + u)

        work([jnp.minimum(g * TEAM + u, count - 1) for u in range(TEAM)])
        return carry

    lax.fori_loop(0, (count + TEAM - 1) // TEAM, team, 0)


def shrink_kernel(
    place_ref,
    slots,
    x0,
    x1,
    x2,
    x3,
    scale_ref,
    gain_ref,
    down_ref,
    keep_ref,
    send_ref,
    jobs,
    parts,
    held_x,
    held,
    x_sems,
    sems,
):
    runs = held.shape[0] // 4
    rank = held.shape[1]
    x_refs = (x0, x1, x2, x3)

    def x_copy(i, d, run):
        rows = pl.ds(pl.multiple_of(run * 16, 16), 16)
        return pltpu.make_async_copy(x_refs[d].at[rows, :], held_x.at[i], x_sems.at[i])

    def copy(i, slot):
        return pltpu.make_async_copy(down_ref.at[slot], held.at[i], sems.at[i])

    def start(i, d, run, slot):
        copy(i, slot).start()
        x_copy(i, d, run).start()

    def wait(i):
        copy(i, 0).wait()
        x_copy(i, 0, 0).wait()

    def work(members):
        results = []
        for i in members:
            job = jobs[i]
            slab = job // runs
            d = jnp.where(slab == 1, 2, jnp.where(slab == 2, 1, slab))
            rows = pl.ds(pl.multiple_of((job % runs) * 16, 16), 16)
            scale = scale_ref[place_ref[0] ^ d, rows, :]
            normed = (held_x[i].astype(F32) * scale * gain_ref[...]).astype(BF16)
            part = lax.dot_general(
                normed, held[i], (((1,), (1,)), ((), ())), preferred_element_type=F32
            )
            results.append((job, part))
        for job, part in results:
            parts[job] = part

    count = list_runs(place_ref, slots, runs, jobs, start)
    parts[...] = jnp.zeros_like(parts)
    work_in_teams(count, wait, work)
    for slab in range(4):
        for i in range(runs // 2):
            low = slab * runs + i
            out_ref = (keep_ref, send_ref)[slab // 2]
            out_ref[slab % 2, i * 16 : (i + 1) * 16, :] = jnp.concatenate(
                [parts[low], parts[low + runs // 2]], axis=1
            )


def shrink_rows(place, slots, blocks, scales, gain, down):
    rows, depth = blocks[0].shape
    rank = down.shape[1]
    runs = rows // 16
    return pl.pallas_call(
        shrink_kernel,
        out_shape=[jax.ShapeDtypeStruct((2, rows // 2, 2 * rank), F32)] * 2,
        in_specs=[SMEM] * 2 + [ANY] * 4 + [VMEM] * 2 + [HBM],
        out_specs=[VMEM] * 2,
        scratch_shapes=[
            pltpu.SMEM((4 * runs,), jnp.int32),
            pltpu.VMEM((4 * runs, 16, rank), F32),
            pltpu.VMEM((4 * runs, 16, depth), BF16),
            pltpu.VMEM((4 * runs, rank, depth), BF16),
            pltpu.SemaphoreType.DMA((4 * runs,)),
            pltpu.SemaphoreType.DMA((4 * runs,)),
        ],
        compiler_params=pltpu.CompilerParams(vmem_limit_bytes=48 * MIB),
        cost_estimate=pl.CostEstimate(
            flops=rows * depth,
            bytes_accessed=rows * depth,
            transcendentals=0,
        ),
        name="shrink_rows",
    )(place, slots, *blocks, scales, gain, down)


def grow_kernel(
    place_ref, slots, s0, s1, up_ref, keep_ref, *refs
):
    *sends, jobs, parts, held, sems = refs
    pieces = len(sends) // 2
    piece = keep_ref.shape[1] // pieces
    runs = held.shape[0] // 4
    rank = held.shape[1]

    def copy(i, slot):
        return pltpu.make_async_copy(up_ref.at[slot], held.at[i], sems.at[i])

    def start(i, d, run, slot):
        copy(i, slot).start()

    def wait(i):
        copy(i, 0).wait()

    def work(members):
        results = []
        for i in members:
            job = jobs[i]
            grown = jnp.dot(parts[job], held[i], preferred_element_type=F32)
            results.append((job, grown))
        for job, grown in results:
            rows = pl.ds(pl.multiple_of((job % runs) * 16, 16), 16)
            slab = job // runs

            @pl.when(slab < 2)
            def _():
                keep_ref[slab, rows, :] = grown

            run = job % runs
            inner = pl.ds(pl.multiple_of(lax.rem(run * 16, piece), 16), 16)
            target = (slab - 2) * pieces + (run * 16) // piece
            for i, send_ref in enumerate(sends):

                @pl.when((slab >= 2) & (target == i))
                def _():
                    send_ref[inner, :] = grown

    count = list_runs(place_ref, slots, runs, jobs, start)
    for slab in range(4):
        for i in range(runs // 2):
            low = slab * runs + i
            both = (s0, s1)[slab // 2][slab % 2, i * 16 : (i + 1) * 16, :]
            parts[low] = both[:, :rank]
            parts[low + runs // 2] = both[:, rank:]
    keep_ref[...] = jnp.zeros_like(keep_ref)
    for send_ref in sends:
        send_ref[...] = jnp.zeros_like(send_ref)
    work_in_teams(count, wait, work)


def grow_rows(place, slots, kept, passed, up, pieces):
    _, pair_rows, _ = kept.shape
    rows = 2 * pair_rows
    rank, columns = up.shape[1:]
    runs = rows // 16
    return pl.pallas_call(
        grow_kernel,
        out_shape=[jax.ShapeDtypeStruct((2, rows, columns), F32)]
        + [jax.ShapeDtypeStruct((rows // pieces, columns), F32)] * (2 * pieces),
        in_specs=[SMEM, SMEM, VMEM, VMEM, HBM],
        out_specs=[VMEM] * (1 + 2 * pieces),
        scratch_shapes=[
            pltpu.SMEM((4 * runs,), jnp.int32),
            pltpu.VMEM((4 * runs, 16, rank), BF16),
            pltpu.VMEM((4 * runs, rank, columns), BF16),
            pltpu.SemaphoreType.DMA((4 * runs,)),
        ],
        compiler_params=pltpu.CompilerParams(vmem_limit_bytes=48 * MIB),
        cost_estimate=pl.CostEstimate(
            flops=rows * columns,
            bytes_accessed=rows * columns,
            transcendentals=0,
        ),
        name="grow_rows",
    )(place, slots, kept, passed, up)


def attend_kernel(
    unit,
    first_row,
    lengths,
    order,
    qkv_ref,
    cos_ref,
    sin_ref,
    cache_ref,
    out_ref,
    queries,
    keys,
    values,
    context,
    held,
    sems,
):
    rows, _, cached, _ = held.shape
    local = STEPS * rows
    q_columns = GROUP * HD
    part = cached // 2
    scale = HD ** (-0.5)
    team = min(4, rows)

    def copy(r, b):
        span = pl.ds(b * part, part)
        return pltpu.make_async_copy(
            cache_ref.at[first_row + r, :, span, :], held.at[r, :, span, :], sems.at[r, b]
        )

    def longest(group):
        return lengths[order[group * team + team - 1]]

    def fetch(i, carry):
        r = order[i]
        copy(r, 0).start()

        @pl.when(longest(i // team) > part)
        def _():
            copy(r, 1).start()

        return carry

    lax.fori_loop(0, rows, fetch, 0)

    cosine = cos_ref[...]
    sine = sin_ref[...]

    def rotated(x):
        x = x.astype(F32)
        turned = x * cosine + pltpu.roll(x, HD // 2, 1) * sine
        return turned.astype(BF16).astype(F32)

    for k in range(KVH):
        for g in range(GROUP):
            queries[k, g * local : (g + 1) * local, :] = rotated(
                qkv_ref[k, :, g * HD : (g + 1) * HD]
            )
        place = q_columns + (k % 2) * HD
        keys[k] = rotated(qkv_ref[k // 2, :, place : place + HD])
        values[k] = qkv_ref[2 + k // 2, :, place : place + HD].astype(F32)

    early = lax.broadcasted_iota(jnp.int32, (4 * GROUP, 1), 0) % (2 * GROUP) < GROUP

    def scores(r, at, pair, span, live):
        heads = (2 * pair, 2 * pair + 1)
        query = [
            jnp.concatenate(
                [queries[k, pl.ds(at[s], GROUP, stride=local), :] for s in range(STEPS)], axis=0
            )
            for k in heads
        ]
        blank = jnp.zeros((2 * GROUP, HD), F32)
        spread = jnp.concatenate(
            [
                jnp.concatenate([query[0], blank], axis=1),
                jnp.concatenate([blank, query[1]], axis=1),
            ],
            axis=0,
        ).astype(BF16)
        old_keys = jnp.concatenate([held[r, k, :span, :HD] for k in heads], axis=1)
        old = lax.dot_general(
            spread, old_keys, (((1,), (1,)), ((), ())), preferred_element_type=F32
        )
        old = jnp.where(live, old * scale, masked)
        fresh = []
        for t in range(STEPS):
            both = jnp.concatenate(
                [
                    jnp.sum(query[i] * keys[k, pl.ds(at[t], 1), :], axis=1, keepdims=True)
                    for i, k in enumerate(heads)
                ],
                axis=0,
            )
            fresh.append(both * scale)
        fresh[1] = jnp.where(early, masked, fresh[1])
        return old, fresh

    def soften(old, fresh):
        peak = jnp.maximum(jnp.max(old, axis=1, keepdims=True), jnp.maximum(fresh[0], fresh[1]))
        p_old = jnp.exp(old - peak)
        p_new = [jnp.exp(f - peak) for f in fresh]
        total = jnp.sum(p_old, axis=1, keepdims=True) + (p_new[0] + p_new[1])
        return p_old.astype(BF16), [p.astype(BF16).astype(F32) for p in p_new], total

    def mix(r, at, pair, span, w_old, w_new, total):
        heads = (2 * pair, 2 * pair + 1)
        old_values = jnp.concatenate([held[r, k, :span, HD:] for k in heads], axis=1)
        mixed = jnp.dot(w_old, old_values, preferred_element_type=F32)
        for i, k in enumerate(heads):
            own = slice(i * 2 * GROUP, (i + 1) * 2 * GROUP)
            result = mixed[own, i * HD : (i + 1) * HD]
            for t in range(STEPS):
                result = result + w_new[t][own] * values[k, pl.ds(at[t], 1), :]
            result = result / total[own]
            for s in range(STEPS):
                context[k, pl.ds(at[s], GROUP, stride=local), :] = result[
                    s * GROUP : (s + 1) * GROUP
                ]

    def attend_team(members, span):
        jobs = []
        for r in members:
            at = [(r // unit) * (STEPS * unit) + s * unit + r % unit for s in range(STEPS)]
            live = lax.broadcasted_iota(jnp.int32, (4 * GROUP, span), 1) < lengths[r]
            for pair in range(KVH // 2):
                jobs.append((r, at, pair, scores(r, at, pair, span, live)))
        softened = [soften(*job[3]) for job in jobs]
        for (r, at, pair, _), weights in zip(jobs, softened):
            mix(r, at, pair, span, *weights)

    def each(group, carry):
        members = [order[group * team + i] for i in range(team)]
        wide = longest(group) > part
        for r in members:
            copy(r, 0).wait()

        @pl.when(wide)
        def _():
            for r in members:
                copy(r, 1).wait()
            attend_team(members, cached)

        @pl.when(jnp.logical_not(wide))
        def _():
            attend_team(members, part)

        return carry

    lax.fori_loop(0, rows // team, each, 0)
    for k in range(KVH):
        for g in range(GROUP):
            place = (k * GROUP + g) * HD
            out_ref[:, place : place + HD] = context[k, g * local : (g + 1) * local, :].astype(BF16)


def attend(lengths, order, qkv, cosine, sine, cache, first_row, unit):
    rows = lengths.shape[0]
    local = STEPS * rows
    _, kv_heads, cached, width = cache.shape
    return pl.pallas_call(
        functools.partial(attend_kernel, unit, first_row),
        out_shape=jax.ShapeDtypeStruct((local, HEADS * HD), BF16),
        in_specs=[SMEM, SMEM, VMEM, VMEM, VMEM, HBM],
        out_specs=VMEM,
        scratch_shapes=[
            pltpu.VMEM((KVH, GROUP * local, HD), F32),
            pltpu.VMEM((KVH, local, HD), F32),
            pltpu.VMEM((KVH, local, HD), F32),
            pltpu.VMEM((KVH, GROUP * local, HD), F32),
            pltpu.VMEM((rows, kv_heads, cached, width), BF16),
            pltpu.SemaphoreType.DMA((rows, 2)),
        ],
        compiler_params=pltpu.CompilerParams(vmem_limit_bytes=28 * MIB),
        cost_estimate=pl.CostEstimate(
            flops=4 * local * HEADS * HD * cached,
            bytes_accessed=2 * rows * kv_heads * cached * width,
            transcendentals=local * HEADS * cached,
        ),
        name="attend",
    )(lengths, order, qkv, cosine, sine, cache)


def out_kernel(count, has_earlier, owners, *refs):
    blocks = refs[:count]
    w_ref = refs[count]
    if has_earlier:
        out_ref, lhs, total = refs[-3:]
    else:
        out_ref, lhs, total, held, sems = refs[-5:]
        tiles, tile, _ = held.shape
        copies = [
            pltpu.make_async_copy(w_ref.at[pl.ds(k * tile, tile), :], held.at[k], sems.at[k])
            for k in range(tiles)
        ]
        for copy in copies:
            copy.start()
    local, depth = blocks[0].shape
    rows = local // STEPS
    columns = w_ref.shape[1]
    halves = out_ref.shape[2]
    slots = count // halves

    def place(j):
        used = jnp.int32(0)
        for i in range(j % slots):
            used = used + (owners[i] >= 0).astype(jnp.int32)
        return (j // slots) * (lhs.shape[0] // halves) + used * local

    lhs[...] = jnp.zeros_like(lhs)
    for j, ref in enumerate(blocks):

        @pl.when(owners[j % slots] >= 0)
        def _():
            lhs[pl.ds(pl.multiple_of(place(j), local), local), :] = ref[...]

    if has_earlier:
        out_ref[...] = refs[count + 1][...]
    width = min(512, columns)
    spans = [slice(j * width, (j + 1) * width) for j in range(columns // width)]
    if has_earlier:
        for span in spans:
            total[:, span] = jnp.dot(lhs[...], w_ref[:, span], preferred_element_type=F32)
    else:
        for k, copy in enumerate(copies):
            copy.wait()
            part = lhs[:, k * tile : (k + 1) * tile]
            for span in spans:
                product = jnp.dot(part, held[k, :, span], preferred_element_type=F32)
                total[:, span] = product if k == 0 else total[:, span] + product
    for j in range(count):

        @pl.when(owners[j % slots] >= 0)
        def _():
            block = total[pl.ds(pl.multiple_of(place(j), local), local), :]
            block = block.reshape(rows // RUN, STEPS, RUN, columns)
            for s in range(STEPS):
                piece = block[:, s].reshape(rows, columns).astype(BF16)
                out_ref[s, owners[j % slots], j // slots] = piece


def project(owners, blocks, weight, present, earlier=None):
    halves = len(blocks)
    flat = [block for part in blocks for block in part]
    local, depth = flat[0].shape
    columns = weight.shape[1]
    rows = local // STEPS
    count = len(flat)
    more = [] if earlier is None else [earlier]
    tile = min(512, depth)
    streamed = [
        pltpu.VMEM((depth // tile, tile, columns), BF16),
        pltpu.SemaphoreType.DMA((depth // tile,)),
    ]
    return pl.pallas_call(
        functools.partial(out_kernel, count, earlier is not None),
        out_shape=jax.ShapeDtypeStruct((STEPS, 4, halves, rows, columns), BF16),
        in_specs=[SMEM] + [VMEM] * count + [VMEM if more else HBM] + [VMEM] * len(more),
        out_specs=VMEM,
        scratch_shapes=[
            pltpu.VMEM((present * halves * local, depth), BF16),
            pltpu.VMEM((present * halves * local, columns), F32),
        ]
        + ([] if more else streamed),
        compiler_params=pltpu.CompilerParams(vmem_limit_bytes=(24 if more else 28) * MIB),
        cost_estimate=pl.CostEstimate(
            flops=2 * present * halves * local * depth * columns,
            bytes_accessed=2 * depth * columns + 4 * present * local * (depth + columns),
            transcendentals=0,
        ),
        name="project",
    )(owners, *flat, weight, *more)


def lookup(identity, table):
    hits = identity[:, None] == jnp.arange(table.shape[0], dtype=jnp.int32)[None, :]
    return jnp.sum(jnp.where(hits, table[None, :], 0), axis=1)


def ascending(lengths):
    count = lengths.shape[0]
    rows = jnp.arange(count, dtype=jnp.int32)
    keyed = lengths * count + rows
    rank = jnp.sum((keyed[None, :] < keyed[:, None]).astype(jnp.int32), axis=1)
    return jnp.sum(jnp.where(rank[:, None] == rows[None, :], rows[:, None], 0), axis=0)


def angle_tables(lengths, unit):
    steps = jnp.arange(STEPS, dtype=jnp.int32)
    position = lengths.reshape(-1, 1, unit) + steps[None, :, None]
    freq = rope_base ** (-(jnp.arange(HD // 2, dtype=F32) * 2.0 / HD))
    angles = position.reshape(-1).astype(F32)[:, None] * freq
    cosine = jnp.cos(angles)
    sine = jnp.sin(angles)
    return jnp.concatenate([cosine, cosine], 1), jnp.concatenate([-sine, sine], 1)


def on_device(
    hidden,
    input_norm_scale,
    query_key_value_weight,
    output_weight,
    adapter_down_weight,
    adapter_up_weight,
    row_adapter_index,
    adapter_store_slot,
    lengths,
    key_value_cache,
):
    tensor_count = lax.axis_size("tensor")
    tensor_pos = lax.axis_index("tensor")
    store_pos = lax.axis_index("store")
    _, rows, span = hidden.shape
    model_width = input_norm_scale.shape[0]
    rows_here = lengths.shape[0]
    unit = min(RUN, rows_here)
    line = tensor_count == 4 and rows_here % (HALVES * RUN) == 0
    halves = HALVES if line else 1
    part_rows = rows_here // halves
    local = STEPS * part_rows
    held_slots = adapter_down_weight.shape[0]
    rank = adapter_down_weight.shape[2]

    raw = hidden.reshape(STEPS, tensor_count, halves, part_rows // unit, unit, span)
    raw = raw.transpose(2, 1, 3, 0, 4, 5).reshape(STEPS * rows, span)
    own_index = tensor_pos.reshape(1).astype(jnp.int32)
    owners = [own_index] + [hop_owners(tensor_pos, hop) for hop in (1, 2, 3)]
    count = tensor_count * local
    parts = [slice(h * count, (h + 1) * count) for h in range(halves)]
    values = raw.astype(F32)
    squares = jnp.sum(values * values, axis=1)
    if line:
        squares = squares + sum(swap(squares, "tensor", d) for d in (1, 2, 3))
        travelling, squares = lax.optimization_barrier((raw, squares))
        hop1 = line_hop(travelling, travelling, "tensor", 1)
    else:
        squares = summed_over(squares, "tensor")
    own_runs = row_adapter_index[::RUN]
    if halves > 1:
        own_runs = own_runs.reshape(tensor_count, halves, -1).swapaxes(0, 1).reshape(-1)
    told = jnp.concatenate([squares, own_runs.astype(F32)]).reshape(1, -1)
    told = jnp.concatenate([told, swap(told, "store", 2)], axis=0)
    if line:
        told, hop1 = lax.optimization_barrier((told, hop1))
        hop2 = line_hop(*hop1, "tensor", 2)
    told = jnp.concatenate([told, swap(told, "store", 1)], axis=0)
    told = jnp.stack([told[d] for d in (0, 2, 1, 3)])
    told = jnp.stack([jnp.stack([told[p ^ q] for q in range(4)]) for p in range(4)])
    told = lax.dynamic_index_in_dim(told, store_pos, 0, keepdims=False)
    runs = told[:, STEPS * rows :].astype(jnp.int32)
    told = told[:, : STEPS * rows]
    scales = lax.rsqrt(told / model_width + eps_norm)
    slots = lookup(runs.reshape(-1), adapter_store_slot).reshape(runs.shape)
    slots = jnp.where(slots // held_slots == store_pos, slots % held_slots, -1)
    place = store_pos.reshape(1).astype(jnp.int32)
    gains = input_norm_scale.reshape(1, -1)
    gain = lax.dynamic_slice_in_dim(gains, tensor_pos * span, span, 1)
    scales = scales[:, :, None]
    own_scale = lax.dynamic_index_in_dim(scales, store_pos, 0, keepdims=False)

    across = swap(raw, "store", 2)
    beside = swap(raw, "store", 1)
    diagonal = swap(across, "store", 1)
    mine = slots.reshape(-1)
    down = jnp.swapaxes(adapter_down_weight, 1, 2)
    kept, passed = shrink_rows(place, mine, (raw, beside, across, diagonal), scales, gain, down)
    kept = kept + swap(passed, "store", 1)
    shrunk = kept[0] + swap(kept[1], "store", 2)
    if line:
        shrunk, early = lax.optimization_barrier((shrunk, (raw,) + hop1))
        near = jnp.concatenate(owners[:2])
        total = base_block(early, own_scale, gains, query_key_value_weight, near, (0,) * 3, 3)
        shrunk = shrunk + swap(shrunk, "tensor", 1)
        shrunk, total, hop2 = lax.optimization_barrier((shrunk, total, hop2))
        sent = [(hop2[0][part], hop2[1][part]) for part in parts]
        shrunk = shrunk + swap(shrunk, "tensor", 2)
        shrunk, sent = lax.optimization_barrier((shrunk, sent))
        hop3 = [line_hop(up, down, "tensor", 3) for up, down in sent]
    else:
        shrunk = summed_over(shrunk, "tensor")
    shrunk = shrunk.astype(BF16)
    shrunk = jnp.stack([shrunk, swap(shrunk, "store", 2)])
    other = swap(shrunk, "store", 1)
    kept, *passed = grow_rows(place, mine, shrunk, other, adapter_up_weight, 1)
    if line:
        passed, hop3[0] = lax.optimization_barrier((passed, hop3[0]))
    passed = [swap(piece, "store", 1) for piece in passed]
    leaving = [(kept[1, part] + passed[1][part]).astype(F16) for part in parts]
    arrived = [swap(piece, "store", 2).astype(F32) for piece in leaving]
    deltas = [(kept[0, p] + passed[0][p]) + far for p, far in zip(parts, arrived)]

    weight = query_key_value_weight
    mixed = []
    if line:
        total, leaving = lax.optimization_barrier((total, leaving))
        far = jnp.concatenate(owners[2:])
        for h, part in enumerate(parts):
            if mixed:
                far, mixed[-1] = lax.optimization_barrier((far, mixed[-1]))
            blocks = hop2 + hop3[h]
            first_rows = (h * count, h * count, 0, 0)
            sums = base_block(
                blocks, own_scale[part], gains, weight, far, first_rows, 2, total[part]
            )
            mixed.append((sums + deltas[h]).astype(BF16))
    else:
        everything = lax.all_gather(raw, "tensor", axis=0, tiled=False)
        own = base_block((raw,), own_scale, gains, weight, own_index, (0,), 1)
        total = base_rows(own_index, everything, own_scale, gains, own, weight, 0)
        mixed.append((total + deltas[0]).astype(BF16))
    mixed = [qkv.reshape(tensor_count, local, -1) for qkv in mixed]

    contexts = []
    exchanged = []
    for qkv in mixed:
        if exchanged:
            qkv, exchanged[-1] = lax.optimization_barrier((qkv, exchanged[-1]))
        exchanged.append(lax.all_to_all(qkv, "tensor", 0, 0, tiled=True))
    for h, moved in enumerate(exchanged):
        if tensor_count != 4:
            q_columns = HEADS * HD // tensor_count
            pieces = []
            for piece in (moved[..., :q_columns], moved[..., q_columns:]):
                joined = piece.transpose(1, 0, 2).reshape(local, 4, -1)
                pieces.append(joined.transpose(1, 0, 2))
            moved = jnp.concatenate(pieces, axis=2)
        here = lengths[h * part_rows : (h + 1) * part_rows]
        cosine, sine = angle_tables(here, unit)
        contexts.append(
            attend(here, ascending(here), moved, cosine, sine, key_value_cache, h * part_rows, unit)
        )

    if line:
        hops = [line_gather(context, "tensor") for context in contexts]
        first = [(context,) + hop[0] for context, hop in zip(contexts, hops)]
        last = [hop[1] + hop[2] for hop in hops]
        output = project(jnp.concatenate(owners[:2]), first, output_weight, 3)
        output = project(jnp.concatenate(owners[2:]), last, output_weight, 2, output)
    else:
        results = []
        for context in contexts:
            context = lax.all_gather(context, "tensor", axis=0, tiled=True)
            result = jnp.dot(context, output_weight, preferred_element_type=F32).astype(BF16)
            result = result.reshape(tensor_count, part_rows // unit, STEPS, unit, -1)
            result = result.transpose(2, 0, 1, 3, 4).reshape(STEPS, tensor_count, part_rows, -1)
            results.append(result)
        output = jnp.stack(results, axis=2)
    return output.reshape(STEPS, rows, -1)


def solution(mesh):
    in_specs = (
        P(None, ("groups", "store"), "tensor"),
        P(),
        P(None, "tensor"),
        P(None, "tensor"),
        P(("groups", "store"), "tensor", None),
        P(("groups", "store"), None, "tensor"),
        P(("groups", "store")),
        P("groups"),
        P(("groups", "store", "tensor")),
        P(("groups", "store", "tensor"), None, None, None),
    )
    out_specs = P(None, ("groups", "store"), "tensor")
    return jax.shard_map(
        on_device, mesh=mesh, in_specs=in_specs, out_specs=out_specs, check_vma=False
    )
```

```python
import functools

import jax
import jax.numpy as jnp
from jax import lax
from jax.experimental import pallas as pl
from jax.experimental.pallas import tpu as pltpu
from jax.sharding import PartitionSpec as P

HEADS = 32
KVH = 4
HD = 128
GROUP = HEADS // KVH
RUN = 8
STEPS = 2
LANES = 128
HALVES = 2

eps_norm = 1e-05
rope_base = 500000.0
masked = -1e30

MIB = 1 << 20
F32 = jnp.float32
BF16 = jnp.bfloat16
F16 = jnp.float16
VMEM = pl.BlockSpec(memory_space=pltpu.VMEM)
SMEM = pl.BlockSpec(memory_space=pltpu.SMEM)
HBM = pl.BlockSpec(memory_space=pltpu.HBM)
ANY = pl.BlockSpec(memory_space=pl.ANY)


def swap(values, axis, distance):
    count = lax.axis_size(axis)
    return lax.ppermute(values, axis, [(i, i ^ distance) for i in range(count)])


def summed_over(values, axis):
    distance = 1
    while distance < lax.axis_size(axis):
        values = values + swap(values, axis, distance)
        distance *= 2
    return values


def line_hop(up, down, axis, hop):
    up = lax.ppermute(up, axis, [(i, i + 1) for i in range(hop - 1, 3)])
    down = lax.ppermute(down, axis, [(i, i - 1) for i in range(4 - hop, 0, -1)])
    return up, down


def line_gather(block, axis):
    hops = [line_hop(block, block, axis, 1)]
    for hop in (2, 3):
        hops.append(line_hop(*hops[-1], axis, hop))
    return hops


def hop_owners(position, hop):
    below = position - hop
    above = position + hop
    return jnp.stack([jnp.where(below >= 0, below, -1), jnp.where(above < 4, above, -1)])


def block_kernel(first_rows, has_total, owners, *refs):
    count = len(first_rows)
    x_refs = refs[:count]
    scale_ref, gain_ref, w_ref = refs[count : count + 3]
    out_ref, held_x, held, x_sems, sems = refs[-5:]
    rows = scale_ref.shape[0]
    _, tiles, depth, _ = held.shape

    def slot(j):
        used = jnp.int32(0)
        for i in range(j):
            used = used + (owners[i] >= 0).astype(jnp.int32)
        return used

    def copy(j, k):
        first = pl.multiple_of((owners[j] * tiles + k) * depth, depth)
        return pltpu.make_async_copy(
            w_ref.at[pl.ds(first, depth), :], held.at[slot(j), k], sems.at[slot(j), k]
        )

    def x_copy(j):
        part = x_refs[j].at[first_rows[j] : first_rows[j] + rows, :]
        return pltpu.make_async_copy(part, held_x.at[slot(j)], x_sems.at[slot(j)])

    for j in range(count):

        @pl.when(owners[j] >= 0)
        def _():
            x_copy(j).start()
            for k in range(tiles):
                copy(j, k).start()

    out_ref[...] = refs[count + 3][...] if has_total else jnp.zeros_like(out_ref)
    for j in range(count):

        @pl.when(owners[j] >= 0)
        def _():
            scale = scale_ref[...]
            x_copy(j).wait()
            for k in range(tiles):
                span = slice(k * depth, (k + 1) * depth)
                first = pl.multiple_of((owners[j] * tiles + k) * depth, depth)
                gain = gain_ref[:, pl.ds(first, depth)]
                part = held_x[slot(j), :, span].astype(F32)
                normed = (part * scale * gain).astype(BF16)
                copy(j, k).wait()
                out_ref[...] += jnp.dot(normed, held[slot(j), k], preferred_element_type=F32)


def base_block(blocks, scale, gain, weight, owners, first_rows, present, total=None):
    depth = blocks[0].shape[1]
    rows = scale.shape[0]
    columns = weight.shape[1]
    tile = min(512, depth)
    count = len(blocks)
    more = [] if total is None else [total]
    return pl.pallas_call(
        functools.partial(block_kernel, first_rows, total is not None),
        out_shape=jax.ShapeDtypeStruct((rows, columns), F32),
        in_specs=[SMEM] + [ANY] * count + [VMEM] * 2 + [HBM] + [VMEM] * len(more),
        out_specs=VMEM,
        scratch_shapes=[
            pltpu.VMEM((present, rows, depth), BF16),
            pltpu.VMEM((present, depth // tile, tile, columns), BF16),
            pltpu.SemaphoreType.DMA((present,)),
            pltpu.SemaphoreType.DMA((present, depth // tile)),
        ],
        compiler_params=pltpu.CompilerParams(vmem_limit_bytes=46 * MIB),
        cost_estimate=pl.CostEstimate(
            flops=rows * columns,
            bytes_accessed=rows * columns,
            transcendentals=0,
        ),
        name="base_block",
    )(owners, *blocks, scale, gain, weight, *more)


def base_kernel(first_row, place_ref, x_ref, scale_ref, gain_ref, own_ref, w_ref, out_ref, held, sems):
    owners, _, span = x_ref.shape
    rows = scale_ref.shape[0]
    tiles, depth, _ = held.shape
    tiles_each = span // depth

    def spot(k):
        owner = lax.rem(place_ref[0] + 1 + k // tiles_each, owners)
        return owner, pl.multiple_of((owner * tiles_each + k % tiles_each) * depth, depth)

    copies = [
        pltpu.make_async_copy(w_ref.at[pl.ds(spot(k)[1], depth), :], held.at[k], sems.at[k])
        for k in range(tiles)
    ]
    for copy in copies:
        copy.start()
    scale = scale_ref[...]
    out_ref[...] = own_ref[first_row : first_row + rows, :]
    for k, copy in enumerate(copies):
        owner, first = spot(k)
        inner = (k % tiles_each) * depth
        gain = gain_ref[:, pl.ds(first, depth)]
        part = x_ref[owner, first_row : first_row + rows, inner : inner + depth].astype(F32)
        normed = (part * scale * gain).astype(BF16)
        copy.wait()
        out_ref[...] += jnp.dot(normed, held[k], preferred_element_type=F32)


def base_rows(place, x, scale, gain, own, weight, first_row):
    owners, _, span = x.shape
    rows = scale.shape[0]
    columns = weight.shape[1]
    tile = min(512, span)
    tiles = (owners - 1) * span // tile
    return pl.pallas_call(
        functools.partial(base_kernel, first_row),
        out_shape=jax.ShapeDtypeStruct((rows, columns), F32),
        in_specs=[SMEM] + [VMEM] * 4 + [HBM],
        out_specs=VMEM,
        scratch_shapes=[
            pltpu.VMEM((tiles, tile, columns), BF16),
            pltpu.SemaphoreType.DMA((tiles,)),
        ],
        compiler_params=pltpu.CompilerParams(vmem_limit_bytes=48 * MIB),
        cost_estimate=pl.CostEstimate(
            flops=2 * rows * tiles * tile * columns,
            bytes_accessed=2 * tiles * tile * (rows + columns) + 8 * rows * columns,
            transcendentals=0,
        ),
        name="base_rows",
    )(place, x, scale, gain, own, weight)


TEAM = 4
SLABS = (0, 2, 1, 3)


def list_runs(place_ref, slots, runs, jobs, start):
    def look(run, carry, slab, d):
        slot = slots[(place_ref[0] ^ d) * runs + run]

        @pl.when(slot >= 0)
        def _():
            jobs[carry] = slab * runs + run
            start(carry, d, run, slot)

        return carry + (slot >= 0).astype(jnp.int32)

    count = jnp.int32(0)
    for slab, d in enumerate(SLABS):
        count = lax.fori_loop(0, runs, functools.partial(look, slab=slab, d=d), count)
    return count


def work_in_teams(count, wait, work):
    def team(g, carry):
        for u in range(TEAM):

            @pl.when(g * TEAM + u < count)
            def _():
                wait(g * TEAM + u)

        work([jnp.minimum(g * TEAM + u, count - 1) for u in range(TEAM)])
        return carry

    lax.fori_loop(0, (count + TEAM - 1) // TEAM, team, 0)


def shrink_kernel(
    place_ref,
    slots,
    x0,
    x1,
    x2,
    x3,
    scale_ref,
    gain_ref,
    down_ref,
    keep_ref,
    send_ref,
    jobs,
    parts,
    held_x,
    held,
    x_sems,
    sems,
):
    runs = held.shape[0] // 4
    rank = held.shape[1]
    x_refs = (x0, x1, x2, x3)

    def x_copy(i, d, run):
        rows = pl.ds(pl.multiple_of(run * 16, 16), 16)
        return pltpu.make_async_copy(x_refs[d].at[rows, :], held_x.at[i], x_sems.at[i])

    def copy(i, slot):
        return pltpu.make_async_copy(down_ref.at[slot], held.at[i], sems.at[i])

    def start(i, d, run, slot):
        copy(i, slot).start()
        x_copy(i, d, run).start()

    def wait(i):
        copy(i, 0).wait()
        x_copy(i, 0, 0).wait()

    def work(members):
        results = []
        for i in members:
            job = jobs[i]
            slab = job // runs
            d = jnp.where(slab == 1, 2, jnp.where(slab == 2, 1, slab))
            rows = pl.ds(pl.multiple_of((job % runs) * 16, 16), 16)
            scale = scale_ref[place_ref[0] ^ d, rows, :]
            normed = (held_x[i].astype(F32) * scale * gain_ref[...]).astype(BF16)
            part = lax.dot_general(
                normed, held[i], (((1,), (1,)), ((), ())), preferred_element_type=F32
            )
            results.append((job, part))
        for job, part in results:
            parts[job] = part

    count = list_runs(place_ref, slots, runs, jobs, start)
    parts[...] = jnp.zeros_like(parts)
    work_in_teams(count, wait, work)
    for slab in range(4):
        for i in range(runs // 2):
            low = slab * runs + i
            out_ref = (keep_ref, send_ref)[slab // 2]
            out_ref[slab % 2, i * 16 : (i + 1) * 16, :] = jnp.concatenate(
                [parts[low], parts[low + runs // 2]], axis=1
            )


def shrink_rows(place, slots, blocks, scales, gain, down):
    rows, depth = blocks[0].shape
    rank = down.shape[1]
    runs = rows // 16
    return pl.pallas_call(
        shrink_kernel,
        out_shape=[jax.ShapeDtypeStruct((2, rows // 2, 2 * rank), F32)] * 2,
        in_specs=[SMEM] * 2 + [ANY] * 4 + [VMEM] * 2 + [HBM],
        out_specs=[VMEM] * 2,
        scratch_shapes=[
            pltpu.SMEM((4 * runs,), jnp.int32),
            pltpu.VMEM((4 * runs, 16, rank), F32),
            pltpu.VMEM((4 * runs, 16, depth), BF16),
            pltpu.VMEM((4 * runs, rank, depth), BF16),
            pltpu.SemaphoreType.DMA((4 * runs,)),
            pltpu.SemaphoreType.DMA((4 * runs,)),
        ],
        compiler_params=pltpu.CompilerParams(vmem_limit_bytes=46 * MIB),
        cost_estimate=pl.CostEstimate(
            flops=rows * depth,
            bytes_accessed=rows * depth,
            transcendentals=0,
        ),
        name="shrink_rows",
    )(place, slots, *blocks, scales, gain, down)


def grow_kernel(
    place_ref, slots, s0, s1, up_ref, keep_ref, *refs
):
    *sends, jobs, parts, held, sems = refs
    pieces = len(sends) // 2
    piece = keep_ref.shape[1] // pieces
    runs = held.shape[0] // 4
    rank = held.shape[1]

    def copy(i, slot):
        return pltpu.make_async_copy(up_ref.at[slot], held.at[i], sems.at[i])

    def start(i, d, run, slot):
        copy(i, slot).start()

    def wait(i):
        copy(i, 0).wait()

    def work(members):
        results = []
        for i in members:
            job = jobs[i]
            grown = jnp.dot(parts[job], held[i], preferred_element_type=F32)
            results.append((job, grown))
        for job, grown in results:
            rows = pl.ds(pl.multiple_of((job % runs) * 16, 16), 16)
            slab = job // runs

            @pl.when(slab < 2)
            def _():
                keep_ref[slab, rows, :] = grown

            run = job % runs
            inner = pl.ds(pl.multiple_of(lax.rem(run * 16, piece), 16), 16)
            target = (slab - 2) * pieces + (run * 16) // piece
            for i, send_ref in enumerate(sends):

                @pl.when((slab >= 2) & (target == i))
                def _():
                    send_ref[inner, :] = grown

    count = list_runs(place_ref, slots, runs, jobs, start)
    for slab in range(4):
        for i in range(runs // 2):
            low = slab * runs + i
            both = (s0, s1)[slab // 2][slab % 2, i * 16 : (i + 1) * 16, :]
            parts[low] = both[:, :rank]
            parts[low + runs // 2] = both[:, rank:]
    keep_ref[...] = jnp.zeros_like(keep_ref)
    for send_ref in sends:
        send_ref[...] = jnp.zeros_like(send_ref)
    work_in_teams(count, wait, work)


def grow_rows(place, slots, kept, passed, up, pieces):
    _, pair_rows, _ = kept.shape
    rows = 2 * pair_rows
    rank, columns = up.shape[1:]
    runs = rows // 16
    return pl.pallas_call(
        grow_kernel,
        out_shape=[jax.ShapeDtypeStruct((2, rows, columns), F32)]
        + [jax.ShapeDtypeStruct((rows // pieces, columns), F32)] * (2 * pieces),
        in_specs=[SMEM, SMEM, VMEM, VMEM, HBM],
        out_specs=[VMEM] * (1 + 2 * pieces),
        scratch_shapes=[
            pltpu.SMEM((4 * runs,), jnp.int32),
            pltpu.VMEM((4 * runs, 16, rank), BF16),
            pltpu.VMEM((4 * runs, rank, columns), BF16),
            pltpu.SemaphoreType.DMA((4 * runs,)),
        ],
        compiler_params=pltpu.CompilerParams(vmem_limit_bytes=30 * MIB),
        cost_estimate=pl.CostEstimate(
            flops=rows * columns,
            bytes_accessed=rows * columns,
            transcendentals=0,
        ),
        name="grow_rows",
    )(place, slots, kept, passed, up)


def attend_kernel(
    unit,
    first_row,
    lengths,
    order,
    qkv_ref,
    cos_ref,
    sin_ref,
    cache_ref,
    out_ref,
    queries,
    keys,
    values,
    context,
    held,
    sems,
):
    rows, _, cached, _ = held.shape
    local = STEPS * rows
    q_columns = GROUP * HD
    part = cached // 2
    scale = HD ** (-0.5)
    team = min(4, rows)

    def copy(r, b):
        span = pl.ds(b * part, part)
        return pltpu.make_async_copy(
            cache_ref.at[first_row + r, :, span, :], held.at[r, :, span, :], sems.at[r, b]
        )

    def longest(group):
        return lengths[order[group * team + team - 1]]

    def fetch(i, carry):
        r = order[i]
        copy(r, 0).start()

        @pl.when(longest(i // team) > part)
        def _():
            copy(r, 1).start()

        return carry

    lax.fori_loop(0, rows, fetch, 0)

    cosine = cos_ref[...]
    sine = sin_ref[...]

    def rotated(x):
        x = x.astype(F32)
        turned = x * cosine + pltpu.roll(x, HD // 2, 1) * sine
        return turned.astype(BF16).astype(F32)

    for k in range(KVH):
        for g in range(GROUP):
            queries[k, g * local : (g + 1) * local, :] = rotated(
                qkv_ref[k, :, g * HD : (g + 1) * HD]
            )
        place = q_columns + (k % 2) * HD
        keys[k] = rotated(qkv_ref[k // 2, :, place : place + HD])
        values[k] = qkv_ref[2 + k // 2, :, place : place + HD].astype(F32)

    early = lax.broadcasted_iota(jnp.int32, (4 * GROUP, 1), 0) % (2 * GROUP) < GROUP

    def scores(r, at, pair, span, live):
        heads = (2 * pair, 2 * pair + 1)
        query = [
            jnp.concatenate(
                [queries[k, pl.ds(at[s], GROUP, stride=local), :] for s in range(STEPS)], axis=0
            )
            for k in heads
        ]
        blank = jnp.zeros((2 * GROUP, HD), F32)
        spread = jnp.concatenate(
            [
                jnp.concatenate([query[0], blank], axis=1),
                jnp.concatenate([blank, query[1]], axis=1),
            ],
            axis=0,
        ).astype(BF16)
        old_keys = jnp.concatenate([held[r, k, :span, :HD] for k in heads], axis=1)
        old = lax.dot_general(
            spread, old_keys, (((1,), (1,)), ((), ())), preferred_element_type=F32
        )
        old = jnp.where(live, old * scale, masked)
        fresh = []
        for t in range(STEPS):
            both = jnp.concatenate(
                [
                    jnp.sum(query[i] * keys[k, pl.ds(at[t], 1), :], axis=1, keepdims=True)
                    for i, k in enumerate(heads)
                ],
                axis=0,
            )
            fresh.append(both * scale)
        fresh[1] = jnp.where(early, masked, fresh[1])
        return old, fresh

    def soften(old, fresh):
        peak = jnp.maximum(jnp.max(old, axis=1, keepdims=True), jnp.maximum(fresh[0], fresh[1]))
        p_old = jnp.exp(old - peak)
        p_new = [jnp.exp(f - peak) for f in fresh]
        total = jnp.sum(p_old, axis=1, keepdims=True) + (p_new[0] + p_new[1])
        return p_old.astype(BF16), [p.astype(BF16).astype(F32) for p in p_new], total

    def mix(r, at, pair, span, w_old, w_new, total):
        heads = (2 * pair, 2 * pair + 1)
        old_values = jnp.concatenate([held[r, k, :span, HD:] for k in heads], axis=1)
        mixed = jnp.dot(w_old, old_values, preferred_element_type=F32)
        for i, k in enumerate(heads):
            own = slice(i * 2 * GROUP, (i + 1) * 2 * GROUP)
            result = mixed[own, i * HD : (i + 1) * HD]
            for t in range(STEPS):
                result = result + w_new[t][own] * values[k, pl.ds(at[t], 1), :]
            result = result / total[own]
            for s in range(STEPS):
                context[k, pl.ds(at[s], GROUP, stride=local), :] = result[
                    s * GROUP : (s + 1) * GROUP
                ]

    def attend_team(members, span):
        jobs = []
        for r in members:
            at = [(r // unit) * (STEPS * unit) + s * unit + r % unit for s in range(STEPS)]
            live = lax.broadcasted_iota(jnp.int32, (4 * GROUP, span), 1) < lengths[r]
            for pair in range(KVH // 2):
                jobs.append((r, at, pair, scores(r, at, pair, span, live)))
        softened = [soften(*job[3]) for job in jobs]
        for (r, at, pair, _), weights in zip(jobs, softened):
            mix(r, at, pair, span, *weights)

    def each(group, carry):
        members = [order[group * team + i] for i in range(team)]
        wide = longest(group) > part
        for r in members:
            copy(r, 0).wait()

        @pl.when(wide)
        def _():
            for r in members:
                copy(r, 1).wait()
            attend_team(members, cached)

        @pl.when(jnp.logical_not(wide))
        def _():
            attend_team(members, part)

        return carry

    lax.fori_loop(0, rows // team, each, 0)
    for k in range(KVH):
        for g in range(GROUP):
            place = (k * GROUP + g) * HD
            out_ref[:, place : place + HD] = context[k, g * local : (g + 1) * local, :].astype(BF16)


def attend(lengths, order, qkv, cosine, sine, cache, first_row, unit):
    rows = lengths.shape[0]
    local = STEPS * rows
    _, kv_heads, cached, width = cache.shape
    return pl.pallas_call(
        functools.partial(attend_kernel, unit, first_row),
        out_shape=jax.ShapeDtypeStruct((local, HEADS * HD), BF16),
        in_specs=[SMEM, SMEM, VMEM, VMEM, VMEM, HBM],
        out_specs=VMEM,
        scratch_shapes=[
            pltpu.VMEM((KVH, GROUP * local, HD), F32),
            pltpu.VMEM((KVH, local, HD), F32),
            pltpu.VMEM((KVH, local, HD), F32),
            pltpu.VMEM((KVH, GROUP * local, HD), F32),
            pltpu.VMEM((rows, kv_heads, cached, width), BF16),
            pltpu.SemaphoreType.DMA((rows, 2)),
        ],
        compiler_params=pltpu.CompilerParams(vmem_limit_bytes=28 * MIB),
        cost_estimate=pl.CostEstimate(
            flops=4 * local * HEADS * HD * cached,
            bytes_accessed=2 * rows * kv_heads * cached * width,
            transcendentals=local * HEADS * cached,
        ),
        name="attend",
    )(lengths, order, qkv, cosine, sine, cache)


def out_kernel(count, has_earlier, owners, *refs):
    blocks = refs[:count]
    w_ref = refs[count]
    if has_earlier:
        out_ref, lhs, total = refs[-3:]
    else:
        out_ref, lhs, total, held, sems = refs[-5:]
        tiles, tile, _ = held.shape
        copies = [
            pltpu.make_async_copy(w_ref.at[pl.ds(k * tile, tile), :], held.at[k], sems.at[k])
            for k in range(tiles)
        ]
        for copy in copies:
            copy.start()
    local, depth = blocks[0].shape
    rows = local // STEPS
    columns = w_ref.shape[1]
    halves = out_ref.shape[2]
    slots = count // halves

    def place(j):
        used = jnp.int32(0)
        for i in range(j % slots):
            used = used + (owners[i] >= 0).astype(jnp.int32)
        return (j // slots) * (lhs.shape[0] // halves) + used * local

    lhs[...] = jnp.zeros_like(lhs)
    for j, ref in enumerate(blocks):

        @pl.when(owners[j % slots] >= 0)
        def _():
            lhs[pl.ds(pl.multiple_of(place(j), local), local), :] = ref[...]

    if has_earlier:
        out_ref[...] = refs[count + 1][...]
    width = min(512, columns)
    spans = [slice(j * width, (j + 1) * width) for j in range(columns // width)]
    if has_earlier:
        for span in spans:
            total[:, span] = jnp.dot(lhs[...], w_ref[:, span], preferred_element_type=F32)
    else:
        for k, copy in enumerate(copies):
            copy.wait()
            part = lhs[:, k * tile : (k + 1) * tile]
            for span in spans:
                product = jnp.dot(part, held[k, :, span], preferred_element_type=F32)
                total[:, span] = product if k == 0 else total[:, span] + product
    for j in range(count):

        @pl.when(owners[j % slots] >= 0)
        def _():
            block = total[pl.ds(pl.multiple_of(place(j), local), local), :]
            block = block.reshape(rows // RUN, STEPS, RUN, columns)
            for s in range(STEPS):
                piece = block[:, s].reshape(rows, columns).astype(BF16)
                out_ref[s, owners[j % slots], j // slots] = piece


def project(owners, blocks, weight, present, earlier=None):
    halves = len(blocks)
    flat = [block for part in blocks for block in part]
    local, depth = flat[0].shape
    columns = weight.shape[1]
    rows = local // STEPS
    count = len(flat)
    more = [] if earlier is None else [earlier]
    tile = min(512, depth)
    streamed = [
        pltpu.VMEM((depth // tile, tile, columns), BF16),
        pltpu.SemaphoreType.DMA((depth // tile,)),
    ]
    return pl.pallas_call(
        functools.partial(out_kernel, count, earlier is not None),
        out_shape=jax.ShapeDtypeStruct((STEPS, 4, halves, rows, columns), BF16),
        in_specs=[SMEM] + [VMEM] * count + [VMEM if more else HBM] + [VMEM] * len(more),
        out_specs=VMEM,
        scratch_shapes=[
            pltpu.VMEM((present * halves * local, depth), BF16),
            pltpu.VMEM((present * halves * local, columns), F32),
        ]
        + ([] if more else streamed),
        compiler_params=pltpu.CompilerParams(vmem_limit_bytes=(24 if more else 28) * MIB),
        cost_estimate=pl.CostEstimate(
            flops=2 * present * halves * local * depth * columns,
            bytes_accessed=2 * depth * columns + 4 * present * local * (depth + columns),
            transcendentals=0,
        ),
        name="project",
    )(owners, *flat, weight, *more)


def lookup(identity, table):
    hits = identity[:, None] == jnp.arange(table.shape[0], dtype=jnp.int32)[None, :]
    return jnp.sum(jnp.where(hits, table[None, :], 0), axis=1)


def ascending(lengths):
    count = lengths.shape[0]
    rows = jnp.arange(count, dtype=jnp.int32)
    keyed = lengths * count + rows
    rank = jnp.sum((keyed[None, :] < keyed[:, None]).astype(jnp.int32), axis=1)
    return jnp.sum(jnp.where(rank[:, None] == rows[None, :], rows[:, None], 0), axis=0)


def angle_tables(lengths, unit):
    steps = jnp.arange(STEPS, dtype=jnp.int32)
    position = lengths.reshape(-1, 1, unit) + steps[None, :, None]
    freq = rope_base ** (-(jnp.arange(HD // 2, dtype=F32) * 2.0 / HD))
    angles = position.reshape(-1).astype(F32)[:, None] * freq
    cosine = jnp.cos(angles)
    sine = jnp.sin(angles)
    return jnp.concatenate([cosine, cosine], 1), jnp.concatenate([-sine, sine], 1)


def on_device(
    hidden,
    input_norm_scale,
    query_key_value_weight,
    output_weight,
    adapter_down_weight,
    adapter_up_weight,
    row_adapter_index,
    adapter_store_slot,
    lengths,
    key_value_cache,
):
    tensor_count = lax.axis_size("tensor")
    tensor_pos = lax.axis_index("tensor")
    store_pos = lax.axis_index("store")
    _, rows, span = hidden.shape
    model_width = input_norm_scale.shape[0]
    rows_here = lengths.shape[0]
    unit = min(RUN, rows_here)
    line = tensor_count == 4 and rows_here % (HALVES * RUN) == 0
    halves = HALVES if line else 1
    part_rows = rows_here // halves
    local = STEPS * part_rows
    held_slots = adapter_down_weight.shape[0]
    rank = adapter_down_weight.shape[2]

    raw = hidden.reshape(STEPS, tensor_count, halves, part_rows // unit, unit, span)
    raw = raw.transpose(2, 1, 3, 0, 4, 5).reshape(STEPS * rows, span)
    own_index = tensor_pos.reshape(1).astype(jnp.int32)
    owners = [own_index] + [hop_owners(tensor_pos, hop) for hop in (1, 2, 3)]
    count = tensor_count * local
    parts = [slice(h * count, (h + 1) * count) for h in range(halves)]
    values = raw.astype(F32)
    squares = jnp.sum(values * values, axis=1)
    if line:
        squares = squares + sum(swap(squares, "tensor", d) for d in (1, 2, 3))
        travelling, squares = lax.optimization_barrier((raw, squares))
        hop1 = line_hop(travelling, travelling, "tensor", 1)
    else:
        squares = summed_over(squares, "tensor")
    own_runs = row_adapter_index[::RUN]
    if halves > 1:
        own_runs = own_runs.reshape(tensor_count, halves, -1).swapaxes(0, 1).reshape(-1)
    told = jnp.concatenate([squares, own_runs.astype(F32)]).reshape(1, -1)
    told = jnp.concatenate([told, swap(told, "store", 2)], axis=0)
    if line:
        told, hop1 = lax.optimization_barrier((told, hop1))
        hop2 = line_hop(*hop1, "tensor", 2)
    told = jnp.concatenate([told, swap(told, "store", 1)], axis=0)
    told = jnp.stack([told[d] for d in (0, 2, 1, 3)])
    told = jnp.stack([jnp.stack([told[p ^ q] for q in range(4)]) for p in range(4)])
    told = lax.dynamic_index_in_dim(told, store_pos, 0, keepdims=False)
    runs = told[:, STEPS * rows :].astype(jnp.int32)
    told = told[:, : STEPS * rows]
    scales = lax.rsqrt(told / model_width + eps_norm)
    slots = lookup(runs.reshape(-1), adapter_store_slot).reshape(runs.shape)
    slots = jnp.where(slots // held_slots == store_pos, slots % held_slots, -1)
    place = store_pos.reshape(1).astype(jnp.int32)
    gains = input_norm_scale.reshape(1, -1)
    gain = lax.dynamic_slice_in_dim(gains, tensor_pos * span, span, 1)
    scales = scales[:, :, None]
    own_scale = lax.dynamic_index_in_dim(scales, store_pos, 0, keepdims=False)

    across = swap(raw, "store", 2)
    beside = swap(raw, "store", 1)
    diagonal = swap(across, "store", 1)
    mine = slots.reshape(-1)
    down = jnp.swapaxes(adapter_down_weight, 1, 2)
    kept, passed = shrink_rows(place, mine, (raw, beside, across, diagonal), scales, gain, down)
    kept = kept + swap(passed, "store", 1)
    shrunk = kept[0] + swap(kept[1], "store", 2)
    if line:
        shrunk, early = lax.optimization_barrier((shrunk, (raw,) + hop1))
        near = jnp.concatenate(owners[:2])
        total = base_block(early, own_scale, gains, query_key_value_weight, near, (0,) * 3, 3)
        shrunk = shrunk + swap(shrunk, "tensor", 1)
        shrunk, total, hop2 = lax.optimization_barrier((shrunk, total, hop2))
        sent = [(hop2[0][part], hop2[1][part]) for part in parts]
        shrunk = shrunk + swap(shrunk, "tensor", 2)
        shrunk, sent = lax.optimization_barrier((shrunk, sent))
        hop3 = [line_hop(up, down, "tensor", 3) for up, down in sent]
    else:
        shrunk = summed_over(shrunk, "tensor")
    shrunk = shrunk.astype(BF16)
    shrunk = jnp.stack([shrunk, swap(shrunk, "store", 2)])
    other = swap(shrunk, "store", 1)
    kept, *passed = grow_rows(place, mine, shrunk, other, adapter_up_weight, 1)
    if line:
        passed, hop3[0] = lax.optimization_barrier((passed, hop3[0]))
    passed = [swap(piece, "store", 1) for piece in passed]
    leaving = [(kept[1, part] + passed[1][part]).astype(F16) for part in parts]
    arrived = [swap(piece, "store", 2).astype(F32) for piece in leaving]
    deltas = [(kept[0, p] + passed[0][p]) + far for p, far in zip(parts, arrived)]

    weight = query_key_value_weight
    mixed = []
    if line:
        total, leaving = lax.optimization_barrier((total, leaving))
        far = jnp.concatenate(owners[2:])
        for h, part in enumerate(parts):
            if mixed:
                far, mixed[-1] = lax.optimization_barrier((far, mixed[-1]))
            blocks = hop2 + hop3[h]
            first_rows = (h * count, h * count, 0, 0)
            sums = base_block(
                blocks, own_scale[part], gains, weight, far, first_rows, 2, total[part]
            )
            mixed.append((sums + deltas[h]).astype(BF16))
    else:
        everything = lax.all_gather(raw, "tensor", axis=0, tiled=False)
        own = base_block((raw,), own_scale, gains, weight, own_index, (0,), 1)
        total = base_rows(own_index, everything, own_scale, gains, own, weight, 0)
        mixed.append((total + deltas[0]).astype(BF16))
    mixed = [qkv.reshape(tensor_count, local, -1) for qkv in mixed]

    contexts = []
    exchanged = []
    for qkv in mixed:
        if exchanged:
            qkv, exchanged[-1] = lax.optimization_barrier((qkv, exchanged[-1]))
        exchanged.append(lax.all_to_all(qkv, "tensor", 0, 0, tiled=True))
    for h, moved in enumerate(exchanged):
        if tensor_count != 4:
            q_columns = HEADS * HD // tensor_count
            pieces = []
            for piece in (moved[..., :q_columns], moved[..., q_columns:]):
                joined = piece.transpose(1, 0, 2).reshape(local, 4, -1)
                pieces.append(joined.transpose(1, 0, 2))
            moved = jnp.concatenate(pieces, axis=2)
        here = lengths[h * part_rows : (h + 1) * part_rows]
        cosine, sine = angle_tables(here, unit)
        contexts.append(
            attend(here, ascending(here), moved, cosine, sine, key_value_cache, h * part_rows, unit)
        )

    if line:
        hops = [line_gather(context, "tensor") for context in contexts]
        first = [(context,) + hop[0] for context, hop in zip(contexts, hops)]
        last = [hop[1] + hop[2] for hop in hops]
        output = project(jnp.concatenate(owners[:2]), first, output_weight, 3)
        output = project(jnp.concatenate(owners[2:]), last, output_weight, 2, output)
    else:
        results = []
        for context in contexts:
            context = lax.all_gather(context, "tensor", axis=0, tiled=True)
            result = jnp.dot(context, output_weight, preferred_element_type=F32).astype(BF16)
            result = result.reshape(tensor_count, part_rows // unit, STEPS, unit, -1)
            result = result.transpose(2, 0, 1, 3, 4).reshape(STEPS, tensor_count, part_rows, -1)
            results.append(result)
        output = jnp.stack(results, axis=2)
    return output.reshape(STEPS, rows, -1)


def solution(mesh):
    in_specs = (
        P(None, ("groups", "store"), "tensor"),
        P(),
        P(None, "tensor"),
        P(None, "tensor"),
        P(("groups", "store"), "tensor", None),
        P(("groups", "store"), None, "tensor"),
        P(("groups", "store")),
        P("groups"),
        P(("groups", "store", "tensor")),
        P(("groups", "store", "tensor"), None, None, None),
    )
    out_specs = P(None, ("groups", "store"), "tensor")
    return jax.shard_map(
        on_device, mesh=mesh, in_specs=in_specs, out_specs=out_specs, check_vma=False
    )
```

```python
import functools

import jax
import jax.numpy as jnp
from jax import lax
from jax.experimental import pallas as pl
from jax.experimental.pallas import tpu as pltpu
from jax.sharding import PartitionSpec as P

HEADS = 32
KVH = 4
HD = 128
GROUP = HEADS // KVH
RUN = 8
STEPS = 2
LANES = 128
HALVES = 2

eps_norm = 1e-05
rope_base = 500000.0
masked = -1e30

MIB = 1 << 20
F32 = jnp.float32
BF16 = jnp.bfloat16
F16 = jnp.float16
VMEM = pl.BlockSpec(memory_space=pltpu.VMEM)
SMEM = pl.BlockSpec(memory_space=pltpu.SMEM)
HBM = pl.BlockSpec(memory_space=pltpu.HBM)
ANY = pl.BlockSpec(memory_space=pl.ANY)


def swap(values, axis, distance):
    count = lax.axis_size(axis)
    return lax.ppermute(values, axis, [(i, i ^ distance) for i in range(count)])


def summed_over(values, axis):
    distance = 1
    while distance < lax.axis_size(axis):
        values = values + swap(values, axis, distance)
        distance *= 2
    return values


def line_hop(up, down, axis, hop):
    up = lax.ppermute(up, axis, [(i, i + 1) for i in range(hop - 1, 3)])
    down = lax.ppermute(down, axis, [(i, i - 1) for i in range(4 - hop, 0, -1)])
    return up, down


def line_gather(block, axis):
    hops = [line_hop(block, block, axis, 1)]
    for hop in (2, 3):
        hops.append(line_hop(*hops[-1], axis, hop))
    return hops


def hop_owners(position, hop):
    below = position - hop
    above = position + hop
    return jnp.stack([jnp.where(below >= 0, below, -1), jnp.where(above < 4, above, -1)])


def block_kernel(first_rows, has_total, owners, *refs):
    count = len(first_rows)
    x_refs = refs[:count]
    scale_ref, gain_ref, w_ref = refs[count : count + 3]
    out_ref, held_x, held, x_sems, sems = refs[-5:]
    rows = scale_ref.shape[0]
    _, tiles, depth, _ = held.shape

    def slot(j):
        used = jnp.int32(0)
        for i in range(j):
            used = used + (owners[i] >= 0).astype(jnp.int32)
        return used

    def copy(j, k):
        first = pl.multiple_of((owners[j] * tiles + k) * depth, depth)
        return pltpu.make_async_copy(
            w_ref.at[pl.ds(first, depth), :], held.at[slot(j), k], sems.at[slot(j), k]
        )

    def x_copy(j):
        part = x_refs[j].at[first_rows[j] : first_rows[j] + rows, :]
        return pltpu.make_async_copy(part, held_x.at[slot(j)], x_sems.at[slot(j)])

    for j in range(count):

        @pl.when(owners[j] >= 0)
        def _():
            x_copy(j).start()
            for k in range(tiles):
                copy(j, k).start()

    out_ref[...] = refs[count + 3][...] if has_total else jnp.zeros_like(out_ref)
    for j in range(count):

        @pl.when(owners[j] >= 0)
        def _():
            scale = scale_ref[...]
            x_copy(j).wait()
            for k in range(tiles):
                span = slice(k * depth, (k + 1) * depth)
                first = pl.multiple_of((owners[j] * tiles + k) * depth, depth)
                gain = gain_ref[:, pl.ds(first, depth)]
                part = held_x[slot(j), :, span].astype(F32)
                normed = (part * scale * gain).astype(BF16)
                copy(j, k).wait()
                out_ref[...] += jnp.dot(normed, held[slot(j), k], preferred_element_type=F32)


def base_block(blocks, scale, gain, weight, owners, first_rows, present, total=None):
    depth = blocks[0].shape[1]
    rows = scale.shape[0]
    columns = weight.shape[1]
    tile = min(512, depth)
    count = len(blocks)
    more = [] if total is None else [total]
    return pl.pallas_call(
        functools.partial(block_kernel, first_rows, total is not None),
        out_shape=jax.ShapeDtypeStruct((rows, columns), F32),
        in_specs=[SMEM] + [ANY] * count + [VMEM] * 2 + [HBM] + [VMEM] * len(more),
        out_specs=VMEM,
        scratch_shapes=[
            pltpu.VMEM((present, rows, depth), BF16),
            pltpu.VMEM((present, depth // tile, tile, columns), BF16),
            pltpu.SemaphoreType.DMA((present,)),
            pltpu.SemaphoreType.DMA((present, depth // tile)),
        ],
        compiler_params=pltpu.CompilerParams(vmem_limit_bytes=46 * MIB),
        cost_estimate=pl.CostEstimate(
            flops=rows * columns,
            bytes_accessed=rows * columns,
            transcendentals=0,
        ),
        name="base_block",
    )(owners, *blocks, scale, gain, weight, *more)


def base_kernel(first_row, place_ref, x_ref, scale_ref, gain_ref, own_ref, w_ref, out_ref, held, sems):
    owners, _, span = x_ref.shape
    rows = scale_ref.shape[0]
    tiles, depth, _ = held.shape
    tiles_each = span // depth

    def spot(k):
        owner = lax.rem(place_ref[0] + 1 + k // tiles_each, owners)
        return owner, pl.multiple_of((owner * tiles_each + k % tiles_each) * depth, depth)

    copies = [
        pltpu.make_async_copy(w_ref.at[pl.ds(spot(k)[1], depth), :], held.at[k], sems.at[k])
        for k in range(tiles)
    ]
    for copy in copies:
        copy.start()
    scale = scale_ref[...]
    out_ref[...] = own_ref[first_row : first_row + rows, :]
    for k, copy in enumerate(copies):
        owner, first = spot(k)
        inner = (k % tiles_each) * depth
        gain = gain_ref[:, pl.ds(first, depth)]
        part = x_ref[owner, first_row : first_row + rows, inner : inner + depth].astype(F32)
        normed = (part * scale * gain).astype(BF16)
        copy.wait()
        out_ref[...] += jnp.dot(normed, held[k], preferred_element_type=F32)


def base_rows(place, x, scale, gain, own, weight, first_row):
    owners, _, span = x.shape
    rows = scale.shape[0]
    columns = weight.shape[1]
    tile = min(512, span)
    tiles = (owners - 1) * span // tile
    return pl.pallas_call(
        functools.partial(base_kernel, first_row),
        out_shape=jax.ShapeDtypeStruct((rows, columns), F32),
        in_specs=[SMEM] + [VMEM] * 4 + [HBM],
        out_specs=VMEM,
        scratch_shapes=[
            pltpu.VMEM((tiles, tile, columns), BF16),
            pltpu.SemaphoreType.DMA((tiles,)),
        ],
        compiler_params=pltpu.CompilerParams(vmem_limit_bytes=48 * MIB),
        cost_estimate=pl.CostEstimate(
            flops=2 * rows * tiles * tile * columns,
            bytes_accessed=2 * tiles * tile * (rows + columns) + 8 * rows * columns,
            transcendentals=0,
        ),
        name="base_rows",
    )(place, x, scale, gain, own, weight)


TEAM = 4
SLABS = (0, 2, 1, 3)


def list_runs(place_ref, slots, runs, jobs, start):
    def look(run, carry, slab, d):
        slot = slots[(place_ref[0] ^ d) * runs + run]

        @pl.when(slot >= 0)
        def _():
            jobs[carry] = slab * runs + run
            start(carry, d, run, slot)

        return carry + (slot >= 0).astype(jnp.int32)

    count = jnp.int32(0)
    for slab, d in enumerate(SLABS):
        count = lax.fori_loop(0, runs, functools.partial(look, slab=slab, d=d), count)
    return count


def work_in_teams(count, wait, work):
    def team(g, carry):
        for u in range(TEAM):

            @pl.when(g * TEAM + u < count)
            def _():
                wait(g * TEAM + u)

        work([jnp.minimum(g * TEAM + u, count - 1) for u in range(TEAM)])
        return carry

    lax.fori_loop(0, (count + TEAM - 1) // TEAM, team, 0)


def shrink_kernel(
    place_ref,
    slots,
    x0,
    x1,
    x2,
    x3,
    scale_ref,
    gain_ref,
    down_ref,
    keep_ref,
    send_ref,
    jobs,
    parts,
    held_x,
    held,
    x_sems,
    sems,
):
    runs = held.shape[0] // 4
    rank = held.shape[1]
    x_refs = (x0, x1, x2, x3)

    def x_copy(i, d, run):
        rows = pl.ds(pl.multiple_of(run * 16, 16), 16)
        return pltpu.make_async_copy(x_refs[d].at[rows, :], held_x.at[i], x_sems.at[i])

    def copy(i, slot):
        return pltpu.make_async_copy(down_ref.at[slot], held.at[i], sems.at[i])

    def start(i, d, run, slot):
        copy(i, slot).start()
        x_copy(i, d, run).start()

    def wait(i):
        copy(i, 0).wait()
        x_copy(i, 0, 0).wait()

    def work(members):
        results = []
        for i in members:
            job = jobs[i]
            slab = job // runs
            d = jnp.where(slab == 1, 2, jnp.where(slab == 2, 1, slab))
            rows = pl.ds(pl.multiple_of((job % runs) * 16, 16), 16)
            scale = scale_ref[place_ref[0] ^ d, rows, :]
            normed = (held_x[i].astype(F32) * scale * gain_ref[...]).astype(BF16)
            part = lax.dot_general(
                normed, held[i], (((1,), (1,)), ((), ())), preferred_element_type=F32
            )
            results.append((job, part))
        for job, part in results:
            parts[job] = part

    count = list_runs(place_ref, slots, runs, jobs, start)
    parts[...] = jnp.zeros_like(parts)
    work_in_teams(count, wait, work)
    for slab in range(4):
        for i in range(runs // 2):
            low = slab * runs + i
            out_ref = (keep_ref, send_ref)[slab // 2]
            out_ref[slab % 2, i * 16 : (i + 1) * 16, :] = jnp.concatenate(
                [parts[low], parts[low + runs // 2]], axis=1
            )


def shrink_rows(place, slots, blocks, scales, gain, down):
    rows, depth = blocks[0].shape
    rank = down.shape[1]
    runs = rows // 16
    return pl.pallas_call(
        shrink_kernel,
        out_shape=[jax.ShapeDtypeStruct((2, rows // 2, 2 * rank), F32)] * 2,
        in_specs=[SMEM] * 2 + [ANY] * 4 + [VMEM] * 2 + [HBM],
        out_specs=[VMEM] * 2,
        scratch_shapes=[
            pltpu.SMEM((4 * runs,), jnp.int32),
            pltpu.VMEM((4 * runs, 16, rank), F32),
            pltpu.VMEM((4 * runs, 16, depth), BF16),
            pltpu.VMEM((4 * runs, rank, depth), BF16),
            pltpu.SemaphoreType.DMA((4 * runs,)),
            pltpu.SemaphoreType.DMA((4 * runs,)),
        ],
        compiler_params=pltpu.CompilerParams(vmem_limit_bytes=48 * MIB),
        cost_estimate=pl.CostEstimate(
            flops=rows * depth,
            bytes_accessed=rows * depth,
            transcendentals=0,
        ),
        name="shrink_rows",
    )(place, slots, *blocks, scales, gain, down)


def grow_kernel(
    place_ref, slots, s0, s1, up_ref, keep_ref, *refs
):
    *sends, jobs, parts, held, sems = refs
    pieces = len(sends) // 2
    piece = keep_ref.shape[1] // pieces
    runs = held.shape[0] // 4
    rank = held.shape[1]

    def copy(i, slot):
        return pltpu.make_async_copy(up_ref.at[slot], held.at[i], sems.at[i])

    def start(i, d, run, slot):
        copy(i, slot).start()

    def wait(i):
        copy(i, 0).wait()

    def work(members):
        results = []
        for i in members:
            job = jobs[i]
            grown = jnp.dot(parts[job], held[i], preferred_element_type=F32)
            results.append((job, grown))
        for job, grown in results:
            rows = pl.ds(pl.multiple_of((job % runs) * 16, 16), 16)
            slab = job // runs

            @pl.when(slab < 2)
            def _():
                keep_ref[slab, rows, :] = grown

            run = job % runs
            inner = pl.ds(pl.multiple_of(lax.rem(run * 16, piece), 16), 16)
            target = (slab - 2) * pieces + (run * 16) // piece
            for i, send_ref in enumerate(sends):

                @pl.when((slab >= 2) & (target == i))
                def _():
                    send_ref[inner, :] = grown

    count = list_runs(place_ref, slots, runs, jobs, start)
    for slab in range(4):
        for i in range(runs // 2):
            low = slab * runs + i
            both = (s0, s1)[slab // 2][slab % 2, i * 16 : (i + 1) * 16, :]
            parts[low] = both[:, :rank]
            parts[low + runs // 2] = both[:, rank:]
    keep_ref[...] = jnp.zeros_like(keep_ref)
    for send_ref in sends:
        send_ref[...] = jnp.zeros_like(send_ref)
    work_in_teams(count, wait, work)


def grow_rows(place, slots, kept, passed, up, pieces):
    _, pair_rows, _ = kept.shape
    rows = 2 * pair_rows
    rank, columns = up.shape[1:]
    runs = rows // 16
    return pl.pallas_call(
        grow_kernel,
        out_shape=[jax.ShapeDtypeStruct((2, rows, columns), F32)]
        + [jax.ShapeDtypeStruct((rows // pieces, columns), F32)] * (2 * pieces),
        in_specs=[SMEM, SMEM, VMEM, VMEM, HBM],
        out_specs=[VMEM] * (1 + 2 * pieces),
        scratch_shapes=[
            pltpu.SMEM((4 * runs,), jnp.int32),
            pltpu.VMEM((4 * runs, 16, rank), BF16),
            pltpu.VMEM((4 * runs, rank, columns), BF16),
            pltpu.SemaphoreType.DMA((4 * runs,)),
        ],
        compiler_params=pltpu.CompilerParams(vmem_limit_bytes=48 * MIB),
        cost_estimate=pl.CostEstimate(
            flops=rows * columns,
            bytes_accessed=rows * columns,
            transcendentals=0,
        ),
        name="grow_rows",
    )(place, slots, kept, passed, up)


def attend_kernel(
    unit,
    first_row,
    lengths,
    order,
    qkv_ref,
    cos_ref,
    sin_ref,
    cache_ref,
    out_ref,
    queries,
    keys,
    values,
    context,
    held,
    sems,
):
    rows, _, cached, _ = held.shape
    local = STEPS * rows
    q_columns = GROUP * HD
    part = cached // 2
    scale = HD ** (-0.5)
    team = min(4, rows)

    def copy(r, b):
        span = pl.ds(b * part, part)
        return pltpu.make_async_copy(
            cache_ref.at[first_row + r, :, span, :], held.at[r, :, span, :], sems.at[r, b]
        )

    def longest(group):
        return lengths[order[group * team + team - 1]]

    def fetch(i, carry):
        r = order[i]
        copy(r, 0).start()

        @pl.when(longest(i // team) > part)
        def _():
            copy(r, 1).start()

        return carry

    lax.fori_loop(0, rows, fetch, 0)

    cosine = cos_ref[...]
    sine = sin_ref[...]

    def rotated(x):
        x = x.astype(F32)
        turned = x * cosine + pltpu.roll(x, HD // 2, 1) * sine
        return turned.astype(BF16).astype(F32)

    for k in range(KVH):
        for g in range(GROUP):
            queries[k, g * local : (g + 1) * local, :] = rotated(
                qkv_ref[k, :, g * HD : (g + 1) * HD]
            )
        place = q_columns + (k % 2) * HD
        keys[k] = rotated(qkv_ref[k // 2, :, place : place + HD])
        values[k] = qkv_ref[2 + k // 2, :, place : place + HD].astype(F32)

    early = lax.broadcasted_iota(jnp.int32, (4 * GROUP, 1), 0) % (2 * GROUP) < GROUP

    def scores(r, at, pair, span, live):
        heads = (2 * pair, 2 * pair + 1)
        query = [
            jnp.concatenate(
                [queries[k, pl.ds(at[s], GROUP, stride=local), :] for s in range(STEPS)], axis=0
            )
            for k in heads
        ]
        blank = jnp.zeros((2 * GROUP, HD), F32)
        spread = jnp.concatenate(
            [
                jnp.concatenate([query[0], blank], axis=1),
                jnp.concatenate([blank, query[1]], axis=1),
            ],
            axis=0,
        ).astype(BF16)
        old_keys = jnp.concatenate([held[r, k, :span, :HD] for k in heads], axis=1)
        old = lax.dot_general(
            spread, old_keys, (((1,), (1,)), ((), ())), preferred_element_type=F32
        )
        old = jnp.where(live, old * scale, masked)
        fresh = []
        for t in range(STEPS):
            both = jnp.concatenate(
                [
                    jnp.sum(query[i] * keys[k, pl.ds(at[t], 1), :], axis=1, keepdims=True)
                    for i, k in enumerate(heads)
                ],
                axis=0,
            )
            fresh.append(both * scale)
        fresh[1] = jnp.where(early, masked, fresh[1])
        return old, fresh

    def soften(old, fresh):
        peak = jnp.maximum(jnp.max(old, axis=1, keepdims=True), jnp.maximum(fresh[0], fresh[1]))
        p_old = jnp.exp(old - peak)
        p_new = [jnp.exp(f - peak) for f in fresh]
        total = jnp.sum(p_old, axis=1, keepdims=True) + (p_new[0] + p_new[1])
        return p_old.astype(BF16), [p.astype(BF16).astype(F32) for p in p_new], total

    def mix(r, at, pair, span, w_old, w_new, total):
        heads = (2 * pair, 2 * pair + 1)
        old_values = jnp.concatenate([held[r, k, :span, HD:] for k in heads], axis=1)
        mixed = jnp.dot(w_old, old_values, preferred_element_type=F32)
        for i, k in enumerate(heads):
            own = slice(i * 2 * GROUP, (i + 1) * 2 * GROUP)
            result = mixed[own, i * HD : (i + 1) * HD]
            for t in range(STEPS):
                result = result + w_new[t][own] * values[k, pl.ds(at[t], 1), :]
            result = result / total[own]
            for s in range(STEPS):
                context[k, pl.ds(at[s], GROUP, stride=local), :] = result[
                    s * GROUP : (s + 1) * GROUP
                ]

    def attend_team(members, span):
        jobs = []
        for r in members:
            at = [(r // unit) * (STEPS * unit) + s * unit + r % unit for s in range(STEPS)]
            live = lax.broadcasted_iota(jnp.int32, (4 * GROUP, span), 1) < lengths[r]
            for pair in range(KVH // 2):
                jobs.append((r, at, pair, scores(r, at, pair, span, live)))
        softened = [soften(*job[3]) for job in jobs]
        for (r, at, pair, _), weights in zip(jobs, softened):
            mix(r, at, pair, span, *weights)

    def each(group, carry):
        members = [order[group * team + i] for i in range(team)]
        wide = longest(group) > part
        for r in members:
            copy(r, 0).wait()

        @pl.when(wide)
        def _():
            for r in members:
                copy(r, 1).wait()
            attend_team(members, cached)

        @pl.when(jnp.logical_not(wide))
        def _():
            attend_team(members, part)

        return carry

    lax.fori_loop(0, rows // team, each, 0)
    for k in range(KVH):
        for g in range(GROUP):
            place = (k * GROUP + g) * HD
            out_ref[:, place : place + HD] = context[k, g * local : (g + 1) * local, :].astype(BF16)


def attend(lengths, order, qkv, cosine, sine, cache, first_row, unit):
    rows = lengths.shape[0]
    local = STEPS * rows
    _, kv_heads, cached, width = cache.shape
    return pl.pallas_call(
        functools.partial(attend_kernel, unit, first_row),
        out_shape=jax.ShapeDtypeStruct((local, HEADS * HD), BF16),
        in_specs=[SMEM, SMEM, VMEM, VMEM, VMEM, HBM],
        out_specs=VMEM,
        scratch_shapes=[
            pltpu.VMEM((KVH, GROUP * local, HD), F32),
            pltpu.VMEM((KVH, local, HD), F32),
            pltpu.VMEM((KVH, local, HD), F32),
            pltpu.VMEM((KVH, GROUP * local, HD), F32),
            pltpu.VMEM((rows, kv_heads, cached, width), BF16),
            pltpu.SemaphoreType.DMA((rows, 2)),
        ],
        compiler_params=pltpu.CompilerParams(vmem_limit_bytes=28 * MIB),
        cost_estimate=pl.CostEstimate(
            flops=4 * local * HEADS * HD * cached,
            bytes_accessed=2 * rows * kv_heads * cached * width,
            transcendentals=local * HEADS * cached,
        ),
        name="attend",
    )(lengths, order, qkv, cosine, sine, cache)


def out_kernel(count, has_earlier, owners, *refs):
    blocks = refs[:count]
    w_ref = refs[count]
    if has_earlier:
        out_ref, lhs, total = refs[-3:]
    else:
        out_ref, lhs, total, held, sems = refs[-5:]
        tiles, tile, _ = held.shape
        copies = [
            pltpu.make_async_copy(w_ref.at[pl.ds(k * tile, tile), :], held.at[k], sems.at[k])
            for k in range(tiles)
        ]
        for copy in copies:
            copy.start()
    local, depth = blocks[0].shape
    rows = local // STEPS
    columns = w_ref.shape[1]
    halves = out_ref.shape[2]
    slots = count // halves

    def place(j):
        used = jnp.int32(0)
        for i in range(j % slots):
            used = used + (owners[i] >= 0).astype(jnp.int32)
        return (j // slots) * (lhs.shape[0] // halves) + used * local

    lhs[...] = jnp.zeros_like(lhs)
    for j, ref in enumerate(blocks):

        @pl.when(owners[j % slots] >= 0)
        def _():
            lhs[pl.ds(pl.multiple_of(place(j), local), local), :] = ref[...]

    if has_earlier:
        out_ref[...] = refs[count + 1][...]
    width = min(512, columns)
    spans = [slice(j * width, (j + 1) * width) for j in range(columns // width)]
    if has_earlier:
        for span in spans:
            total[:, span] = jnp.dot(lhs[...], w_ref[:, span], preferred_element_type=F32)
    else:
        for k, copy in enumerate(copies):
            copy.wait()
            part = lhs[:, k * tile : (k + 1) * tile]
            for span in spans:
                product = jnp.dot(part, held[k, :, span], preferred_element_type=F32)
                total[:, span] = product if k == 0 else total[:, span] + product
    for j in range(count):

        @pl.when(owners[j % slots] >= 0)
        def _():
            block = total[pl.ds(pl.multiple_of(place(j), local), local), :]
            block = block.reshape(rows // RUN, STEPS, RUN, columns)
            for s in range(STEPS):
                piece = block[:, s].reshape(rows, columns).astype(BF16)
                out_ref[s, owners[j % slots], j // slots] = piece


def project(owners, blocks, weight, present, earlier=None):
    halves = len(blocks)
    flat = [block for part in blocks for block in part]
    local, depth = flat[0].shape
    columns = weight.shape[1]
    rows = local // STEPS
    count = len(flat)
    more = [] if earlier is None else [earlier]
    tile = min(512, depth)
    streamed = [
        pltpu.VMEM((depth // tile, tile, columns), BF16),
        pltpu.SemaphoreType.DMA((depth // tile,)),
    ]
    return pl.pallas_call(
        functools.partial(out_kernel, count, earlier is not None),
        out_shape=jax.ShapeDtypeStruct((STEPS, 4, halves, rows, columns), BF16),
        in_specs=[SMEM] + [VMEM] * count + [VMEM if more else HBM] + [VMEM] * len(more),
        out_specs=VMEM,
        scratch_shapes=[
            pltpu.VMEM((present * halves * local, depth), BF16),
            pltpu.VMEM((present * halves * local, columns), F32),
        ]
        + ([] if more else streamed),
        compiler_params=pltpu.CompilerParams(vmem_limit_bytes=(24 if more else 28) * MIB),
        cost_estimate=pl.CostEstimate(
            flops=2 * present * halves * local * depth * columns,
            bytes_accessed=2 * depth * columns + 4 * present * local * (depth + columns),
            transcendentals=0,
        ),
        name="project",
    )(owners, *flat, weight, *more)


def lookup(identity, table):
    hits = identity[:, None] == jnp.arange(table.shape[0], dtype=jnp.int32)[None, :]
    return jnp.sum(jnp.where(hits, table[None, :], 0), axis=1)


def ascending(lengths):
    count = lengths.shape[0]
    rows = jnp.arange(count, dtype=jnp.int32)
    keyed = lengths * count + rows
    rank = jnp.sum((keyed[None, :] < keyed[:, None]).astype(jnp.int32), axis=1)
    return jnp.sum(jnp.where(rank[:, None] == rows[None, :], rows[:, None], 0), axis=0)


def angle_tables(lengths, unit):
    steps = jnp.arange(STEPS, dtype=jnp.int32)
    position = lengths.reshape(-1, 1, unit) + steps[None, :, None]
    freq = rope_base ** (-(jnp.arange(HD // 2, dtype=F32) * 2.0 / HD))
    angles = position.reshape(-1).astype(F32)[:, None] * freq
    cosine = jnp.cos(angles)
    sine = jnp.sin(angles)
    return jnp.concatenate([cosine, cosine], 1), jnp.concatenate([-sine, sine], 1)


def on_device(
    hidden,
    input_norm_scale,
    query_key_value_weight,
    output_weight,
    adapter_down_weight,
    adapter_up_weight,
    row_adapter_index,
    adapter_store_slot,
    lengths,
    key_value_cache,
):
    tensor_count = lax.axis_size("tensor")
    tensor_pos = lax.axis_index("tensor")
    store_pos = lax.axis_index("store")
    _, rows, span = hidden.shape
    model_width = input_norm_scale.shape[0]
    rows_here = lengths.shape[0]
    unit = min(RUN, rows_here)
    line = tensor_count == 4 and rows_here % (HALVES * RUN) == 0
    halves = HALVES if line else 1
    part_rows = rows_here // halves
    local = STEPS * part_rows
    held_slots = adapter_down_weight.shape[0]
    rank = adapter_down_weight.shape[2]

    raw = hidden.reshape(STEPS, tensor_count, halves, part_rows // unit, unit, span)
    raw = raw.transpose(2, 1, 3, 0, 4, 5).reshape(STEPS * rows, span)
    own_index = tensor_pos.reshape(1).astype(jnp.int32)
    owners = [own_index] + [hop_owners(tensor_pos, hop) for hop in (1, 2, 3)]
    count = tensor_count * local
    parts = [slice(h * count, (h + 1) * count) for h in range(halves)]
    values = raw.astype(F32)
    squares = jnp.sum(values * values, axis=1)
    if line:
        squares = squares + sum(swap(squares, "tensor", d) for d in (1, 2, 3))
        travelling, squares = lax.optimization_barrier((raw, squares))
        hop1 = line_hop(travelling, travelling, "tensor", 1)
    else:
        squares = summed_over(squares, "tensor")
    own_runs = row_adapter_index[::RUN]
    if halves > 1:
        own_runs = own_runs.reshape(tensor_count, halves, -1).swapaxes(0, 1).reshape(-1)
    told = jnp.concatenate([squares, own_runs.astype(F32)]).reshape(1, -1)
    told = jnp.concatenate([told, swap(told, "store", 2)], axis=0)
    if line:
        told, hop1 = lax.optimization_barrier((told, hop1))
        hop2 = line_hop(*hop1, "tensor", 2)
    told = jnp.concatenate([told, swap(told, "store", 1)], axis=0)
    told = jnp.stack([told[d] for d in (0, 2, 1, 3)])
    told = jnp.stack([jnp.stack([told[p ^ q] for q in range(4)]) for p in range(4)])
    told = lax.dynamic_index_in_dim(told, store_pos, 0, keepdims=False)
    runs = told[:, STEPS * rows :].astype(jnp.int32)
    told = told[:, : STEPS * rows]
    scales = lax.rsqrt(told / model_width + eps_norm)
    slots = lookup(runs.reshape(-1), adapter_store_slot).reshape(runs.shape)
    slots = jnp.where(slots // held_slots == store_pos, slots % held_slots, -1)
    place = store_pos.reshape(1).astype(jnp.int32)
    gains = input_norm_scale.reshape(1, -1)
    gain = lax.dynamic_slice_in_dim(gains, tensor_pos * span, span, 1)
    scales = scales[:, :, None]
    own_scale = lax.dynamic_index_in_dim(scales, store_pos, 0, keepdims=False)

    across = swap(raw, "store", 2)
    beside = swap(raw, "store", 1)
    diagonal = swap(across, "store", 1)
    mine = slots.reshape(-1)
    down = jnp.swapaxes(adapter_down_weight, 1, 2)
    kept, passed = shrink_rows(place, mine, (raw, beside, across, diagonal), scales, gain, down)
    kept = kept + swap(passed, "store", 1)
    shrunk = kept[0] + swap(kept[1], "store", 2)
    if line:
        shrunk, early = lax.optimization_barrier((shrunk, (raw,) + hop1))
        near = jnp.concatenate(owners[:2])
        total = base_block(early, own_scale, gains, query_key_value_weight, near, (0,) * 3, 3)
        shrunk = shrunk + swap(shrunk, "tensor", 1)
        shrunk, total, hop2 = lax.optimization_barrier((shrunk, total, hop2))
        sent = [(hop2[0][part], hop2[1][part]) for part in parts]
        shrunk = shrunk + swap(shrunk, "tensor", 2)
        shrunk, sent = lax.optimization_barrier((shrunk, sent))
        hop3 = [line_hop(*sent[0], "tensor", 3)]
    else:
        shrunk = summed_over(shrunk, "tensor")
    shrunk = shrunk.astype(BF16)
    shrunk = jnp.stack([shrunk, swap(shrunk, "store", 2)])
    other = swap(shrunk, "store", 1)
    kept, *passed = grow_rows(place, mine, shrunk, other, adapter_up_weight, 1)
    if line:
        passed, hop3[0] = lax.optimization_barrier((passed, hop3[0]))
    passed = [swap(piece, "store", 1) for piece in passed]
    leaving = [(kept[1, part] + passed[1][part]).astype(F16) for part in parts]
    if line:
        later, _ = lax.optimization_barrier((sent[1], leaving))
        hop3.append(line_hop(*later, "tensor", 3))
    arrived = [swap(piece, "store", 2).astype(F32) for piece in leaving]
    deltas = [(kept[0, p] + passed[0][p]) + far for p, far in zip(parts, arrived)]

    weight = query_key_value_weight
    mixed = []
    if line:
        total, leaving = lax.optimization_barrier((total, leaving))
        far = jnp.concatenate(owners[2:])
        for h, part in enumerate(parts):
            if mixed:
                far, mixed[-1] = lax.optimization_barrier((far, mixed[-1]))
            blocks = hop2 + hop3[h]
            first_rows = (h * count, h * count, 0, 0)
            sums = base_block(
                blocks, own_scale[part], gains, weight, far, first_rows, 2, total[part]
            )
            mixed.append((sums + deltas[h]).astype(BF16))
    else:
        everything = lax.all_gather(raw, "tensor", axis=0, tiled=False)
        own = base_block((raw,), own_scale, gains, weight, own_index, (0,), 1)
        total = base_rows(own_index, everything, own_scale, gains, own, weight, 0)
        mixed.append((total + deltas[0]).astype(BF16))
    mixed = [qkv.reshape(tensor_count, local, -1) for qkv in mixed]

    contexts = []
    exchanged = []
    for qkv in mixed:
        if exchanged:
            qkv, exchanged[-1] = lax.optimization_barrier((qkv, exchanged[-1]))
        exchanged.append(lax.all_to_all(qkv, "tensor", 0, 0, tiled=True))
    for h, moved in enumerate(exchanged):
        if tensor_count != 4:
            q_columns = HEADS * HD // tensor_count
            pieces = []
            for piece in (moved[..., :q_columns], moved[..., q_columns:]):
                joined = piece.transpose(1, 0, 2).reshape(local, 4, -1)
                pieces.append(joined.transpose(1, 0, 2))
            moved = jnp.concatenate(pieces, axis=2)
        here = lengths[h * part_rows : (h + 1) * part_rows]
        cosine, sine = angle_tables(here, unit)
        contexts.append(
            attend(here, ascending(here), moved, cosine, sine, key_value_cache, h * part_rows, unit)
        )

    if line:
        hops = [line_gather(context, "tensor") for context in contexts]
        first = [(context,) + hop[0] for context, hop in zip(contexts, hops)]
        last = [hop[1] + hop[2] for hop in hops]
        output = project(jnp.concatenate(owners[:2]), first, output_weight, 3)
        output = project(jnp.concatenate(owners[2:]), last, output_weight, 2, output)
    else:
        results = []
        for context in contexts:
            context = lax.all_gather(context, "tensor", axis=0, tiled=True)
            result = jnp.dot(context, output_weight, preferred_element_type=F32).astype(BF16)
            result = result.reshape(tensor_count, part_rows // unit, STEPS, unit, -1)
            result = result.transpose(2, 0, 1, 3, 4).reshape(STEPS, tensor_count, part_rows, -1)
            results.append(result)
        output = jnp.stack(results, axis=2)
    return output.reshape(STEPS, rows, -1)


def solution(mesh):
    in_specs = (
        P(None, ("groups", "store"), "tensor"),
        P(),
        P(None, "tensor"),
        P(None, "tensor"),
        P(("groups", "store"), "tensor", None),
        P(("groups", "store"), None, "tensor"),
        P(("groups", "store")),
        P("groups"),
        P(("groups", "store", "tensor")),
        P(("groups", "store", "tensor"), None, None, None),
    )
    out_specs = P(None, ("groups", "store"), "tensor")
    return jax.shard_map(
        on_device, mesh=mesh, in_specs=in_specs, out_specs=out_specs, check_vma=False
    )
```
